512 devices in a mesh: gx: 16 (over y, core), gy: 32 (over z, x).
Axes of the slice: x: 4, y: 8, z: 8, core: 2. Of those that a mesh axis runs over, the one named last changes fastest.
Arguments:
- species: float32 [9, 128, 256, 128], P(None, 'gx', 'gy'), may hold values from -4 to 4
- flow_fields: float32 [5, 128, 256, 128], P(None, 'gx', 'gy'), may hold values from -5 to 5
- classes: int32 [128, 256], P('gx', 'gy'), may hold values from 1 to 4, as said below
- diffusivity: float32 [14], replicated, may hold values from 0.2 to 0.6
- left_form: float32 [19, 9], replicated, may hold values from -2 to 2
- right_form: float32 [19, 9], replicated, may hold values from -2 to 2
- stoich: float32 [19, 9], replicated, may hold values from -1.25 to 1.25
- heat_release: float32 [19], replicated, may hold values from -3 to 3
- arrhenius_prefactor: float32 [19], replicated, may hold values from 0.4 to 4
- arrhenius_energy: float32 [19], replicated, may hold values from 0.5 to 2
- newton_matrix: float32 [10, 10], replicated, may hold values from -0.5 to 1.5
Outputs:
- species_out: float32 [9, 128, 256, 128], P(None, 'gx', 'gy')
- flow_out: float32 [5, 128, 256, 128], P(None, 'gx', 'gy')
The draws below stay inside these ranges and needn't reach their ends.
Inputs may be any that keep to these rules, and one draw needn't show every extreme that they name: `classes`: 1 where a column takes one substep, 2 to 4 otherwise. Among the columns of one device at most 32 have a class over 1, and some device has exactly that many; two devices with the same gx index whose gy indices differ by half the gy axis hold at most 40 such columns together, and some pair has exactly that many.
All inputs are finite; a program needn't handle non-finite values.
Results may differ from the reference program's by a relative error of at most 0.0003.
Values sent between devices are 32-bit elements; how exact they have to be, the bound alone decides.
No kernel may reach another device: no remote copies, remote signals or barrier semaphores. Data moves between devices by JAX's collectives and lax.ppermute only.
A program may use at most 64 MiB of HBM per device.

```python
import math
import jax
import jax.numpy as jnp
from jax import lax

NSPEC = 9
NREAC = 19
FLOW = 5
CX = 8
CY = 8
NZ = 128
NFIELD = 14
NX = 128
NY = 256


def draw_classes(key, part):
    blocks_x = NX // CX
    blocks_y = NY // CY
    half_axis = blocks_y // 2
    columns = CX * CY
    stiff_cap = columns // 2
    pairing_limit = 5 * columns // 8
    subkeys = jax.random.split(key, 6)
    flagged = jax.random.randint(subkeys[0], (blocks_x, half_axis), 0, 2)
    forcing_applied = jax.random.randint(subkeys[1], (), 0, blocks_x * half_axis)
    chosen_pair = (jnp.arange(blocks_x * half_axis).reshape(blocks_x, half_axis) == forcing_applied).astype(jnp.int32)
    flagged = jnp.maximum(flagged, chosen_pair)
    heavy_left = jax.random.randint(subkeys[2], (blocks_x, half_axis), 0, 2)
    quiet_count = jax.random.randint(subkeys[3], (blocks_x, blocks_y), columns // 16, columns // 8 + 1)
    front_left = jnp.where(heavy_left == 1, stiff_cap, pairing_limit - stiff_cap)
    leading_east_neighbour = pairing_limit - front_left
    left_count = jnp.where(flagged == 1, front_left, quiet_count[:, :half_axis])
    right_count = jnp.where(flagged == 1, leading_east_neighbour, quiet_count[:, half_axis:])
    counts = jnp.concatenate([left_count, right_count], axis=1)
    scores = jax.random.randint(subkeys[4], (blocks_x, blocks_y, columns), 0, 1 << 20) * columns + jnp.arange(columns)
    rank_order = jnp.argsort(jnp.argsort(scores, axis=-1, stable=True), axis=-1, stable=True)
    levels = jax.random.randint(subkeys[5], (blocks_x, blocks_y, columns), 2, 5)
    marked = jnp.where(rank_order < counts[..., None], levels, 1)
    class_grid = marked.reshape(blocks_x, blocks_y, CX, CY).transpose(0, 2, 1, 3).reshape(NX, NY)
    return class_grid.astype(jnp.int32)


def draw_newton_matrix(key, part):
    components = NSPEC + 1
    spread = jnp.clip(jax.random.normal(key, (components, components), jnp.float32), -4.0, 4.0) * 0.12
    return jnp.eye(components, dtype=jnp.float32) + spread


def block_scale(key, dims, shards, least, high):
    loudness = 1.0
    for axis_at, shards_of in shards:
        draws = jax.random.uniform(jax.random.fold_in(jax.random.fold_in(key, 6), axis_at), (shards_of,), jnp.float32, least / len(shards), high / len(shards))
        loudness = loudness * jnp.repeat(jnp.exp(draws), dims[axis_at] // shards_of).reshape((-1,) + (1,) * (len(dims) - 1 - axis_at))
    return loudness


def noise(rng, extent, scale, limit, cuts=(), kind=jnp.bfloat16):
    level = block_scale(rng, extent, cuts, -0.22, 0.18) if cuts else 1.0
    drawn = jax.random.normal(rng, extent, jnp.float32) * scale * level
    return jnp.minimum(jnp.maximum(drawn, -limit), limit).astype(kind)


def setup_inputs(seed: int = 0) -> dict:
    keys = jax.random.split(jax.random.key(seed), 12)
    species = noise(keys[0], (NSPEC, NX, NY, NZ), 0.7, 4.0, ((1, 16), (2, 32)), jnp.float32)
    flow_fields = noise(keys[1], (FLOW, NX, NY, NZ), 1.0, 5.0, ((1, 16), (2, 32)), jnp.float32)
    classes = draw_classes(jax.random.fold_in(keys[11], 71), 0)
    diffusivity = jnp.clip(jnp.exp(jax.random.uniform(keys[3], (NFIELD,), jnp.float32, math.log(0.2), math.log(0.6))), 0.2, 0.6)
    left_form = noise(keys[4], (NREAC, NSPEC), NSPEC ** -0.5, 2.0, (), jnp.float32)
    right_form = noise(keys[5], (NREAC, NSPEC), NSPEC ** -0.5, 2.0, (), jnp.float32)
    stoich = noise(keys[6], (NREAC, NSPEC), NREAC ** -0.5, 1.25, (), jnp.float32)
    heat_release = noise(keys[7], (NREAC,), 0.3, 3.0, (), jnp.float32)
    arrhenius_prefactor = jnp.clip(jnp.exp(jax.random.uniform(keys[8], (NREAC,), jnp.float32, math.log(0.4), math.log(4.0))), 0.4, 4.0)
    arrhenius_energy = jnp.clip(jax.random.uniform(keys[9], (NREAC,), jnp.float32, 0.5, 2.0), 0.5, 2.0)
    newton_matrix = draw_newton_matrix(jax.random.fold_in(keys[11], 71), 0)
    return {"species": species, "flow_fields": flow_fields, "classes": classes, "diffusivity": diffusivity, "left_form": left_form, "right_form": right_form, "stoich": stoich, "heat_release": heat_release, "arrhenius_prefactor": arrhenius_prefactor, "arrhenius_energy": arrhenius_energy, "newton_matrix": newton_matrix}


TIME_STEP = 0.25
PRECISE = lax.Precision.HIGHEST


def reaction_rates(burning_mixture_status, params):
    left_form, right_form, stoich, heat_release, arrhenius_prefactor, arrhenius_energy = params
    fractions = burning_mixture_status[:-1]
    thermal_kelvin_field = burning_mixture_status[-1]
    left_sum = jnp.tanh(jnp.einsum("rs,scn->rcn", left_form, fractions, precision=PRECISE))
    right_sum = jnp.tanh(jnp.einsum("rs,scn->rcn", right_form, fractions, precision=PRECISE))
    flow_speed_norm = arrhenius_prefactor[:, None, None] * jax.nn.sigmoid(arrhenius_energy[:, None, None] * thermal_kelvin_field[None])
    progress = flow_speed_norm * left_sum * right_sum
    species_rate = jnp.einsum("rs,rcn->scn", stoich, progress, precision=PRECISE)
    heat_rate = jnp.einsum("r,rcn->cn", heat_release, progress, precision=PRECISE)
    return jnp.concatenate([species_rate, heat_rate[None]], axis=0)


def substep(start, step_size, newton_matrix, params):
    current = start
    for repeat in range(3):
        residue = current - start - step_size[None] * reaction_rates(current, params)
        current = current - jnp.einsum("ij,jcn->icn", newton_matrix, residue, precision=PRECISE)
    return current


def wave_line(length):
    waves = 2.0 * jnp.pi * jnp.fft.fftfreq(length)
    return jnp.where(jnp.arange(length) == length // 2, 0.0, waves)


def reference(species, flow_fields, classes, diffusivity, left_form, right_form, stoich, heat_release, arrhenius_prefactor, arrhenius_energy, newton_matrix):
    params = (left_form, right_form, stoich, heat_release, arrhenius_prefactor, arrhenius_energy)
    nspec = species.shape[0]
    fields = jnp.concatenate([species, flow_fields], axis=0)
    stream_vel = flow_fields[1]
    span_vel = flow_fields[2]
    depth_vel = flow_fields[3]

    def transport(pieces):
        field, coefficient = pieces
        ahead_x = jnp.roll(field, -1, 0)
        behind_x = jnp.roll(field, 1, 0)
        ahead_y = jnp.roll(field, -1, 1)
        behind_y = jnp.roll(field, 1, 1)
        ahead_z = jnp.roll(field, -1, 2)
        behind_z = jnp.roll(field, 1, 2)
        laplace_sum = ahead_x + behind_x + ahead_y + behind_y + ahead_z + behind_z - 6.0 * field
        advection = 0.5 * (stream_vel * (ahead_x - behind_x) + span_vel * (ahead_y - behind_y) + depth_vel * (ahead_z - behind_z))
        return field + TIME_STEP * (coefficient * laplace_sum - advection)

    transported = lax.map(transport, (fields, diffusivity))
    burning_mixture_status = jnp.concatenate([transported[:nspec], transported[nspec + 4:nspec + 5]], axis=0)

    def react_row(pieces):
        row_state, row_class = pieces
        class_value = row_class.astype(jnp.float32)
        step_size = (TIME_STEP / class_value)[:, None]
        current = substep(row_state, step_size, newton_matrix, params)
        for section in (1, 2, 3):
            active = (class_value > section)[None, :, None]
            current = jnp.where(active, substep(current, step_size, newton_matrix, params), current)
        return current

    reacted = jnp.moveaxis(lax.map(react_row, (jnp.moveaxis(burning_mixture_status, 1, 0), classes)), 0, 1)
    source = (reacted[nspec] - transported[nspec + 4]) / TIME_STEP
    velocity = transported[nspec + 1:nspec + 4]
    vel_hat = jnp.fft.fftn(velocity, axes=(1, 2, 3))
    source_hat = jnp.fft.fftn(source)
    wave_x = wave_line(NX).reshape(-1, 1, 1)
    wave_y = wave_line(NY).reshape(1, -1, 1)
    wave_z = wave_line(NZ).reshape(1, 1, -1)
    wavenumber_squared = wave_x * wave_x + wave_y * wave_y + wave_z * wave_z
    denom = jnp.where(wavenumber_squared > 0, wavenumber_squared, 1.0)
    dotted = wave_x * vel_hat[0] + wave_y * vel_hat[1] + wave_z * vel_hat[2]
    waves = (wave_x, wave_y, wave_z)
    projected_hat = jnp.stack([vel_hat[axis] - waves[axis] * dotted / denom - 1j * waves[axis] * source_hat / denom for axis in range(3)])
    projected = jnp.real(jnp.fft.ifftn(projected_hat, axes=(1, 2, 3))).astype(jnp.float32)
    species_out = reacted[:nspec]
    flow_out = jnp.concatenate([transported[nspec:nspec + 1], projected, reacted[nspec:nspec + 1]], axis=0)
    return (species_out, flow_out)
```

```python
import functools

import jax
import jax.numpy as jnp
import numpy as np
from jax import lax
from jax.experimental import pallas as pl
from jax.experimental.pallas import tpu as pltpu
from jax.sharding import Mesh
from jax.sharding import PartitionSpec as P

GX = ("y", "c")
GY = ("z", "x")
MODES = ("y", "c", "z")

NSPEC = 9
NREAC = 19
NS = NSPEC + 1
NF = 14
NX = 128
NY = 256
NZ = 128
CX = 8
CY = 8
COLS = CX * CY
CAP = COLS // 2
CHUNK = 16
DT = 0.25
PRECISE = lax.Precision.HIGHEST
F32 = jnp.float32
VMEM = pl.BlockSpec(memory_space=pltpu.VMEM)
SMEM = pl.BlockSpec(memory_space=pltpu.SMEM)
LIMIT = 32 * 1024 * 1024


def basis(n):
    j = np.arange(n)
    h = n // 2
    f = np.zeros((n, n))
    k = np.zeros(n)
    f[0] = 1.0 / np.sqrt(n)
    f[h] = (-1.0) ** j / np.sqrt(n)
    for m in range(1, h):
        f[m] = np.sqrt(2.0 / n) * np.cos(2 * np.pi * (m * j % n) / n)
        f[h + m] = np.sqrt(2.0 / n) * np.sin(2 * np.pi * (m * j % n) / n)
        k[m] = k[h + m] = 2 * np.pi * m / n
    d = np.zeros((n, n))
    for m in range(1, h):
        d[m] = k[m] * f[h + m]
        d[h + m] = -k[m] * f[m]
    return f, d, k


def dot(a, b, dims=((1,), (0,))):
    return lax.dot_general(a, b, (dims, ((), ())), precision=PRECISE, preferred_element_type=F32)


def rates(z, left, right, msa, energy):
    acc = None
    for j in range(NREAC):
        a = left[j, 0] * z[0]
        b = right[j, 0] * z[0]
        for s in range(1, NSPEC):
            a = a + left[j, s] * z[s]
            b = b + right[j, s] * z[s]
        r = jnp.tanh(a) * jnp.tanh(b)
        r = r + r * jnp.tanh(energy[j] * z[NSPEC])
        term = [msa[i, j] * r for i in range(NS)]
        acc = term if acc is None else [p + q for p, q in zip(acc, term)]
    return acc


def substep(load, store, h, left, right, msa, energy, newton):
    z0 = [load(i) for i in range(NS)]
    acc = rates(z0, left, right, msa, energy)
    z = tuple(z0[i] + h * acc[i] for i in range(NS))

    def again(_, z):
        acc = rates(z, left, right, msa, energy)
        d = [z[i] - load(i) for i in range(NS)]
        out = []
        for i in range(NS):
            m = newton[i, 0] * d[0]
            for j in range(1, NS):
                m = m + newton[i, j] * d[j]
            out.append(z[i] + (h * acc[i] - m))
        return tuple(out)

    z = lax.fori_loop(0, 2, again, z)
    for i in range(NS):
        store(i, z[i])


def react_kernel(
    species,
    flow,
    xlo,
    xhi,
    ylo,
    yhi,
    classes,
    diff,
    left,
    right,
    msa,
    energy,
    newton,
    fz,
    dz,
    species_out,
    flow_mid,
    spectra,
    state,
    temp0,
    hcol,
    buf,
):
    ysub = lax.broadcasted_iota(jnp.int32, (CY, NZ), 0)
    half = [0.5 * flow[c] for c in (1, 2, 3)]

    def transport(f, field, coef):
        ahead_x = jnp.concatenate([field[1:], xhi[f][None]], axis=0)
        behind_x = jnp.concatenate([xlo[f][None], field[:-1]], axis=0)
        up = pltpu.roll(field, CY - 1, 1)
        down = pltpu.roll(field, 1, 1)
        ahead_y = jnp.stack([jnp.where(ysub == CY - 1, yhi[f, x : x + 1, :], up[x]) for x in range(CX)])
        behind_y = jnp.stack([jnp.where(ysub == 0, ylo[f, x : x + 1, :], down[x]) for x in range(CX)])
        ahead_z = pltpu.roll(field, NZ - 1, 2)
        behind_z = pltpu.roll(field, 1, 2)
        lap = (ahead_x + behind_x) + (ahead_y + behind_y) + (ahead_z + behind_z) - 6.0 * field
        adv = (
            half[0] * (ahead_x - behind_x)
            + half[1] * (ahead_y - behind_y)
            + half[2] * (ahead_z - behind_z)
        )
        return field + DT * (coef * lap - adv)

    for f in range(NF):
        field = species[f] if f < NSPEC else flow[f - NSPEC]
        moved = transport(f, field, diff[f])
        if f < NSPEC:
            state[:, f * NZ : (f + 1) * NZ] = moved.reshape(COLS, NZ)
        elif f == NF - 1:
            state[:, NSPEC * NZ :] = moved.reshape(COLS, NZ)
            temp0[...] = moved.reshape(COLS, NZ)
        else:
            flow_mid[f - NSPEC] = moved

    cls = classes[...].astype(F32)
    col = lax.broadcasted_iota(jnp.int32, (COLS, CX), 0)
    lane = lax.broadcasted_iota(jnp.int32, (COLS, CX), 1)
    pick_x = (col // CY == lane).astype(F32)
    pick_y = (col % CY == lane).astype(F32)
    class_col = jnp.sum(dot(pick_x, cls) * pick_y, axis=1, keepdims=True)
    rows = dot(cls, pick_y, ((1,), (1,)))
    row_x = lax.broadcasted_iota(jnp.int32, (CX, COLS), 0)
    row_c = lax.broadcasted_iota(jnp.int32, (CX, COLS), 1)
    class_row = jnp.sum(jnp.where(row_c // CY == row_x, rows, 0.0), axis=0, keepdims=True)
    hcol[...] = jnp.broadcast_to(DT / class_col, (COLS, NZ))
    ii = lax.broadcasted_iota(jnp.int32, (COLS, COLS), 0).astype(F32)
    jj = lax.broadcasted_iota(jnp.int32, (COLS, COLS), 1).astype(F32)
    key_col = class_col * COLS - ii
    key_row = class_row * COLS - jj
    rank_row = jnp.sum((key_col > key_row).astype(F32), axis=0, keepdims=True)
    rank_col = jnp.sum((key_row > key_col).astype(F32), axis=1, keepdims=True)
    place = lax.broadcasted_iota(jnp.int32, (CAP, COLS), 0).astype(F32)
    gather = (place == rank_row).astype(F32)
    place_t = lax.broadcasted_iota(jnp.int32, (COLS, CAP), 1).astype(F32)
    scatter = (place_t == rank_col).astype(F32)
    counts = [jnp.sum((class_row > float(s)).astype(jnp.int32)) for s in (1, 2, 3)]

    def first(g, _):
        rows16 = pl.ds(pl.multiple_of(g * CHUNK, CHUNK), CHUNK)

        def load(i):
            return state[rows16, i * NZ : (i + 1) * NZ]

        def store(i, value):
            state[rows16, i * NZ : (i + 1) * NZ] = value

        substep(load, store, hcol[rows16, :], left, right, msa, energy, newton)
        return 0

    lax.fori_loop(0, COLS // CHUNK, first, 0)

    buf[...] = dot(gather, state[...])
    class_sorted = jnp.sum(gather * class_row, axis=1, keepdims=True)
    hcol[0:CAP, :] = jnp.broadcast_to(DT / class_sorted, (CAP, NZ))

    def extra(g, _):
        start = g * CHUNK
        rows16 = pl.ds(pl.multiple_of(start, CHUNK), CHUNK)
        more = sum((c > start).astype(jnp.int32) for c in counts)

        def again(s, _):
            h = hcol[rows16, :]
            active = h < DT / (s + 1.5)

            def load(i):
                return buf[rows16, i * NZ : (i + 1) * NZ]

            def store(i, value):
                buf[rows16, i * NZ : (i + 1) * NZ] = jnp.where(active, value, load(i))

            substep(load, store, h, left, right, msa, energy, newton)
            return 0

        lax.fori_loop(0, more, again, 0)
        return 0

    lax.fori_loop(0, CAP // CHUNK, extra, 0)

    spread = dot(scatter, buf[...])
    chosen = rank_col < CAP - 0.5
    final = [
        jnp.where(chosen, spread[:, i * NZ : (i + 1) * NZ], state[:, i * NZ : (i + 1) * NZ])
        for i in range(NS)
    ]
    for i in range(NSPEC):
        species_out[i] = final[i].reshape(CX, CY, NZ)
    flow_mid[4] = final[NSPEC].reshape(CX, CY, NZ)
    source = (final[NSPEC] - temp0[...]) * (1.0 / DT)
    nt = ((1,), (1,))
    horizontal = flow_mid[1:3].reshape(2 * COLS, NZ)
    spectra[:, 0, :] = dot(fz[...], horizontal, nt)
    vertical = flow_mid[3].reshape(COLS, NZ)
    third = dot(dz[...], vertical, nt) - dot(fz[...], source, nt)
    spectra[:, 1, :] = jnp.concatenate([third, jnp.zeros_like(third)], axis=1)


def swap_blocks(v):
    rows, lanes = v.shape
    r = lax.broadcasted_iota(jnp.int32, v.shape, 0)
    k = lax.broadcasted_iota(jnp.int32, v.shape, 1) // 8
    for b in (1, 2, 4):
        low_r, low_k = (r & b) == 0, (k & b) == 0
        from_above = pltpu.roll(pltpu.roll(v, b, 0), lanes - 8 * b, 1)
        from_below = pltpu.roll(pltpu.roll(v, rows - b, 0), 8 * b, 1)
        v = jnp.where(low_r == low_k, v, jnp.where(low_r, from_below, from_above))
    return v


def stream_kernel(got, fx, dx, out):
    a = swap_blocks(got[:, 0, :])
    w = swap_blocks(got[:, 1, :])
    u = a[:, :COLS]
    h = dot(dx[...], u) + dot(fx[...], w[:, :COLS])
    y = dot(fx[...], a[:, COLS:])
    both = jnp.concatenate([h, y], axis=1)
    for i in range(4):
        out[i] = both


def solve_kernel(place, kz2, got, forth, back, kx2, ky2, fxt, dxt, out):
    full = dot(got[0], forth[0])
    for i in range(1, 4):
        full = full + dot(got[i], forth[i])
    k2 = kx2[...] + ky2[...] + kz2[place[0]]
    q = full / jnp.where(k2 > 0, k2, 1.0)
    lines = dot(q, back[place[1]])
    first = dot(fxt[...], lines)
    second = dot(dxt[...], lines)
    out[:, 0, :] = swap_blocks(first)
    out[:, 1, :] = swap_blocks(second)


def finish_kernel(got, mid, fz, dz, out):
    tn = ((0,), (0,))
    first = got[:, 0, :]
    second = got[:, 1, :]
    a = dot(second, fz[...], tn)[:COLS]
    b = dot(first[:, COLS:], fz[...], tn)
    c = dot(first[:, :COLS], dz[...], tn)
    out[0] = mid[0]
    out[1] = mid[1] + a.reshape(CX, CY, NZ)
    out[2] = mid[2] + b.reshape(CX, CY, NZ)
    out[3] = mid[3] - c.reshape(CX, CY, NZ)
    out[4] = mid[4]


def call(kernel, out_shapes, specs, scratch=(), flops=0, nbytes=0):
    out = [jax.ShapeDtypeStruct(s, F32) for s in out_shapes]
    return pl.pallas_call(
        kernel,
        out_shape=out if len(out) > 1 else out[0],
        in_specs=specs,
        out_specs=[VMEM] * len(out) if len(out) > 1 else VMEM,
        scratch_shapes=list(scratch),
        compiler_params=pltpu.CompilerParams(vmem_limit_bytes=LIMIT),
    )


def ring(axes, n, step):
    return functools.partial(
        lax.ppermute, axis_name=axes, perm=[(i, (i + step) % n) for i in range(n)]
    )


def shards(
    species,
    flow,
    classes,
    diffusivity,
    left,
    right,
    stoich,
    heat,
    prefactor,
    energy,
    newton,
):
    fields = lambda *at: jnp.concatenate([species[at], flow[at]], axis=0)
    every = slice(None)
    n_gx, n_gy = NX // CX, NY // CY
    ylo = ring(GY, n_gy, 1)(fields(every, every, CY - 1))
    yhi = ring(GY, n_gy, -1)(fields(every, every, 0))
    xlo = ring(GX, n_gx, 1)(fields(every, CX - 1))
    xhi = ring(GX, n_gx, -1)(fields(every, 0))

    both = jnp.concatenate([stoich, heat[:, None]], axis=1)
    msa = jnp.einsum("ij,rj->ir", newton, both, precision=PRECISE) * (0.5 * prefactor)[None, :]

    fz, dz, kz = basis(NZ)
    fy, dy, ky = basis(NY)
    fx, dx, kx = basis(NX)
    f32 = lambda v: np.ascontiguousarray(v, np.float32)
    y_of = ((np.arange(8)[None, :, None] * 4 + np.arange(4)[:, None, None]) * CY + np.arange(CY)).reshape(4, COLS)
    forth = np.stack([np.concatenate([fy[:, y].T, dy[:, y].T], axis=0) for y in y_of])
    back = np.stack([np.concatenate([fy[:, y], -dy[:, y]], axis=1) for y in y_of])

    species_out, mid, spectra = call(
        react_kernel,
        [(NSPEC, CX, CY, NZ), (5, CX, CY, NZ), (NZ, 2, 2 * COLS)],
        [VMEM] * 7 + [SMEM] * 6 + [VMEM] * 2,
        [
            pltpu.VMEM((COLS, NS * NZ), F32),
            pltpu.VMEM((COLS, NZ), F32),
            pltpu.VMEM((COLS, NZ), F32),
            pltpu.VMEM((CAP, NS * NZ), F32),
        ],
    )(
        species,
        flow,
        xlo,
        xhi,
        ylo,
        yhi,
        classes,
        diffusivity,
        left,
        right,
        msa,
        0.5 * energy,
        newton,
        f32(fz),
        f32(dz),
    )
    got = lax.all_to_all(spectra, MODES, 0, 0, tiled=True)
    lines = call(stream_kernel, [(4, NX, 2 * COLS)], [VMEM] * 3)(got, f32(fx), f32(dx))
    lines = lax.all_to_all(lines, "x", 0, 0, tiled=True)
    place = jnp.stack([lax.axis_index(MODES), lax.axis_index("x")]).astype(jnp.int32)
    grads = call(solve_kernel, [(NX, 2, 2 * COLS)], [SMEM] * 2 + [VMEM] * 7)(
        place,
        f32(kz * kz),
        lines,
        f32(forth),
        f32(back),
        f32(kx * kx)[:, None],
        f32(ky * ky)[None, :],
        f32(fx.T),
        f32(-dx.T),
    )
    got = lax.all_to_all(grads, MODES, 0, 0, tiled=True)
    flow_out = call(finish_kernel, [(5, CX, CY, NZ)], [VMEM] * 4)(got, mid, f32(fz), f32(dz))
    return (species_out, flow_out)


def solution(mesh):
    finer = Mesh(mesh.devices.reshape(8, 2, 8, 4), GX + GY)
    return jax.shard_map(
        shards,
        mesh=finer,
        in_specs=(P(None, GX, GY, None), P(None, GX, GY, None), P(GX, GY)) + (P(),) * 8,
        out_specs=(P(None, GX, GY, None), P(None, GX, GY, None)),
        check_vma=False,
    )
```

```python
import functools

import jax
import jax.numpy as jnp
import numpy as np
from jax import lax
from jax.experimental import pallas as pl
from jax.experimental.pallas import tpu as pltpu
from jax.sharding import Mesh
from jax.sharding import PartitionSpec as P

GX = ("y", "c")
GY = ("z", "x")
MODES = ("y", "c", "z")

NSPEC = 9
NREAC = 19
NS = NSPEC + 1
NF = 14
NX = 128
NY = 256
NZ = 128
CX = 8
CY = 8
COLS = CX * CY
CAP = COLS // 2
CHUNK = 16
DT = 0.25
PRECISE = lax.Precision.HIGHEST
F32 = jnp.float32
VMEM = pl.BlockSpec(memory_space=pltpu.VMEM)
SMEM = pl.BlockSpec(memory_space=pltpu.SMEM)
LIMIT = 32 * 1024 * 1024


def basis(n):
    j = np.arange(n)
    h = n // 2
    f = np.zeros((n, n))
    k = np.zeros(n)
    f[0] = 1.0 / np.sqrt(n)
    f[h] = (-1.0) ** j / np.sqrt(n)
    for m in range(1, h):
        f[m] = np.sqrt(2.0 / n) * np.cos(2 * np.pi * (m * j % n) / n)
        f[h + m] = np.sqrt(2.0 / n) * np.sin(2 * np.pi * (m * j % n) / n)
        k[m] = k[h + m] = 2 * np.pi * m / n
    d = np.zeros((n, n))
    for m in range(1, h):
        d[m] = k[m] * f[h + m]
        d[h + m] = -k[m] * f[m]
    return f, d, k


def dot(a, b, dims=((1,), (0,))):
    return lax.dot_general(a, b, (dims, ((), ())), precision=PRECISE, preferred_element_type=F32)


def parts(v):
    hi = v.astype(jnp.bfloat16)
    return hi, (v - hi.astype(F32)).astype(jnp.bfloat16)


def dot3(a, b, dims=((1,), (0,))):
    one = lambda p, q: lax.dot_general(p, q, (dims, ((), ())), preferred_element_type=F32)
    return one(a[0], b[0]) + (one(a[0], b[1]) + one(a[1], b[0]))


def rates(z, left, right, msa, energy):
    acc = None
    for j in range(NREAC):
        a = left[j, 0] * z[0]
        b = right[j, 0] * z[0]
        for s in range(1, NSPEC):
            a = a + left[j, s] * z[s]
            b = b + right[j, s] * z[s]
        r = jnp.tanh(a) * jnp.tanh(b)
        r = r + r * jnp.tanh(energy[j] * z[NSPEC])
        term = [msa[i, j] * r for i in range(NS)]
        acc = term if acc is None else [p + q for p, q in zip(acc, term)]
    return acc


def substep(load, store, h, left, right, msa, energy, newton):
    z0 = [load(i) for i in range(NS)]
    acc = rates(z0, left, right, msa, energy)
    z = tuple(z0[i] + h * acc[i] for i in range(NS))

    def again(_, z):
        acc = rates(z, left, right, msa, energy)
        d = [z[i] - load(i) for i in range(NS)]
        out = []
        for i in range(NS):
            m = newton[i, 0] * d[0]
            for j in range(1, NS):
                m = m + newton[i, j] * d[j]
            out.append(z[i] + (h * acc[i] - m))
        return tuple(out)

    z = lax.fori_loop(0, 2, again, z)
    for i in range(NS):
        store(i, z[i])


def react_kernel(
    species,
    flow,
    xlo,
    xhi,
    ylo,
    yhi,
    classes,
    diff,
    left,
    right,
    msa,
    energy,
    newton,
    fz,
    dz,
    species_out,
    flow_mid,
    spectra,
    state,
    temp0,
    hcol,
    buf,
):
    ysub = lax.broadcasted_iota(jnp.int32, (CY, NZ), 0)
    half = [0.5 * flow[c] for c in (1, 2, 3)]

    def transport(f, field, coef):
        ahead_x = jnp.concatenate([field[1:], xhi[f][None]], axis=0)
        behind_x = jnp.concatenate([xlo[f][None], field[:-1]], axis=0)
        up = pltpu.roll(field, CY - 1, 1)
        down = pltpu.roll(field, 1, 1)
        ahead_y = jnp.stack([jnp.where(ysub == CY - 1, yhi[f, x : x + 1, :], up[x]) for x in range(CX)])
        behind_y = jnp.stack([jnp.where(ysub == 0, ylo[f, x : x + 1, :], down[x]) for x in range(CX)])
        ahead_z = pltpu.roll(field, NZ - 1, 2)
        behind_z = pltpu.roll(field, 1, 2)
        lap = (ahead_x + behind_x) + (ahead_y + behind_y) + (ahead_z + behind_z) - 6.0 * field
        adv = (
            half[0] * (ahead_x - behind_x)
            + half[1] * (ahead_y - behind_y)
            + half[2] * (ahead_z - behind_z)
        )
        return field + DT * (coef * lap - adv)

    for f in range(NF):
        field = species[f] if f < NSPEC else flow[f - NSPEC]
        moved = transport(f, field, diff[f])
        if f < NSPEC:
            state[:, f * NZ : (f + 1) * NZ] = moved.reshape(COLS, NZ)
        elif f == NF - 1:
            state[:, NSPEC * NZ :] = moved.reshape(COLS, NZ)
            temp0[...] = moved.reshape(COLS, NZ)
        else:
            flow_mid[f - NSPEC] = moved

    cls = classes[...].astype(F32)
    col = lax.broadcasted_iota(jnp.int32, (COLS, CX), 0)
    lane = lax.broadcasted_iota(jnp.int32, (COLS, CX), 1)
    pick_x = (col // CY == lane).astype(F32)
    pick_y = (col % CY == lane).astype(F32)
    class_col = jnp.sum(dot(pick_x, cls) * pick_y, axis=1, keepdims=True)
    rows = dot(cls, pick_y, ((1,), (1,)))
    row_x = lax.broadcasted_iota(jnp.int32, (CX, COLS), 0)
    row_c = lax.broadcasted_iota(jnp.int32, (CX, COLS), 1)
    class_row = jnp.sum(jnp.where(row_c // CY == row_x, rows, 0.0), axis=0, keepdims=True)
    hcol[...] = jnp.broadcast_to(DT / class_col, (COLS, NZ))
    ii = lax.broadcasted_iota(jnp.int32, (COLS, COLS), 0).astype(F32)
    jj = lax.broadcasted_iota(jnp.int32, (COLS, COLS), 1).astype(F32)
    key_col = class_col * COLS - ii
    key_row = class_row * COLS - jj
    rank_row = jnp.sum((key_col > key_row).astype(F32), axis=0, keepdims=True)
    rank_col = jnp.sum((key_row > key_col).astype(F32), axis=1, keepdims=True)
    place = lax.broadcasted_iota(jnp.int32, (CAP, COLS), 0).astype(F32)
    gather = (place == rank_row).astype(F32)
    place_t = lax.broadcasted_iota(jnp.int32, (COLS, CAP), 1).astype(F32)
    scatter = (place_t == rank_col).astype(F32)
    counts = [jnp.sum((class_row > float(s)).astype(jnp.int32)) for s in (1, 2, 3)]

    def first(g, _):
        rows16 = pl.ds(pl.multiple_of(g * CHUNK, CHUNK), CHUNK)

        def load(i):
            return state[rows16, i * NZ : (i + 1) * NZ]

        def store(i, value):
            state[rows16, i * NZ : (i + 1) * NZ] = value

        substep(load, store, hcol[rows16, :], left, right, msa, energy, newton)
        return 0

    lax.fori_loop(0, COLS // CHUNK, first, 0)

    buf[...] = dot(gather, state[...])
    class_sorted = jnp.sum(gather * class_row, axis=1, keepdims=True)
    hcol[0:CAP, :] = jnp.broadcast_to(DT / class_sorted, (CAP, NZ))

    def extra(g, _):
        start = g * CHUNK
        rows16 = pl.ds(pl.multiple_of(start, CHUNK), CHUNK)
        more = sum((c > start).astype(jnp.int32) for c in counts)

        def again(s, _):
            h = hcol[rows16, :]
            active = h < DT / (s + 1.5)

            def load(i):
                return buf[rows16, i * NZ : (i + 1) * NZ]

            def store(i, value):
                buf[rows16, i * NZ : (i + 1) * NZ] = jnp.where(active, value, load(i))

            substep(load, store, h, left, right, msa, energy, newton)
            return 0

        lax.fori_loop(0, more, again, 0)
        return 0

    lax.fori_loop(0, CAP // CHUNK, extra, 0)

    spread = dot(scatter, buf[...])
    chosen = rank_col < CAP - 0.5
    final = [
        jnp.where(chosen, spread[:, i * NZ : (i + 1) * NZ], state[:, i * NZ : (i + 1) * NZ])
        for i in range(NS)
    ]
    for i in range(NSPEC):
        species_out[i] = final[i].reshape(CX, CY, NZ)
    flow_mid[4] = final[NSPEC].reshape(CX, CY, NZ)
    source = (final[NSPEC] - temp0[...]) * (1.0 / DT)
    nt = ((1,), (1,))
    horizontal = flow_mid[1:3].reshape(2 * COLS, NZ)
    fz2, dz2 = (fz[0], fz[1]), (dz[0], dz[1])
    spectra[:, 0, :] = dot3(fz2, parts(horizontal), nt)
    vertical = flow_mid[3].reshape(COLS, NZ)
    third = dot3(dz2, parts(vertical), nt) - dot3(fz2, parts(source), nt)
    spectra[:, 1, :] = jnp.concatenate([third, jnp.zeros_like(third)], axis=1)


def swap_blocks(v):
    rows, lanes = v.shape
    r = lax.broadcasted_iota(jnp.int32, v.shape, 0)
    k = lax.broadcasted_iota(jnp.int32, v.shape, 1) // 8
    for b in (1, 2, 4):
        low_r, low_k = (r & b) == 0, (k & b) == 0
        from_above = pltpu.roll(pltpu.roll(v, b, 0), lanes - 8 * b, 1)
        from_below = pltpu.roll(pltpu.roll(v, rows - b, 0), 8 * b, 1)
        v = jnp.where(low_r == low_k, v, jnp.where(low_r, from_below, from_above))
    return v


def stream_kernel(got, fx, dx, out):
    a = swap_blocks(got[:, 0, :])
    w = swap_blocks(got[:, 1, :])
    upper = lax.broadcasted_iota(jnp.int32, a.shape, 1) < COLS
    fx2, dx2 = (fx[0], fx[1]), (dx[0], dx[1])
    moved = jnp.where(upper, w, a)
    both = dot3(fx2, parts(moved)) + jnp.where(upper, dot3(dx2, parts(a)), 0.0)
    for i in range(4):
        out[i] = both


def solve_kernel(place, kz2, got, forth, back, kx2, ky2, fxt, dxt, out):
    full = None
    for i in range(4):
        term = dot3(parts(got[i]), (forth[0, i], forth[1, i]))
        full = term if full is None else full + term
    k2 = kx2[...] + ky2[...] + kz2[place[0]]
    q = full / jnp.where(k2 > 0, k2, 1.0)
    lines = parts(dot3(parts(q), (back[0, place[1]], back[1, place[1]])))
    first = dot3((fxt[0], fxt[1]), lines)
    second = dot3((dxt[0], dxt[1]), lines)
    out[:, 0, :] = swap_blocks(first)
    out[:, 1, :] = swap_blocks(second)


def finish_kernel(got, mid, fz, dz, out):
    fz2, dz2 = (fz[0], fz[1]), (dz[0], dz[1])
    first = parts(jnp.transpose(got[:, 0, :]))
    second = parts(jnp.transpose(got[:, 1, :]))
    a = dot3(second, fz2)[:COLS]
    b = dot3(first, fz2)[COLS:]
    c = dot3(first, dz2)[:COLS]
    out[0] = mid[0]
    out[1] = mid[1] + a.reshape(CX, CY, NZ)
    out[2] = mid[2] + b.reshape(CX, CY, NZ)
    out[3] = mid[3] - c.reshape(CX, CY, NZ)
    out[4] = mid[4]


def call(kernel, out_shapes, specs, scratch=(), flops=0, nbytes=0):
    out = [jax.ShapeDtypeStruct(s, F32) for s in out_shapes]
    return pl.pallas_call(
        kernel,
        out_shape=out if len(out) > 1 else out[0],
        in_specs=specs,
        out_specs=[VMEM] * len(out) if len(out) > 1 else VMEM,
        scratch_shapes=list(scratch),
        compiler_params=pltpu.CompilerParams(vmem_limit_bytes=LIMIT),
    )


def ring(axes, n, step):
    return functools.partial(
        lax.ppermute, axis_name=axes, perm=[(i, (i + step) % n) for i in range(n)]
    )


def shards(
    species,
    flow,
    classes,
    diffusivity,
    left,
    right,
    stoich,
    heat,
    prefactor,
    energy,
    newton,
):
    fields = lambda *at: jnp.concatenate([species[at], flow[at]], axis=0)
    every = slice(None)
    n_gx, n_gy = NX // CX, NY // CY
    ylo = ring(GY, n_gy, 1)(fields(every, every, CY - 1))
    yhi = ring(GY, n_gy, -1)(fields(every, every, 0))
    xlo = ring(GX, n_gx, 1)(fields(every, CX - 1))
    xhi = ring(GX, n_gx, -1)(fields(every, 0))

    both = jnp.concatenate([stoich, heat[:, None]], axis=1)
    msa = jnp.einsum("ij,rj->ir", newton, both, precision=PRECISE) * (0.5 * prefactor)[None, :]

    fz, dz, kz = basis(NZ)
    fy, dy, ky = basis(NY)
    fx, dx, kx = basis(NX)
    f32 = lambda v: np.ascontiguousarray(v, np.float32)

    def table(v):
        v = f32(v)
        hi = v.astype(jnp.bfloat16)
        return np.stack([hi, (v - hi.astype(np.float32)).astype(jnp.bfloat16)])

    y_of = ((np.arange(8)[None, :, None] * 4 + np.arange(4)[:, None, None]) * CY + np.arange(CY)).reshape(4, COLS)
    forth = np.stack([np.concatenate([fy[:, y].T, dy[:, y].T], axis=0) for y in y_of])
    back = np.stack([np.concatenate([fy[:, y], -dy[:, y]], axis=1) for y in y_of])

    species_out, mid, spectra = call(
        react_kernel,
        [(NSPEC, CX, CY, NZ), (5, CX, CY, NZ), (NZ, 2, 2 * COLS)],
        [VMEM] * 7 + [SMEM] * 6 + [VMEM] * 2,
        [
            pltpu.VMEM((COLS, NS * NZ), F32),
            pltpu.VMEM((COLS, NZ), F32),
            pltpu.VMEM((COLS, NZ), F32),
            pltpu.VMEM((CAP, NS * NZ), F32),
        ],
    )(
        species,
        flow,
        xlo,
        xhi,
        ylo,
        yhi,
        classes,
        diffusivity,
        left,
        right,
        msa,
        0.5 * energy,
        newton,
        table(fz),
        table(dz),
    )
    place = jnp.stack([lax.axis_index(MODES), lax.axis_index("x")]).astype(jnp.int32)
    spectra, place = lax.optimization_barrier((spectra, place))
    got = lax.all_to_all(spectra, MODES, 0, 0, tiled=True)
    lines = call(stream_kernel, [(4, NX, 2 * COLS)], [VMEM] * 3)(got, table(fx), table(dx))
    lines = lax.all_to_all(lines, "x", 0, 0, tiled=True)
    grads = call(solve_kernel, [(NX, 2, 2 * COLS)], [SMEM] * 2 + [VMEM] * 7)(
        place,
        f32(kz * kz),
        lines,
        table(forth),
        table(back),
        f32(kx * kx)[:, None],
        f32(ky * ky)[None, :],
        table(fx.T),
        table(-dx.T),
    )
    got = lax.all_to_all(grads, MODES, 0, 0, tiled=True)
    flow_out = call(finish_kernel, [(5, CX, CY, NZ)], [VMEM] * 4)(got, mid, table(fz), table(dz))
    return (species_out, flow_out)


def solution(mesh):
    finer = Mesh(mesh.devices.reshape(8, 2, 8, 4), GX + GY)
    return jax.shard_map(
        shards,
        mesh=finer,
        in_specs=(P(None, GX, GY, None), P(None, GX, GY, None), P(GX, GY)) + (P(),) * 8,
        out_specs=(P(None, GX, GY, None), P(None, GX, GY, None)),
        check_vma=False,
    )
```

```python
import functools

import jax
import jax.numpy as jnp
import numpy as np
from jax import lax
from jax.experimental import pallas as pl
from jax.experimental.pallas import tpu as pltpu
from jax.sharding import Mesh
from jax.sharding import PartitionSpec as P

GX = ("y", "c")
GY = ("z", "x")
MODES = ("y", "c", "z")

NSPEC = 9
NREAC = 19
NS = NSPEC + 1
NF = 14
NX = 128
NY = 256
NZ = 128
CX = 8
CY = 8
COLS = CX * CY
CAP = COLS // 2
DT = 0.25
PRECISE = lax.Precision.HIGHEST
F32 = jnp.float32
VMEM = pl.BlockSpec(memory_space=pltpu.VMEM)
SMEM = pl.BlockSpec(memory_space=pltpu.SMEM)
LIMIT = 32 * 1024 * 1024


def basis(n):
    j = np.arange(n)
    h = n // 2
    f = np.zeros((n, n))
    k = np.zeros(n)
    f[0] = 1.0 / np.sqrt(n)
    f[h] = (-1.0) ** j / np.sqrt(n)
    for m in range(1, h):
        f[m] = np.sqrt(2.0 / n) * np.cos(2 * np.pi * (m * j % n) / n)
        f[h + m] = np.sqrt(2.0 / n) * np.sin(2 * np.pi * (m * j % n) / n)
        k[m] = k[h + m] = 2 * np.pi * m / n
    d = np.zeros((n, n))
    for m in range(1, h):
        d[m] = k[m] * f[h + m]
        d[h + m] = -k[m] * f[m]
    return f, d, k


def dot(a, b, dims=((1,), (0,))):
    return lax.dot_general(a, b, (dims, ((), ())), precision=PRECISE, preferred_element_type=F32)


def parts(v):
    hi = v.astype(jnp.bfloat16)
    return hi, (v - hi.astype(F32)).astype(jnp.bfloat16)


def dot3(a, b, dims=((1,), (0,))):
    one = lambda p, q: lax.dot_general(p, q, (dims, ((), ())), preferred_element_type=F32)
    return one(a[0], b[0]) + (one(a[0], b[1]) + one(a[1], b[0]))


OFF = 3
ROWS = 16
LINES = 24
FORM = 3 * LINES
GROUPS = 4


def one_hot(shape, f):
    r = lax.broadcasted_iota(jnp.int32, shape, 0)
    c = lax.broadcasted_iota(jnp.int32, shape, 1)
    return f(r, c).astype(F32)


def weights_kernel(left, right, stoich, heat, prefactor, energy, newton, classes, forms, update, plan):
    down = lambda k: one_hot((FORM, NREAC), lambda r, c: r == c + k * LINES)
    across = one_hot((NSPEC, ROWS), lambda r, c: c == r + OFF)
    eye = one_hot((NREAC, NREAC), lambda r, c: r == c)
    energy_col = jnp.sum(eye * energy[...][None, :], axis=1, keepdims=True)
    temp = one_hot((NREAC, ROWS), lambda r, c: c == OFF + NSPEC)
    w = (
        dot(down(0), dot(left[...], across))
        + dot(down(1), dot(right[...], across))
        + dot(down(2), 0.5 * energy_col * temp)
    )
    wide = GROUPS * 3 * ROWS
    tall = GROUPS * FORM
    copies = dot(w, one_hot((ROWS, wide), lambda r, c: r == c % ROWS))
    every = jnp.concatenate([copies] * GROUPS, axis=0)
    r = lax.broadcasted_iota(jnp.int32, (tall, wide), 0)
    c = lax.broadcasted_iota(jnp.int32, (tall, wide), 1)
    hi, lo = parts(jnp.where(r // FORM == c // (3 * ROWS), every, 0.0))
    forms[...] = jnp.where(c % (3 * ROWS) < 2 * ROWS, hi.astype(F32), lo.astype(F32)).astype(jnp.bfloat16)

    heat_col = jnp.sum(eye * heat[...][None, :], axis=1, keepdims=True)
    both = dot(stoich[...], one_hot((NSPEC, NS), lambda r, c: r == c))
    both = both + heat_col * one_hot((NREAC, NS), lambda r, c: c == NSPEC)
    msa = dot(newton[...], both, ((1,), (1,))) * (0.5 * prefactor[...][None, :])
    v = dot(msa, one_hot((NREAC, 32), lambda r, c: r == c))
    v = v - dot(newton[...], one_hot((NS, 32), lambda r, c: c == r + NREAC))
    v = dot(one_hot((ROWS, NS), lambda r, c: r == c + OFF), v)
    copies = dot(v, one_hot((32, 192), lambda r, c: r == c % 32))
    every = jnp.concatenate([copies, copies], axis=0)
    r = lax.broadcasted_iota(jnp.int32, (2 * ROWS, 192), 0)
    c = lax.broadcasted_iota(jnp.int32, (2 * ROWS, 192), 1)
    hi, lo = parts(jnp.where(r // ROWS == c // 96, every, 0.0))
    update[...] = jnp.where(c % 96 < 64, hi.astype(F32), lo.astype(F32)).astype(jnp.bfloat16)

    cls = classes[...].astype(F32)
    pick_x = one_hot((COLS, CX), lambda r, c: r // CY == c)
    pick_y = one_hot((COLS, CY), lambda r, c: r % CY == c)
    class_col = jnp.sum(dot(pick_x, cls) * pick_y, axis=1, keepdims=True)
    rows = dot(cls, pick_y, ((1,), (1,)))
    class_row = jnp.sum(one_hot((CX, COLS), lambda r, c: c // CY == r) * rows, axis=0, keepdims=True)
    ii = lax.broadcasted_iota(jnp.int32, (COLS, COLS), 0).astype(F32)
    jj = lax.broadcasted_iota(jnp.int32, (COLS, COLS), 1).astype(F32)
    rank_col = jnp.sum((class_row * COLS - jj > class_col * COLS - ii).astype(F32), axis=1, keepdims=True)
    at = (rank_col == jj).astype(F32)
    order = jnp.sum(at * ii, axis=0, keepdims=True)
    sorted_class = jnp.sum(at * class_col, axis=0, keepdims=True)
    table = jnp.concatenate([order, class_row, sorted_class, jnp.zeros((5, COLS), F32)], axis=0)
    plan[...] = jnp.concatenate([table, jnp.zeros_like(table)], axis=1).astype(jnp.int32)


def step_of(c):
    return jnp.where(c == 1, DT, jnp.where(c == 2, DT / 2, jnp.where(c == 3, DT / 3, DT / 4)))


def substep(cols, steps, forms, update):
    per = len(cols) // GROUPS
    wide = per * NZ
    z0 = [jnp.concatenate(cols[g * per : (g + 1) * per], axis=1) for g in range(GROUPS)]
    h = [
        jnp.concatenate([jnp.full((1, NZ), 1.0, F32) * steps[g * per + i] for i in range(per)], axis=1)
        for g in range(GROUPS)
    ]
    z = z0
    for repeat in range(3):
        stack = []
        for g in range(GROUPS):
            hi, lo = parts(z[g])
            stack += [hi, lo, hi]
        t = jnp.dot(forms, jnp.concatenate(stack, axis=0), preferred_element_type=F32)
        pairs = []
        for g in range(GROUPS):
            at = g * FORM
            p = jnp.tanh(t[at : at + LINES]) * jnp.tanh(t[at + LINES : at + 2 * LINES])
            p = (p + p * jnp.tanh(t[at + 2 * LINES : at + FORM])) * h[g]
            if repeat:
                d = z[g] - z0[g]
                x = jnp.concatenate([p[:16], p[16:] + d[:8], d[8:]], axis=0)
            else:
                x = jnp.concatenate([p, jnp.zeros((8, wide), F32)], axis=0)
            hi, lo = parts(x)
            pairs.append(jnp.concatenate([hi, lo, hi], axis=0))
        side = [jnp.concatenate(pairs[2 * k : 2 * k + 2], axis=0) for k in range(2)]
        change = [jnp.dot(update, s, preferred_element_type=F32) for s in side]
        z = [z[g] + change[g // 2][(g % 2) * ROWS : (g % 2 + 1) * ROWS] for g in range(GROUPS)]
    return [z[k // per][:, (k % per) * NZ : (k % per + 1) * NZ] for k in range(len(cols))]


def react_kernel(
    species,
    flow,
    xlo,
    xhi,
    ylo,
    yhi,
    diff,
    plan,
    forms,
    update,
    fz,
    dz,
    species_out,
    flow_mid,
    spectra,
    state,
    temp0,
    buf,
):
    ysub = lax.broadcasted_iota(jnp.int32, (CY, NZ), 0)
    half = [0.5 * flow[c] for c in (1, 2, 3)]

    def transport(f, field, coef):
        ahead_x = jnp.concatenate([field[1:], xhi[f][None]], axis=0)
        behind_x = jnp.concatenate([xlo[f][None], field[:-1]], axis=0)
        up = pltpu.roll(field, CY - 1, 1)
        down = pltpu.roll(field, 1, 1)
        ahead_y = jnp.stack([jnp.where(ysub == CY - 1, yhi[f, x : x + 1, :], up[x]) for x in range(CX)])
        behind_y = jnp.stack([jnp.where(ysub == 0, ylo[f, x : x + 1, :], down[x]) for x in range(CX)])
        ahead_z = pltpu.roll(field, NZ - 1, 2)
        behind_z = pltpu.roll(field, 1, 2)
        lap = (ahead_x + behind_x) + (ahead_y + behind_y) + (ahead_z + behind_z) - 6.0 * field
        adv = (
            half[0] * (ahead_x - behind_x)
            + half[1] * (ahead_y - behind_y)
            + half[2] * (ahead_z - behind_z)
        )
        return field + DT * (coef * lap - adv)

    zero = jnp.zeros((COLS, NZ), F32)
    for row in list(range(OFF)) + list(range(OFF + NS, ROWS)):
        state[:, row, :] = zero
    for f in range(NF):
        field = species[f] if f < NSPEC else flow[f - NSPEC]
        moved = transport(f, field, diff[f])
        if f < NSPEC:
            state[:, OFF + f, :] = moved.reshape(COLS, NZ)
        elif f == NF - 1:
            state[:, OFF + NSPEC, :] = moved.reshape(COLS, NZ)
            temp0[...] = moved.reshape(COLS, NZ)
        else:
            flow_mid[f - NSPEC] = moved

    def first(g, _):
        start = g * CAP
        cols = [state[start + k] for k in range(CAP)]
        steps = [step_of(plan[1, start + k]) for k in range(CAP)]
        done = substep(cols, steps, forms[...], update[...])
        for k in range(CAP):
            state[start + k] = done[k]
        return 0

    lax.fori_loop(0, COLS // CAP, first, 0)

    for k in range(CAP):
        buf[k] = state[plan[0, k]]

    def some(count, s):
        classes = [plan[2, k] for k in range(count)]
        cols = [buf[k] for k in range(count)]
        done = substep(cols, [step_of(c) for c in classes], forms[...], update[...])
        for k in range(count):
            buf[k] = jnp.where(classes[k] > s, done[k], cols[k])

    def section(s, _):
        many = plan[2, CAP // 2] > s

        @pl.when(many)
        def _():
            some(CAP, s)

        @pl.when(jnp.logical_and(jnp.logical_not(many), plan[2, 0] > s))
        def _():
            some(CAP // 2, s)

        return 0

    lax.fori_loop(1, 4, section, 0)

    for k in range(CAP):
        state[plan[0, k]] = buf[k]
    for i in range(NSPEC):
        species_out[i] = state[:, OFF + i, :].reshape(CX, CY, NZ)
    last = state[:, OFF + NSPEC, :]
    flow_mid[4] = last.reshape(CX, CY, NZ)
    source = (last - temp0[...]) * (1.0 / DT)
    nt = ((1,), (1,))
    horizontal = flow_mid[1:3].reshape(2 * COLS, NZ)
    fz2, dz2 = (fz[0], fz[1]), (dz[0], dz[1])
    spectra[:, 0, :] = dot3(fz2, parts(horizontal), nt)
    vertical = flow_mid[3].reshape(COLS, NZ)
    third = dot3(dz2, parts(vertical), nt) - dot3(fz2, parts(source), nt)
    spectra[:, 1, :] = jnp.concatenate([third, jnp.zeros_like(third)], axis=1)


def swap_blocks(v):
    rows, lanes = v.shape
    r = lax.broadcasted_iota(jnp.int32, v.shape, 0)
    k = lax.broadcasted_iota(jnp.int32, v.shape, 1) // 8
    for b in (1, 2, 4):
        low_r, low_k = (r & b) == 0, (k & b) == 0
        from_above = pltpu.roll(pltpu.roll(v, b, 0), lanes - 8 * b, 1)
        from_below = pltpu.roll(pltpu.roll(v, rows - b, 0), 8 * b, 1)
        v = jnp.where(low_r == low_k, v, jnp.where(low_r, from_below, from_above))
    return v


def stream_kernel(got, fx, dx, out):
    a = swap_blocks(got[:, 0, :])
    w = swap_blocks(got[:, 1, :])
    upper = lax.broadcasted_iota(jnp.int32, a.shape, 1) < COLS
    fx2, dx2 = (fx[0], fx[1]), (dx[0], dx[1])
    moved = jnp.where(upper, w, a)
    both = dot3(fx2, parts(moved)) + jnp.where(upper, dot3(dx2, parts(a)), 0.0)
    for i in range(4):
        out[i] = both


def solve_kernel(place, kz2, got, forth, back, kx2, ky2, fxt, dxt, out):
    full = None
    for i in range(4):
        term = dot3(parts(got[i]), (forth[0, i], forth[1, i]))
        full = term if full is None else full + term
    k2 = kx2[...] + ky2[...] + kz2[place[0]]
    q = full / jnp.where(k2 > 0, k2, 1.0)
    lines = parts(dot3(parts(q), (back[0, place[1]], back[1, place[1]])))
    first = dot3((fxt[0], fxt[1]), lines)
    second = dot3((dxt[0], dxt[1]), lines)
    out[:, 0, :] = swap_blocks(first)
    out[:, 1, :] = swap_blocks(second)


def finish_kernel(got, mid, fz, dz, out):
    fz2, dz2 = (fz[0], fz[1]), (dz[0], dz[1])
    first = parts(jnp.transpose(got[:, 0, :]))
    second = parts(jnp.transpose(got[:, 1, :]))
    a = dot3(second, fz2)[:COLS]
    b = dot3(first, fz2)[COLS:]
    c = dot3(first, dz2)[:COLS]
    out[0] = mid[0]
    out[1] = mid[1] + a.reshape(CX, CY, NZ)
    out[2] = mid[2] + b.reshape(CX, CY, NZ)
    out[3] = mid[3] - c.reshape(CX, CY, NZ)
    out[4] = mid[4]


def call(kernel, out_shapes, specs, scratch=()):
    pairs = [s if isinstance(s[0], tuple) else (s, F32) for s in out_shapes]
    out = [jax.ShapeDtypeStruct(*s) for s in pairs]
    return pl.pallas_call(
        kernel,
        out_shape=out if len(out) > 1 else out[0],
        in_specs=specs,
        out_specs=[VMEM] * len(out) if len(out) > 1 else VMEM,
        scratch_shapes=list(scratch),
        compiler_params=pltpu.CompilerParams(vmem_limit_bytes=LIMIT),
    )


def ring(axes, n, step):
    return functools.partial(
        lax.ppermute, axis_name=axes, perm=[(i, (i + step) % n) for i in range(n)]
    )


def shards(
    species,
    flow,
    classes,
    diffusivity,
    left,
    right,
    stoich,
    heat,
    prefactor,
    energy,
    newton,
):
    fields = lambda *at: jnp.concatenate([species[at], flow[at]], axis=0)
    every = slice(None)
    n_gx, n_gy = NX // CX, NY // CY
    ylo = ring(GY, n_gy, 1)(fields(every, every, CY - 1))
    yhi = ring(GY, n_gy, -1)(fields(every, every, 0))
    xlo = ring(GX, n_gx, 1)(fields(every, CX - 1))
    xhi = ring(GX, n_gx, -1)(fields(every, 0))

    forms, update, plan = call(
        weights_kernel,
        [
            ((GROUPS * FORM, GROUPS * 3 * ROWS), jnp.bfloat16),
            ((2 * ROWS, 192), jnp.bfloat16),
            ((8, 128), jnp.int32),
        ],
        [VMEM] * 8,
    )(left, right, stoich, heat, prefactor, energy, newton, classes)

    fz, dz, kz = basis(NZ)
    fy, dy, ky = basis(NY)
    fx, dx, kx = basis(NX)
    f32 = lambda v: np.ascontiguousarray(v, np.float32)

    def table(v):
        v = f32(v)
        hi = v.astype(jnp.bfloat16)
        return np.stack([hi, (v - hi.astype(np.float32)).astype(jnp.bfloat16)])

    y_of = ((np.arange(8)[None, :, None] * 4 + np.arange(4)[:, None, None]) * CY + np.arange(CY)).reshape(4, COLS)
    forth = np.stack([np.concatenate([fy[:, y].T, dy[:, y].T], axis=0) for y in y_of])
    back = np.stack([np.concatenate([fy[:, y], -dy[:, y]], axis=1) for y in y_of])

    species_out, mid, spectra = call(
        react_kernel,
        [(NSPEC, CX, CY, NZ), (5, CX, CY, NZ), (NZ, 2, 2 * COLS)],
        [VMEM] * 6 + [SMEM] * 2 + [VMEM] * 4,
        [
            pltpu.VMEM((COLS, ROWS, NZ), F32),
            pltpu.VMEM((COLS, NZ), F32),
            pltpu.VMEM((CAP, ROWS, NZ), F32),
        ],
    )(species, flow, xlo, xhi, ylo, yhi, diffusivity, plan, forms, update, table(fz), table(dz))
    place = jnp.stack([lax.axis_index(MODES), lax.axis_index("x")]).astype(jnp.int32)
    spectra, place = lax.optimization_barrier((spectra, place))
    got = lax.all_to_all(spectra, MODES, 0, 0, tiled=True)
    lines = call(stream_kernel, [(4, NX, 2 * COLS)], [VMEM] * 3)(got, table(fx), table(dx))
    lines = lax.all_to_all(lines, "x", 0, 0, tiled=True)
    grads = call(solve_kernel, [(NX, 2, 2 * COLS)], [SMEM] * 2 + [VMEM] * 7)(
        place,
        f32(kz * kz),
        lines,
        table(forth),
        table(back),
        f32(kx * kx)[:, None],
        f32(ky * ky)[None, :],
        table(fx.T),
        table(-dx.T),
    )
    got = lax.all_to_all(grads, MODES, 0, 0, tiled=True)
    flow_out = call(finish_kernel, [(5, CX, CY, NZ)], [VMEM] * 4)(got, mid, table(fz), table(dz))
    return (species_out, flow_out)


def solution(mesh):
    finer = Mesh(mesh.devices.reshape(8, 2, 8, 4), GX + GY)
    return jax.shard_map(
        shards,
        mesh=finer,
        in_specs=(P(None, GX, GY, None), P(None, GX, GY, None), P(GX, GY)) + (P(),) * 8,
        out_specs=(P(None, GX, GY, None), P(None, GX, GY, None)),
        check_vma=False,
    )
```

```python
import functools

import jax
import jax.numpy as jnp
import numpy as np
from jax import lax
from jax.experimental import pallas as pl
from jax.experimental.pallas import tpu as pltpu
from jax.sharding import Mesh
from jax.sharding import PartitionSpec as P

GX = ("y", "c")
GY = ("z", "x")
MODES = ("y", "c", "z")

NSPEC = 9
NREAC = 19
NS = NSPEC + 1
NF = 14
NX = 128
NY = 256
NZ = 128
CX = 8
CY = 8
COLS = CX * CY
CAP = COLS // 2
DT = 0.25
PRECISE = lax.Precision.HIGHEST
F32 = jnp.float32
VMEM = pl.BlockSpec(memory_space=pltpu.VMEM)
LIMIT = 32 * 1024 * 1024


def basis(n):
    j = np.arange(n)
    h = n // 2
    f = np.zeros((n, n))
    k = np.zeros(n)
    f[0] = 1.0 / np.sqrt(n)
    f[h] = (-1.0) ** j / np.sqrt(n)
    for m in range(1, h):
        f[m] = np.sqrt(2.0 / n) * np.cos(2 * np.pi * (m * j % n) / n)
        f[h + m] = np.sqrt(2.0 / n) * np.sin(2 * np.pi * (m * j % n) / n)
        k[m] = k[h + m] = 2 * np.pi * m / n
    d = np.zeros((n, n))
    for m in range(1, h):
        d[m] = k[m] * f[h + m]
        d[h + m] = -k[m] * f[m]
    return f, d, k


def dot(a, b, dims=((1,), (0,))):
    return lax.dot_general(a, b, (dims, ((), ())), precision=PRECISE, preferred_element_type=F32)


def parts(v):
    hi = v.astype(jnp.bfloat16)
    return hi, (v - hi.astype(F32)).astype(jnp.bfloat16)


def dot3(a, b, dims=((1,), (0,))):
    one = lambda p, q: lax.dot_general(p, q, (dims, ((), ())), preferred_element_type=F32)
    return one(a[0], b[0]) + (one(a[0], b[1]) + one(a[1], b[0]))


OFF = 3
ROWS = 16
FORM = 40
MAIN = 16
REST = NREAC - MAIN
GROUPS = 4
WIDE = GROUPS * 3 * ROWS


def one_hot(shape, f):
    r = lax.broadcasted_iota(jnp.int32, shape, 0)
    c = lax.broadcasted_iota(jnp.int32, shape, 1)
    return f(r, c).astype(F32)


def spread(block, height, width, copies, low):
    every = jnp.concatenate([block] * copies, axis=0)
    r = lax.broadcasted_iota(jnp.int32, every.shape, 0)
    c = lax.broadcasted_iota(jnp.int32, every.shape, 1)
    hi, lo = parts(jnp.where(r // height == c // width, every, 0.0))
    return jnp.where(c % width < low, hi.astype(F32), lo.astype(F32)).astype(jnp.bfloat16)


def form_weights(left_t, right_t):
    tn = ((1,), (1,))
    pick_l = one_hot((FORM, NREAC), lambda r, c: r == c + jnp.where(c < MAIN, 0, MAIN))
    pick_r = one_hot((FORM, NREAC), lambda r, c: r == c + jnp.where(c < MAIN, MAIN, MAIN + REST))
    w = dot(pick_l, left_t, tn) + dot(pick_r, right_t, tn)
    w = dot(w, one_hot((NSPEC, WIDE), lambda r, c: c % ROWS == r + OFF))
    return spread(w, FORM, 3 * ROWS, GROUPS, 2 * ROWS)


def update_weights(stoich_t, heat, prefactor, newton):
    both = dot(one_hot((NS, NSPEC), lambda r, c: r == c), stoich_t)
    both = both + one_hot((NS, NREAC), lambda r, c: r == NSPEC) * heat
    msa = dot(newton, both) * (0.5 * prefactor)
    v = dot(msa, one_hot((NREAC, 192), lambda r, c: c % 32 == r))
    v = v - dot(newton, one_hot((NS, 192), lambda r, c: c % 32 == r + NREAC))
    v = dot(one_hot((ROWS, NS), lambda r, c: r == c + OFF), v)
    return spread(v, ROWS, 96, 2, 64)


def column_plan(cls):
    pick_x = one_hot((COLS, CX), lambda r, c: r // CY == c)
    pick_y = one_hot((COLS, CY), lambda r, c: r % CY == c)
    class_col = jnp.sum(dot(pick_x, cls) * pick_y, axis=1, keepdims=True)
    rows = dot(cls, pick_y, ((1,), (1,)))
    class_row = jnp.sum(one_hot((CX, COLS), lambda r, c: c // CY == r) * rows, axis=0, keepdims=True)
    ii = lax.broadcasted_iota(jnp.int32, (COLS, COLS), 0).astype(F32)
    jj = lax.broadcasted_iota(jnp.int32, (COLS, COLS), 1).astype(F32)
    rank_col = jnp.sum((class_row * COLS - jj > class_col * COLS - ii).astype(F32), axis=1, keepdims=True)
    at = (rank_col == jj).astype(F32)
    order = jnp.sum(at * ii, axis=0, keepdims=True)
    sorted_class = jnp.sum(at * class_col, axis=0, keepdims=True)
    table = jnp.concatenate([order, class_row, sorted_class, jnp.zeros((5, COLS), F32)], axis=0)
    return jnp.concatenate([table, jnp.zeros_like(table)], axis=1).astype(jnp.int32)


def step_of(c):
    return jnp.where(c == 1, DT, jnp.where(c == 2, DT / 2, jnp.where(c == 3, DT / 3, DT / 4)))


def substep(cols, steps, forms, update, energy):
    per = len(cols) // GROUPS
    wide = per * NZ
    z0 = [jnp.concatenate(cols[g * per : (g + 1) * per], axis=1) for g in range(GROUPS)]
    h = [
        jnp.concatenate([jnp.full((1, NZ), 1.0, F32) * steps[g * per + i] for i in range(per)], axis=1)
        for g in range(GROUPS)
    ]
    top = lax.broadcasted_iota(jnp.int32, (8, wide), 0) < REST
    z = z0
    for repeat in range(3):
        stack = []
        for g in range(GROUPS):
            hi, lo = parts(z[g])
            stack += [hi, lo, hi]
        t = jnp.dot(forms, jnp.concatenate(stack, axis=0), preferred_element_type=F32)
        pairs = []
        for g in range(GROUPS):
            at = g * FORM
            heat = jnp.tanh(energy * z[g][OFF + NSPEC : OFF + NS])
            p = jnp.tanh(t[at : at + MAIN]) * jnp.tanh(t[at + MAIN : at + 2 * MAIN])
            p = (p + p * heat[:MAIN]) * h[g]
            q = jnp.tanh(t[at + 2 * MAIN : at + FORM])
            q = q * pltpu.roll(q, 8 - REST, 0)
            q = (q + q * heat[MAIN:]) * h[g]
            if repeat:
                d = z[g] - z0[g]
                x = jnp.concatenate([p, jnp.where(top, q, d[:8]), d[8:]], axis=0)
            else:
                zero = jnp.zeros((8, wide), F32)
                x = jnp.concatenate([p, jnp.where(top, q, zero), zero], axis=0)
            hi, lo = parts(x)
            pairs.append(jnp.concatenate([hi, lo, hi], axis=0))
        side = jnp.concatenate([jnp.concatenate(pairs[2 * k : 2 * k + 2], axis=0) for k in range(2)], axis=1)
        change = jnp.dot(update, side, preferred_element_type=F32)
        z = [
            z[g] + change[(g % 2) * ROWS : (g % 2 + 1) * ROWS, (g // 2) * wide : (g // 2 + 1) * wide]
            for g in range(GROUPS)
        ]
    return [z[k // per][:, (k % per) * NZ : (k % per + 1) * NZ] for k in range(len(cols))]


def halo_kernel(species, flow, last_x, first_x, last_y, first_y):
    for f in range(NF):
        src, at = (species, f) if f < NSPEC else (flow, f - NSPEC)
        last_x[f] = src[at, CX - 1]
        first_x[f] = src[at, 0]
        last_y[f] = src[at, :, CY - 1, :]
        first_y[f] = src[at, :, 0, :]


def react_kernel(
    species,
    flow,
    xlo,
    xhi,
    ylo,
    yhi,
    classes,
    diff,
    left_t,
    right_t,
    stoich_t,
    heat,
    prefactor,
    energy,
    newton,
    fz,
    dz,
    species_out,
    flow_mid,
    spectra,
    state,
    temp0,
    buf,
    table,
    plan,
    burnt,
    sems,
):
    table[...] = column_plan(classes[...].astype(F32))
    to_scalar = pltpu.make_async_copy(table, plan, sems.at[0])
    to_scalar.start()
    forms = form_weights(left_t[...], right_t[...])
    update = update_weights(stoich_t[...], heat[...], prefactor[...], newton[...])
    at_e = one_hot((MAIN + 8, NREAC), lambda r, c: r == c)
    energy_col = jnp.sum(at_e * (0.5 * energy[...]), axis=1, keepdims=True)

    ysub = lax.broadcasted_iota(jnp.int32, (CY, NZ), 0)
    half = [0.5 * flow[c] for c in (1, 2, 3)]

    def transport(f, field):
        coef = diff[:, f : f + 1].reshape(1, 1, 1)
        ahead_x = jnp.concatenate([field[1:], xhi[f][None]], axis=0)
        behind_x = jnp.concatenate([xlo[f][None], field[:-1]], axis=0)
        up = pltpu.roll(field, CY - 1, 1)
        down = pltpu.roll(field, 1, 1)
        ahead_y = jnp.stack([jnp.where(ysub == CY - 1, yhi[f, x : x + 1, :], up[x]) for x in range(CX)])
        behind_y = jnp.stack([jnp.where(ysub == 0, ylo[f, x : x + 1, :], down[x]) for x in range(CX)])
        ahead_z = pltpu.roll(field, NZ - 1, 2)
        behind_z = pltpu.roll(field, 1, 2)
        lap = (ahead_x + behind_x) + (ahead_y + behind_y) + (ahead_z + behind_z) - 6.0 * field
        adv = (
            half[0] * (ahead_x - behind_x)
            + half[1] * (ahead_y - behind_y)
            + half[2] * (ahead_z - behind_z)
        )
        return field + DT * (coef * lap - adv)

    zero = jnp.zeros((COLS, NZ), F32)
    for row in list(range(OFF)) + list(range(OFF + NS, ROWS)):
        state[:, row, :] = zero
    for f in range(NF):
        field = species[f] if f < NSPEC else flow[f - NSPEC]
        moved = transport(f, field)
        if f < NSPEC:
            state[:, OFF + f, :] = moved.reshape(COLS, NZ)
        elif f == NF - 1:
            state[:, OFF + NSPEC, :] = moved.reshape(COLS, NZ)
            temp0[...] = moved.reshape(COLS, NZ)
        else:
            flow_mid[f - NSPEC] = moved

    to_scalar.wait()
    steps = [step_of(plan[1, k]) for k in range(COLS)]
    done = substep([state[k] for k in range(COLS)], steps, forms, update, energy_col)
    for k in range(COLS):
        state[k] = done[k]

    for k in range(CAP):
        buf[k] = state[plan[0, k]]

    def some(count, s):
        kinds = [plan[2, k] for k in range(count)]
        cols = [buf[k] for k in range(count)]
        done = substep(cols, [step_of(c) for c in kinds], forms, update, energy_col)
        for k in range(count):
            buf[k] = jnp.where(kinds[k] > s, done[k], cols[k])

    def section(s, _):
        many = plan[2, CAP // 2] > s

        @pl.when(many)
        def _():
            some(CAP, s)

        @pl.when(jnp.logical_and(jnp.logical_not(many), plan[2, 0] > s))
        def _():
            some(CAP // 2, s)

        return 0

    lax.fori_loop(1, 4, section, 0)

    for k in range(CAP):
        state[plan[0, k]] = buf[k]
    for i in range(NSPEC):
        burnt[i] = state[:, OFF + i, :].reshape(CX, CY, NZ)
    to_out = pltpu.make_async_copy(burnt, species_out, sems.at[1])
    to_out.start()
    last = state[:, OFF + NSPEC, :]
    flow_mid[4] = last.reshape(CX, CY, NZ)
    source = (last - temp0[...]) * (1.0 / DT)
    nt = ((1,), (1,))
    horizontal = flow_mid[1:3].reshape(2 * COLS, NZ)
    fz2, dz2 = (fz[0], fz[1]), (dz[0], dz[1])
    spectra[:, 0, :] = dot3(fz2, parts(horizontal), nt)
    vertical = flow_mid[3].reshape(COLS, NZ)
    third = dot3(dz2, parts(vertical), nt) - dot3(fz2, parts(source), nt)
    spectra[:, 1, :] = jnp.concatenate([third, jnp.zeros_like(third)], axis=1)
    to_out.wait()


def swap_blocks(v):
    rows, lanes = v.shape
    r = lax.broadcasted_iota(jnp.int32, v.shape, 0)
    k = lax.broadcasted_iota(jnp.int32, v.shape, 1) // 8
    for b in (1, 2, 4):
        low_r, low_k = (r & b) == 0, (k & b) == 0
        from_above = pltpu.roll(pltpu.roll(v, b, 0), lanes - 8 * b, 1)
        from_below = pltpu.roll(pltpu.roll(v, rows - b, 0), 8 * b, 1)
        v = jnp.where(low_r == low_k, v, jnp.where(low_r, from_below, from_above))
    return v


def stream_kernel(got, fx, dx, out):
    a = swap_blocks(got[:, 0, :])
    w = swap_blocks(got[:, 1, :])
    upper = lax.broadcasted_iota(jnp.int32, a.shape, 1) < COLS
    fx2, dx2 = (fx[0], fx[1]), (dx[0], dx[1])
    moved = jnp.where(upper, w, a)
    both = dot3(fx2, parts(moved)) + jnp.where(upper, dot3(dx2, parts(a)), 0.0)
    for i in range(4):
        out[i] = both


def solve_kernel(place, got, forth, back, kx2, ky2, fxt, dxt, out):
    full = None
    for i in range(4):
        term = dot3(parts(got[i]), (forth[0, i], forth[1, i]))
        full = term if full is None else full + term
    mode = (place[:, 0:1] % (NZ // 2)).astype(F32) * (2 * np.pi / NZ)
    k2 = kx2[...] + ky2[...] + mode * mode
    mine = jnp.max(place[:, 1:2])
    q = full / jnp.where(k2 > 0, k2, 1.0)
    lines = parts(dot3(parts(q), (back[0, mine], back[1, mine])))
    first = dot3((fxt[0], fxt[1]), lines)
    second = dot3((dxt[0], dxt[1]), lines)
    out[:, 0, :] = swap_blocks(first)
    out[:, 1, :] = swap_blocks(second)


def finish_kernel(got, mid, fz, dz, out):
    fz2, dz2 = (fz[0], fz[1]), (dz[0], dz[1])
    first = parts(jnp.transpose(got[:, 0, :]))
    second = parts(jnp.transpose(got[:, 1, :]))
    a = dot3(second, fz2)[:COLS]
    b = dot3(first, fz2)[COLS:]
    c = dot3(first, dz2)[:COLS]
    out[0] = mid[0]
    out[1] = mid[1] + a.reshape(CX, CY, NZ)
    out[2] = mid[2] + b.reshape(CX, CY, NZ)
    out[3] = mid[3] - c.reshape(CX, CY, NZ)
    out[4] = mid[4]


def call(kernel, out_shapes, n_in, scratch=(), out_specs=None):
    out = [jax.ShapeDtypeStruct(s, F32) for s in out_shapes]
    one = len(out) == 1
    return pl.pallas_call(
        kernel,
        out_shape=out[0] if one else out,
        in_specs=[VMEM] * n_in,
        out_specs=VMEM if one else out_specs or [VMEM] * len(out),
        scratch_shapes=list(scratch),
        compiler_params=pltpu.CompilerParams(vmem_limit_bytes=LIMIT),
    )


def react(fields, halos, classes, diffusivity, left, right, stoich, heat, prefactor, energy, newton, fz, dz):
    row = lambda v: v[None, :]
    return call(
        react_kernel,
        [(NSPEC, CX, CY, NZ), (5, CX, CY, NZ), (NZ, 2, 2 * COLS)],
        17,
        [
            pltpu.VMEM((COLS, ROWS, NZ), F32),
            pltpu.VMEM((COLS, NZ), F32),
            pltpu.VMEM((CAP, ROWS, NZ), F32),
            pltpu.VMEM((8, NZ), jnp.int32),
            pltpu.SMEM((8, NZ), jnp.int32),
            pltpu.VMEM((NSPEC, CX, CY, NZ), F32),
            pltpu.SemaphoreType.DMA((2,)),
        ],
        [pl.BlockSpec(memory_space=pl.ANY), VMEM, VMEM],
    )(
        *fields,
        *halos,
        classes,
        row(diffusivity),
        left.T,
        right.T,
        stoich.T,
        row(heat),
        row(prefactor),
        row(energy),
        newton,
        fz,
        dz,
    )


def ring(axes, n, step):
    return functools.partial(
        lax.ppermute, axis_name=axes, perm=[(i, (i + step) % n) for i in range(n)]
    )


def shards(
    species,
    flow,
    classes,
    diffusivity,
    left,
    right,
    stoich,
    heat,
    prefactor,
    energy,
    newton,
):
    n_gx, n_gy = NX // CX, NY // CY
    edges = call(halo_kernel, [(NF, 8, NZ)] * 4, 2)(species, flow)
    ylo = ring(GY, n_gy, 1)(edges[2])
    yhi = ring(GY, n_gy, -1)(edges[3])
    xlo = ring(GX, n_gx, 1)(edges[0])
    xhi = ring(GX, n_gx, -1)(edges[1])

    fz, dz, _ = basis(NZ)
    fy, dy, ky = basis(NY)
    fx, dx, kx = basis(NX)
    f32 = lambda v: np.ascontiguousarray(v, np.float32)

    def table(v):
        v = f32(v)
        hi = v.astype(jnp.bfloat16)
        return np.stack([hi, (v - hi.astype(np.float32)).astype(jnp.bfloat16)])

    y_of = ((np.arange(8)[None, :, None] * 4 + np.arange(4)[:, None, None]) * CY + np.arange(CY)).reshape(4, COLS)
    forth = np.stack([np.concatenate([fy[:, y].T, dy[:, y].T], axis=0) for y in y_of])
    back = np.stack([np.concatenate([fy[:, y], -dy[:, y]], axis=1) for y in y_of])

    species_out, mid, spectra = react(
        (species, flow),
        (xlo, xhi, ylo, yhi),
        classes,
        diffusivity,
        left,
        right,
        stoich,
        heat,
        prefactor,
        energy,
        newton,
        table(fz),
        table(dz),
    )
    place = jnp.stack([lax.axis_index(MODES), lax.axis_index("x")]).astype(jnp.int32)[None, :]
    spectra, place = lax.optimization_barrier((spectra, place))
    got = lax.all_to_all(spectra, MODES, 0, 0, tiled=True)
    lines = call(stream_kernel, [(4, NX, 2 * COLS)], 3)(got, table(fx), table(dx))
    lines = lax.all_to_all(lines, "x", 0, 0, tiled=True)
    grads = call(solve_kernel, [(NX, 2, 2 * COLS)], 8)(
        place,
        lines,
        table(forth),
        table(back),
        f32(kx * kx)[:, None],
        f32(ky * ky)[None, :],
        table(fx.T),
        table(-dx.T),
    )
    got = lax.all_to_all(grads, MODES, 0, 0, tiled=True)
    flow_out = call(finish_kernel, [(5, CX, CY, NZ)], 4)(got, mid, table(fz), table(dz))
    return (species_out, flow_out)


def solution(mesh):
    finer = Mesh(mesh.devices.reshape(8, 2, 8, 4), GX + GY)
    return jax.shard_map(
        shards,
        mesh=finer,
        in_specs=(P(None, GX, GY, None), P(None, GX, GY, None), P(GX, GY)) + (P(),) * 8,
        out_specs=(P(None, GX, GY, None), P(None, GX, GY, None)),
        check_vma=False,
    )
```

```python
import functools

import jax
import jax.numpy as jnp
import numpy as np
from jax import lax
from jax.experimental import pallas as pl
from jax.experimental.pallas import tpu as pltpu
from jax.sharding import Mesh
from jax.sharding import PartitionSpec as P

GX = ("y", "c")
GY = ("z", "x")
MODES = ("y", "c", "z")

NSPEC = 9
NREAC = 19
NS = NSPEC + 1
NF = 14
NX = 128
NY = 256
NZ = 128
CX = 8
CY = 8
COLS = CX * CY
CAP = COLS // 2
DT = 0.25
PRECISE = lax.Precision.HIGHEST
F32 = jnp.float32
VMEM = pl.BlockSpec(memory_space=pltpu.VMEM)
HBM = pl.BlockSpec(memory_space=pltpu.HBM)
LIMIT = 32 * 1024 * 1024


def basis(n):
    j = np.arange(n)
    h = n // 2
    f = np.zeros((n, n))
    k = np.zeros(n)
    f[0] = 1.0 / np.sqrt(n)
    f[h] = (-1.0) ** j / np.sqrt(n)
    for m in range(1, h):
        f[m] = np.sqrt(2.0 / n) * np.cos(2 * np.pi * (m * j % n) / n)
        f[h + m] = np.sqrt(2.0 / n) * np.sin(2 * np.pi * (m * j % n) / n)
        k[m] = k[h + m] = 2 * np.pi * m / n
    d = np.zeros((n, n))
    for m in range(1, h):
        d[m] = k[m] * f[h + m]
        d[h + m] = -k[m] * f[m]
    return f, d, k


def dot(a, b, dims=((1,), (0,))):
    return lax.dot_general(a, b, (dims, ((), ())), precision=PRECISE, preferred_element_type=F32)


def parts(v):
    hi = v.astype(jnp.bfloat16)
    return hi, (v - hi.astype(F32)).astype(jnp.bfloat16)


def dot3(a, b, dims=((1,), (0,))):
    one = lambda p, q: lax.dot_general(p, q, (dims, ((), ())), preferred_element_type=F32)
    return one(a[0], b[0]) + (one(a[0], b[1]) + one(a[1], b[0]))


OFF = 3
ROWS = 16
FORM = 40
MAIN = 16
REST = NREAC - MAIN
GROUPS = 4
WIDE = GROUPS * 3 * ROWS


def one_hot(shape, f):
    r = lax.broadcasted_iota(jnp.int32, shape, 0)
    c = lax.broadcasted_iota(jnp.int32, shape, 1)
    return f(r, c).astype(F32)


def spread(block, height, width, copies, low):
    every = jnp.concatenate([block] * copies, axis=0)
    r = lax.broadcasted_iota(jnp.int32, every.shape, 0)
    c = lax.broadcasted_iota(jnp.int32, every.shape, 1)
    hi, lo = parts(jnp.where(r // height == c // width, every, 0.0))
    return jnp.where(c % width < low, hi.astype(F32), lo.astype(F32)).astype(jnp.bfloat16)


def form_weights(left_t, right_t):
    tn = ((1,), (1,))
    pick_l = one_hot((FORM, NREAC), lambda r, c: r == c + jnp.where(c < MAIN, 0, MAIN))
    pick_r = one_hot((FORM, NREAC), lambda r, c: r == c + jnp.where(c < MAIN, MAIN, MAIN + REST))
    w = dot(pick_l, left_t, tn) + dot(pick_r, right_t, tn)
    w = dot(w, one_hot((NSPEC, WIDE), lambda r, c: c % ROWS == r + OFF))
    return spread(w, FORM, 3 * ROWS, GROUPS, 2 * ROWS)


def update_weights(stoich_t, heat, prefactor, newton):
    both = dot(one_hot((NS, NSPEC), lambda r, c: r == c), stoich_t)
    both = both + one_hot((NS, NREAC), lambda r, c: r == NSPEC) * heat
    msa = dot(newton, both) * (0.5 * prefactor)
    v = dot(msa, one_hot((NREAC, 192), lambda r, c: c % 32 == r))
    v = v - dot(newton, one_hot((NS, 192), lambda r, c: c % 32 == r + NREAC))
    v = dot(one_hot((ROWS, NS), lambda r, c: r == c + OFF), v)
    return spread(v, ROWS, 96, 2, 64)


def column_plan(cls):
    pick_x = one_hot((COLS, CX), lambda r, c: r // CY == c)
    pick_y = one_hot((COLS, CY), lambda r, c: r % CY == c)
    class_col = jnp.sum(dot(pick_x, cls) * pick_y, axis=1, keepdims=True)
    rows = dot(cls, pick_y, ((1,), (1,)))
    class_row = jnp.sum(one_hot((CX, COLS), lambda r, c: c // CY == r) * rows, axis=0, keepdims=True)
    ii = lax.broadcasted_iota(jnp.int32, (COLS, COLS), 0).astype(F32)
    jj = lax.broadcasted_iota(jnp.int32, (COLS, COLS), 1).astype(F32)
    rank_col = jnp.sum((class_row * COLS - jj > class_col * COLS - ii).astype(F32), axis=1, keepdims=True)
    at = (rank_col == jj).astype(F32)
    order = jnp.sum(at * ii, axis=0, keepdims=True)
    sorted_class = jnp.sum(at * class_col, axis=0, keepdims=True)
    table = jnp.concatenate([order, class_row, sorted_class, jnp.zeros((5, COLS), F32)], axis=0)
    return jnp.concatenate([table, jnp.zeros_like(table)], axis=1).astype(jnp.int32)


def step_of(c):
    return jnp.where(c == 1, DT, jnp.where(c == 2, DT / 2, jnp.where(c == 3, DT / 3, DT / 4)))


def substep(cols, steps, forms, update, energy):
    per = len(cols) // GROUPS
    wide = per * NZ
    z0 = [jnp.concatenate(cols[g * per : (g + 1) * per], axis=1) for g in range(GROUPS)]
    h = [
        jnp.concatenate([jnp.full((1, NZ), 1.0, F32) * steps[g * per + i] for i in range(per)], axis=1)
        for g in range(GROUPS)
    ]
    top = lax.broadcasted_iota(jnp.int32, (8, wide), 0) < REST
    z = z0
    for repeat in range(3):
        stack = []
        for g in range(GROUPS):
            hi, lo = parts(z[g])
            stack += [hi, lo, hi]
        t = jnp.dot(forms, jnp.concatenate(stack, axis=0), preferred_element_type=F32)
        pairs = []
        for g in range(GROUPS):
            at = g * FORM
            heat = jnp.tanh(energy * z[g][OFF + NSPEC : OFF + NS])
            p = jnp.tanh(t[at : at + MAIN]) * jnp.tanh(t[at + MAIN : at + 2 * MAIN])
            p = (p + p * heat[:MAIN]) * h[g]
            q = jnp.tanh(t[at + 2 * MAIN : at + FORM])
            q = q * pltpu.roll(q, 8 - REST, 0)
            q = (q + q * heat[MAIN:]) * h[g]
            if repeat:
                d = z[g] - z0[g]
                x = jnp.concatenate([p, jnp.where(top, q, d[:8]), d[8:]], axis=0)
            else:
                zero = jnp.zeros((8, wide), F32)
                x = jnp.concatenate([p, jnp.where(top, q, zero), zero], axis=0)
            hi, lo = parts(x)
            pairs.append(jnp.concatenate([hi, lo, hi], axis=0))
        side = jnp.concatenate([jnp.concatenate(pairs[2 * k : 2 * k + 2], axis=0) for k in range(2)], axis=1)
        change = jnp.dot(update, side, preferred_element_type=F32)
        z = [
            z[g] + change[(g % 2) * ROWS : (g % 2 + 1) * ROWS, (g // 2) * wide : (g // 2 + 1) * wide]
            for g in range(GROUPS)
        ]
    return [z[k // per][:, (k % per) * NZ : (k % per + 1) * NZ] for k in range(len(cols))]


def halo_kernel(species, flow, last_x, first_x, last_y, first_y, own_s, own_f, sems):
    copies = [
        pltpu.make_async_copy(species, own_s, sems.at[0]),
        pltpu.make_async_copy(flow, own_f, sems.at[1]),
    ]
    for c in copies:
        c.start()
    for c in copies:
        c.wait()
    for f in range(NF):
        src, at = (own_s, f) if f < NSPEC else (own_f, f - NSPEC)
        last_x[f] = src[at, CX - 1]
        first_x[f] = src[at, 0]
        last_y[f] = src[at, :, CY - 1, :]
        first_y[f] = src[at, :, 0, :]


def weights_kernel(classes, left_t, right_t, stoich_t, heat, prefactor, energy, newton, diffusivity, forms, update, energy_col, diff, table):
    table[...] = column_plan(classes[...].astype(F32))
    forms[...] = form_weights(left_t[...], right_t[...])
    update[...] = update_weights(stoich_t[...], heat[...], prefactor[...], newton[...])
    at_e = one_hot((MAIN + 8, NREAC), lambda r, c: r == c)
    col = jnp.sum(at_e * (0.5 * energy[...]), axis=1, keepdims=True)
    energy_col[...] = jnp.broadcast_to(col, (MAIN + 8, NZ))
    col = jnp.sum(one_hot((16, NF), lambda r, c: r == c) * diffusivity[...], axis=1, keepdims=True)
    diff[...] = jnp.broadcast_to(col, (16, NZ))


def react_kernel(
    species,
    flow,
    xlo,
    xhi,
    ylo,
    yhi,
    forms,
    update,
    energy_col,
    diff,
    table,
    fz_far,
    dz_far,
    species_out,
    flow_mid,
    spectra,
    state,
    temp0,
    buf,
    plan,
    burnt,
    fz,
    dz,
    sems,
):
    to_scalar = pltpu.make_async_copy(table, plan, sems.at[0])
    to_scalar.start()
    near = [pltpu.make_async_copy(fz_far, fz, sems.at[2]), pltpu.make_async_copy(dz_far, dz, sems.at[3])]
    for c in near:
        c.start()

    ysub = lax.broadcasted_iota(jnp.int32, (CY, NZ), 0)
    half = [0.5 * flow[c] for c in (1, 2, 3)]

    def transport(f, field):
        coef = diff[f : f + 1, :]
        ahead_x = jnp.concatenate([field[1:], xhi[f][None]], axis=0)
        behind_x = jnp.concatenate([xlo[f][None], field[:-1]], axis=0)
        up = pltpu.roll(field, CY - 1, 1)
        down = pltpu.roll(field, 1, 1)
        ahead_y = jnp.stack([jnp.where(ysub == CY - 1, yhi[f, x : x + 1, :], up[x]) for x in range(CX)])
        behind_y = jnp.stack([jnp.where(ysub == 0, ylo[f, x : x + 1, :], down[x]) for x in range(CX)])
        ahead_z = pltpu.roll(field, NZ - 1, 2)
        behind_z = pltpu.roll(field, 1, 2)
        lap = (ahead_x + behind_x) + (ahead_y + behind_y) + (ahead_z + behind_z) - 6.0 * field
        adv = (
            half[0] * (ahead_x - behind_x)
            + half[1] * (ahead_y - behind_y)
            + half[2] * (ahead_z - behind_z)
        )
        return field + DT * (coef * lap - adv)

    zero = jnp.zeros((COLS, NZ), F32)
    for row in list(range(OFF)) + list(range(OFF + NS, ROWS)):
        state[:, row, :] = zero
    for f in range(NF):
        field = species[f] if f < NSPEC else flow[f - NSPEC]
        moved = transport(f, field)
        if f < NSPEC:
            state[:, OFF + f, :] = moved.reshape(COLS, NZ)
        elif f == NF - 1:
            state[:, OFF + NSPEC, :] = moved.reshape(COLS, NZ)
            temp0[...] = moved.reshape(COLS, NZ)
        else:
            flow_mid[f - NSPEC] = moved

    to_scalar.wait()
    steps = [step_of(plan[1, k]) for k in range(COLS)]
    done = substep([state[k] for k in range(COLS)], steps, forms[...], update[...], energy_col[:, 0:1])
    for k in range(COLS):
        state[k] = done[k]

    for k in range(CAP):
        buf[k] = state[plan[0, k]]

    def some(count, s):
        kinds = [plan[2, k] for k in range(count)]
        cols = [buf[k] for k in range(count)]
        done = substep(cols, [step_of(c) for c in kinds], forms[...], update[...], energy_col[:, 0:1])
        for k in range(count):
            buf[k] = jnp.where(kinds[k] > s, done[k], cols[k])

    def section(s, _):
        many = plan[2, CAP // 2] > s

        @pl.when(many)
        def _():
            some(CAP, s)

        @pl.when(jnp.logical_and(jnp.logical_not(many), plan[2, 0] > s))
        def _():
            some(CAP // 2, s)

        return 0

    lax.fori_loop(1, 4, section, 0)

    for k in range(CAP):
        state[plan[0, k]] = buf[k]
    for i in range(NSPEC):
        burnt[i] = state[:, OFF + i, :].reshape(CX, CY, NZ)
    to_out = pltpu.make_async_copy(burnt, species_out, sems.at[1])
    to_out.start()
    last = state[:, OFF + NSPEC, :]
    flow_mid[4] = last.reshape(CX, CY, NZ)
    source = (last - temp0[...]) * (1.0 / DT)
    for c in near:
        c.wait()
    nt = ((1,), (1,))
    horizontal = flow_mid[1:3].reshape(2 * COLS, NZ)
    fz2, dz2 = (fz[0], fz[1]), (dz[0], dz[1])
    spectra[:, 0, :] = dot3(fz2, parts(horizontal), nt)
    vertical = flow_mid[3].reshape(COLS, NZ)
    third = dot3(dz2, parts(vertical), nt) - dot3(fz2, parts(source), nt)
    spectra[:, 1, :] = jnp.concatenate([third, jnp.zeros_like(third)], axis=1)
    to_out.wait()


def swap_blocks(v):
    rows, lanes = v.shape
    r = lax.broadcasted_iota(jnp.int32, v.shape, 0)
    k = lax.broadcasted_iota(jnp.int32, v.shape, 1) // 8
    for b in (1, 2, 4):
        low_r, low_k = (r & b) == 0, (k & b) == 0
        from_above = pltpu.roll(pltpu.roll(v, b, 0), lanes - 8 * b, 1)
        from_below = pltpu.roll(pltpu.roll(v, rows - b, 0), 8 * b, 1)
        v = jnp.where(low_r == low_k, v, jnp.where(low_r, from_below, from_above))
    return v


def stream_kernel(got, fx, dx, out):
    a = swap_blocks(got[:, 0, :])
    w = swap_blocks(got[:, 1, :])
    upper = lax.broadcasted_iota(jnp.int32, a.shape, 1) < COLS
    fx2, dx2 = (fx[0], fx[1]), (dx[0], dx[1])
    moved = jnp.where(upper, w, a)
    both = dot3(fx2, parts(moved)) + jnp.where(upper, dot3(dx2, parts(a)), 0.0)
    for i in range(4):
        out[i] = both


def solve_kernel(place, got, forth, back, kx2, ky2, fxt, dxt, out):
    full = None
    for i in range(4):
        term = dot3(parts(got[i]), (forth[0, i], forth[1, i]))
        full = term if full is None else full + term
    mode = (place[:, 0:1] % (NZ // 2)).astype(F32) * (2 * np.pi / NZ)
    k2 = kx2[...] + ky2[...] + mode * mode
    mine = jnp.max(place[:, 1:2])
    q = full / jnp.where(k2 > 0, k2, 1.0)
    lines = parts(dot3(parts(q), (back[0, mine], back[1, mine])))
    first = dot3((fxt[0], fxt[1]), lines)
    second = dot3((dxt[0], dxt[1]), lines)
    out[:, 0, :] = swap_blocks(first)
    out[:, 1, :] = swap_blocks(second)


def finish_kernel(got, mid, fz, dz, out):
    fz2, dz2 = (fz[0], fz[1]), (dz[0], dz[1])
    first = parts(jnp.transpose(got[:, 0, :]))
    second = parts(jnp.transpose(got[:, 1, :]))
    a = dot3(second, fz2)[:COLS]
    b = dot3(first, fz2)[COLS:]
    c = dot3(first, dz2)[:COLS]
    out[0] = mid[0]
    out[1] = mid[1] + a.reshape(CX, CY, NZ)
    out[2] = mid[2] + b.reshape(CX, CY, NZ)
    out[3] = mid[3] - c.reshape(CX, CY, NZ)
    out[4] = mid[4]


def far(v):
    return pltpu.with_memory_space_constraint(jnp.asarray(v), pltpu.HBM)


def call(kernel, out_shapes, in_specs, scratch=(), out_specs=None):
    pairs = [v if isinstance(v[0], tuple) else (v, F32) for v in out_shapes]
    out = [jax.ShapeDtypeStruct(*v) for v in pairs]
    one = len(out) == 1
    return pl.pallas_call(
        kernel,
        out_shape=out[0] if one else out,
        in_specs=[VMEM] * in_specs if isinstance(in_specs, int) else in_specs,
        out_specs=VMEM if one else out_specs or [VMEM] * len(out),
        scratch_shapes=list(scratch),
        compiler_params=pltpu.CompilerParams(vmem_limit_bytes=LIMIT),
    )


def react(fields, halos, classes, diffusivity, left, right, stoich, heat, prefactor, energy, newton, fz, dz):
    row = lambda v: v[None, :]
    bf16 = jnp.bfloat16
    weights = call(
        weights_kernel,
        [
            ((GROUPS * FORM, WIDE), bf16),
            ((2 * ROWS, 192), bf16),
            ((MAIN + 8, NZ), F32),
            ((16, NZ), F32),
            ((8, NZ), jnp.int32),
        ],
        9,
    )(classes, left.T, right.T, stoich.T, row(heat), row(prefactor), row(energy), newton, row(diffusivity))
    return call(
        react_kernel,
        [(NSPEC, CX, CY, NZ), (5, CX, CY, NZ), (NZ, 2, 2 * COLS)],
        [VMEM] * 11 + [HBM] * 2,
        [
            pltpu.VMEM((COLS, ROWS, NZ), F32),
            pltpu.VMEM((COLS, NZ), F32),
            pltpu.VMEM((CAP, ROWS, NZ), F32),
            pltpu.SMEM((8, NZ), jnp.int32),
            pltpu.VMEM((NSPEC, CX, CY, NZ), F32),
            pltpu.VMEM((2, NZ, NZ), bf16),
            pltpu.VMEM((2, NZ, NZ), bf16),
            pltpu.SemaphoreType.DMA((4,)),
        ],
        [HBM, VMEM, VMEM],
    )(*fields, *halos, *weights, far(fz), far(dz))


def ring(axes, n, step):
    return functools.partial(
        lax.ppermute, axis_name=axes, perm=[(i, (i + step) % n) for i in range(n)]
    )


def shards(
    species,
    flow,
    classes,
    diffusivity,
    left,
    right,
    stoich,
    heat,
    prefactor,
    energy,
    newton,
):
    n_gx, n_gy = NX // CX, NY // CY
    edges = call(
        halo_kernel,
        [(NF, 8, NZ)] * 4,
        [HBM] * 2,
        [
            pltpu.VMEM((NSPEC, CX, CY, NZ), F32),
            pltpu.VMEM((5, CX, CY, NZ), F32),
            pltpu.SemaphoreType.DMA((2,)),
        ],
    )(far(species), far(flow))
    ylo = ring(GY, n_gy, 1)(edges[2])
    yhi = ring(GY, n_gy, -1)(edges[3])
    xlo = ring(GX, n_gx, 1)(edges[0])
    xhi = ring(GX, n_gx, -1)(edges[1])

    fz, dz, _ = basis(NZ)
    fy, dy, ky = basis(NY)
    fx, dx, kx = basis(NX)
    f32 = lambda v: np.ascontiguousarray(v, np.float32)

    def table(v):
        v = f32(v)
        hi = v.astype(jnp.bfloat16)
        return np.stack([hi, (v - hi.astype(np.float32)).astype(jnp.bfloat16)])

    y_of = ((np.arange(8)[None, :, None] * 4 + np.arange(4)[:, None, None]) * CY + np.arange(CY)).reshape(4, COLS)
    forth = np.stack([np.concatenate([fy[:, y].T, dy[:, y].T], axis=0) for y in y_of])
    back = np.stack([np.concatenate([fy[:, y], -dy[:, y]], axis=1) for y in y_of])

    species_out, mid, spectra = react(
        (species, flow),
        (xlo, xhi, ylo, yhi),
        classes,
        diffusivity,
        left,
        right,
        stoich,
        heat,
        prefactor,
        energy,
        newton,
        table(fz),
        table(dz),
    )
    place = jnp.stack([lax.axis_index(MODES), lax.axis_index("x")]).astype(jnp.int32)[None, :]
    spectra, place = lax.optimization_barrier((spectra, place))
    got = lax.all_to_all(spectra, MODES, 0, 0, tiled=True)
    lines = call(stream_kernel, [(4, NX, 2 * COLS)], 3)(got, table(fx), table(dx))
    lines = lax.all_to_all(lines, "x", 0, 0, tiled=True)
    grads = call(solve_kernel, [(NX, 2, 2 * COLS)], 8)(
        place,
        lines,
        table(forth),
        table(back),
        f32(kx * kx)[:, None],
        f32(ky * ky)[None, :],
        table(fx.T),
        table(-dx.T),
    )
    got = lax.all_to_all(grads, MODES, 0, 0, tiled=True)
    flow_out = call(finish_kernel, [(5, CX, CY, NZ)], 4)(got, mid, table(fz), table(dz))
    return (species_out, flow_out)


def solution(mesh):
    finer = Mesh(mesh.devices.reshape(8, 2, 8, 4), GX + GY)
    return jax.shard_map(
        shards,
        mesh=finer,
        in_specs=(P(None, GX, GY, None), P(None, GX, GY, None), P(GX, GY)) + (P(),) * 8,
        out_specs=(P(None, GX, GY, None), P(None, GX, GY, None)),
        check_vma=False,
    )
```

```python
import functools

import jax
import jax.numpy as jnp
import numpy as np
from jax import lax
from jax.experimental import pallas as pl
from jax.experimental.pallas import tpu as pltpu
from jax.sharding import Mesh
from jax.sharding import PartitionSpec as P

GX = ("y", "c")
GY = ("z", "x")
MODES = ("y", "c", "z")

NSPEC = 9
NREAC = 19
NS = NSPEC + 1
NF = 14
NX = 128
NY = 256
NZ = 128
CX = 8
CY = 8
COLS = CX * CY
CAP = COLS // 2
DT = 0.25
PRECISE = lax.Precision.HIGHEST
F32 = jnp.float32
VMEM = pl.BlockSpec(memory_space=pltpu.VMEM)
HBM = pl.BlockSpec(memory_space=pltpu.HBM)
LIMIT = 32 * 1024 * 1024


def basis(n):
    j = np.arange(n)
    h = n // 2
    f = np.zeros((n, n))
    k = np.zeros(n)
    f[0] = 1.0 / np.sqrt(n)
    f[h] = (-1.0) ** j / np.sqrt(n)
    for m in range(1, h):
        f[m] = np.sqrt(2.0 / n) * np.cos(2 * np.pi * (m * j % n) / n)
        f[h + m] = np.sqrt(2.0 / n) * np.sin(2 * np.pi * (m * j % n) / n)
        k[m] = k[h + m] = 2 * np.pi * m / n
    d = np.zeros((n, n))
    for m in range(1, h):
        d[m] = k[m] * f[h + m]
        d[h + m] = -k[m] * f[m]
    return f, d, k


def dot(a, b, dims=((1,), (0,))):
    return lax.dot_general(a, b, (dims, ((), ())), precision=PRECISE, preferred_element_type=F32)


def parts(v):
    hi = v.astype(jnp.bfloat16)
    return hi, (v - hi.astype(F32)).astype(jnp.bfloat16)


def dot3(a, b, dims=((1,), (0,))):
    one = lambda p, q: lax.dot_general(p, q, (dims, ((), ())), preferred_element_type=F32)
    return one(a[0], b[0]) + (one(a[0], b[1]) + one(a[1], b[0]))


OFF = 3
ROWS = 16
FORM = 40
MAIN = 16
REST = NREAC - MAIN
GROUPS = 4
WIDE = GROUPS * 3 * ROWS


def one_hot(shape, f):
    r = lax.broadcasted_iota(jnp.int32, shape, 0)
    c = lax.broadcasted_iota(jnp.int32, shape, 1)
    return f(r, c).astype(F32)


def spread(block, height, width, copies, low):
    every = jnp.concatenate([block] * copies, axis=0)
    r = lax.broadcasted_iota(jnp.int32, every.shape, 0)
    c = lax.broadcasted_iota(jnp.int32, every.shape, 1)
    hi, lo = parts(jnp.where(r // height == c // width, every, 0.0))
    return jnp.where(c % width < low, hi.astype(F32), lo.astype(F32)).astype(jnp.bfloat16)


def form_weights(left_t, right_t):
    tn = ((1,), (1,))
    pick_l = one_hot((FORM, NREAC), lambda r, c: r == c + jnp.where(c < MAIN, 0, MAIN))
    pick_r = one_hot((FORM, NREAC), lambda r, c: r == c + jnp.where(c < MAIN, MAIN, MAIN + REST))
    w = dot(pick_l, left_t, tn) + dot(pick_r, right_t, tn)
    wide = dot(w, one_hot((NSPEC, WIDE), lambda r, c: c % ROWS == r + OFF))
    return w, spread(wide, FORM, 3 * ROWS, GROUPS, 2 * ROWS)


def update_weights(w, stoich_t, heat, prefactor, newton):
    both = dot(one_hot((NS, NSPEC), lambda r, c: r == c), stoich_t)
    both = both + one_hot((NS, NREAC), lambda r, c: r == NSPEC) * heat
    msa = dot(newton, both) * (0.5 * prefactor)
    v = dot(msa, one_hot((NREAC, 192), lambda r, c: c % 32 == r))
    v = v - dot(newton, one_hot((NS, 192), lambda r, c: c % 32 == r + NREAC))
    by_forms = dot(w, v[:NSPEC])
    by_rows = dot(one_hot((ROWS, NS), lambda r, c: r == c + OFF), v)
    return spread(jnp.concatenate([by_forms, by_rows], axis=0), FORM + ROWS, 96, 2, 64)


def column_plan(cls):
    pick_x = one_hot((COLS, CX), lambda r, c: r // CY == c)
    pick_y = one_hot((COLS, CY), lambda r, c: r % CY == c)
    class_col = jnp.sum(dot(pick_x, cls) * pick_y, axis=1, keepdims=True)
    rows = dot(cls, pick_y, ((1,), (1,)))
    class_row = jnp.sum(one_hot((CX, COLS), lambda r, c: c // CY == r) * rows, axis=0, keepdims=True)
    ii = lax.broadcasted_iota(jnp.int32, (COLS, COLS), 0).astype(F32)
    jj = lax.broadcasted_iota(jnp.int32, (COLS, COLS), 1).astype(F32)
    rank_col = jnp.sum((class_row * COLS - jj > class_col * COLS - ii).astype(F32), axis=1, keepdims=True)
    at = (rank_col == jj).astype(F32)
    order = jnp.sum(at * ii, axis=0, keepdims=True)
    sorted_class = jnp.sum(at * class_col, axis=0, keepdims=True)
    table = jnp.concatenate([order, class_row, sorted_class, jnp.zeros((5, COLS), F32)], axis=0)
    return jnp.concatenate([table, jnp.zeros_like(table)], axis=1).astype(jnp.int32)


def step_of(c):
    return jnp.where(c == 1, DT, jnp.where(c == 2, DT / 2, jnp.where(c == 3, DT / 3, DT / 4)))


def joined(cols):
    per = len(cols) // GROUPS
    return [jnp.concatenate(cols[g * per : (g + 1) * per], axis=1) for g in range(GROUPS)]


def all_forms(cols, forms):
    stack = []
    for z in joined(cols):
        hi, lo = parts(z)
        stack += [hi, lo, hi]
    t = jnp.dot(forms, jnp.concatenate(stack, axis=0), preferred_element_type=F32)
    return [t[g * FORM : (g + 1) * FORM] for g in range(GROUPS)]


def substep(cols, a, steps, update, energy):
    per = len(cols) // GROUPS
    wide = per * NZ
    z0 = joined(cols)
    h = joined([jnp.full((1, NZ), 1.0, F32) * v for v in steps])
    top = lax.broadcasted_iota(jnp.int32, (8, wide), 0) < REST
    z = z0
    for repeat in range(3):
        pairs = []
        for g in range(GROUPS):
            heat = jnp.tanh(energy * z[g][OFF + NSPEC : OFF + NS])
            p = jnp.tanh(a[g][:MAIN]) * jnp.tanh(a[g][MAIN : 2 * MAIN])
            p = (p + p * heat[:MAIN]) * h[g]
            q = jnp.tanh(a[g][2 * MAIN :])
            q = q * pltpu.roll(q, 8 - REST, 0)
            q = (q + q * heat[MAIN:]) * h[g]
            if repeat:
                d = z[g] - z0[g]
                x = jnp.concatenate([p, jnp.where(top, q, d[:8]), d[8:]], axis=0)
            else:
                zero = jnp.zeros((8, wide), F32)
                x = jnp.concatenate([p, jnp.where(top, q, zero), zero], axis=0)
            hi, lo = parts(x)
            pairs.append(jnp.concatenate([hi, lo, hi], axis=0))
        side = jnp.concatenate([jnp.concatenate(pairs[2 * k : 2 * k + 2], axis=0) for k in range(2)], axis=1)
        change = jnp.dot(update, side, preferred_element_type=F32)
        both = FORM + ROWS
        part = [
            change[(g % 2) * both : (g % 2 + 1) * both, (g // 2) * wide : (g // 2 + 1) * wide] for g in range(GROUPS)
        ]
        a = [a[g] + part[g][:FORM] for g in range(GROUPS)]
        z = [z[g] + part[g][FORM:] for g in range(GROUPS)]
    cut = lambda v: [v[k // per][:, (k % per) * NZ : (k % per + 1) * NZ] for k in range(len(cols))]
    return cut(z), cut(a)


def halo_kernel(species, flow, last_x, first_x, last_y, first_y, own_s, own_f, sems):
    copies = [
        pltpu.make_async_copy(species, own_s, sems.at[0]),
        pltpu.make_async_copy(flow, own_f, sems.at[1]),
    ]
    for c in copies:
        c.start()
    for c in copies:
        c.wait()
    for f in range(NF):
        src, at = (own_s, f) if f < NSPEC else (own_f, f - NSPEC)
        last_x[f] = src[at, CX - 1]
        first_x[f] = src[at, 0]
        last_y[f] = src[at, :, CY - 1, :]
        first_y[f] = src[at, :, 0, :]


def weights_kernel(classes, left_t, right_t, stoich_t, heat, prefactor, energy, newton, diffusivity, forms, update, energy_col, diff, table):
    table[...] = column_plan(classes[...].astype(F32))
    w, forms[...] = form_weights(left_t[...], right_t[...])
    update[...] = update_weights(w, stoich_t[...], heat[...], prefactor[...], newton[...])
    at_e = one_hot((MAIN + 8, NREAC), lambda r, c: r == c)
    col = jnp.sum(at_e * (0.5 * energy[...]), axis=1, keepdims=True)
    energy_col[...] = jnp.broadcast_to(col, (MAIN + 8, NZ))
    col = jnp.sum(one_hot((16, NF), lambda r, c: r == c) * diffusivity[...], axis=1, keepdims=True)
    diff[...] = jnp.broadcast_to(col, (16, NZ))


def react_kernel(
    species,
    flow,
    ylo,
    yhi,
    xlo,
    xhi,
    forms,
    update,
    energy_col,
    diff,
    table,
    fz_far,
    dz_far,
    species_out,
    flow_mid,
    spectra,
    state,
    temp0,
    buf,
    held,
    buf_forms,
    plan,
    burnt,
    fz,
    dz,
    sems,
):
    to_scalar = pltpu.make_async_copy(table, plan, sems.at[0])
    to_scalar.start()
    near = [pltpu.make_async_copy(fz_far, fz, sems.at[2]), pltpu.make_async_copy(dz_far, dz, sems.at[3])]
    for c in near:
        c.start()

    ysub = lax.broadcasted_iota(jnp.int32, (CY, NZ), 0)
    half = [0.5 * flow[c] for c in (1, 2, 3)]

    def transport(f, field):
        coef = diff[f : f + 1, :]
        ahead_x = jnp.concatenate([field[1:], xhi[f][None]], axis=0)
        behind_x = jnp.concatenate([xlo[f][None], field[:-1]], axis=0)
        up = pltpu.roll(field, CY - 1, 1)
        down = pltpu.roll(field, 1, 1)
        ahead_y = jnp.stack([jnp.where(ysub == CY - 1, yhi[f, x : x + 1, :], up[x]) for x in range(CX)])
        behind_y = jnp.stack([jnp.where(ysub == 0, ylo[f, x : x + 1, :], down[x]) for x in range(CX)])
        ahead_z = pltpu.roll(field, NZ - 1, 2)
        behind_z = pltpu.roll(field, 1, 2)
        lap = (ahead_x + behind_x) + (ahead_y + behind_y) + (ahead_z + behind_z) - 6.0 * field
        adv = (
            half[0] * (ahead_x - behind_x)
            + half[1] * (ahead_y - behind_y)
            + half[2] * (ahead_z - behind_z)
        )
        return field + DT * (coef * lap - adv)

    zero = jnp.zeros((COLS, NZ), F32)
    for row in list(range(OFF)) + list(range(OFF + NS, ROWS)):
        state[:, row, :] = zero
    for f in range(NF):
        field = species[f] if f < NSPEC else flow[f - NSPEC]
        moved = transport(f, field)
        if f < NSPEC:
            state[:, OFF + f, :] = moved.reshape(COLS, NZ)
        elif f == NF - 1:
            state[:, OFF + NSPEC, :] = moved.reshape(COLS, NZ)
            temp0[...] = moved.reshape(COLS, NZ)
        else:
            flow_mid[f - NSPEC] = moved

    to_scalar.wait()
    steps = [step_of(plan[1, k]) for k in range(COLS)]
    cols = [state[k] for k in range(COLS)]
    done, lines = substep(cols, all_forms(cols, forms[...]), steps, update[...], energy_col[:, 0:1])
    for k in range(COLS):
        state[k] = done[k]
        held[k] = lines[k]

    for k in range(CAP):
        buf[k] = state[plan[0, k]]
        buf_forms[k] = held[plan[0, k]]

    def some(count, s):
        kinds = [plan[2, k] for k in range(count)]
        cols = [buf[k] for k in range(count)]
        olds = [buf_forms[k] for k in range(count)]
        done, lines = substep(cols, joined(olds), [step_of(c) for c in kinds], update[...], energy_col[:, 0:1])
        for k in range(count):
            buf[k] = jnp.where(kinds[k] > s, done[k], cols[k])
            buf_forms[k] = jnp.where(kinds[k] > s, lines[k], olds[k])

    def section(s, _):
        many = plan[2, CAP // 2] > s

        @pl.when(many)
        def _():
            some(CAP, s)

        @pl.when(jnp.logical_and(jnp.logical_not(many), plan[2, 0] > s))
        def _():
            some(CAP // 2, s)

        return 0

    lax.fori_loop(1, 4, section, 0)

    for k in range(CAP):
        state[plan[0, k]] = buf[k]
    for i in range(NSPEC):
        burnt[i] = state[:, OFF + i, :].reshape(CX, CY, NZ)
    to_out = pltpu.make_async_copy(burnt, species_out, sems.at[1])
    to_out.start()
    last = state[:, OFF + NSPEC, :]
    flow_mid[4] = last.reshape(CX, CY, NZ)
    source = (last - temp0[...]) * (1.0 / DT)
    for c in near:
        c.wait()
    nt = ((1,), (1,))
    horizontal = flow_mid[1:3].reshape(2 * COLS, NZ)
    fz2, dz2 = (fz[0], fz[1]), (dz[0], dz[1])
    spectra[:, 0, :] = dot3(fz2, parts(horizontal), nt)
    vertical = flow_mid[3].reshape(COLS, NZ)
    third = dot3(dz2, parts(vertical), nt) - dot3(fz2, parts(source), nt)
    spectra[:, 1, :] = jnp.concatenate([third, jnp.zeros_like(third)], axis=1)
    to_out.wait()


def swap_blocks(v):
    rows, lanes = v.shape
    r = lax.broadcasted_iota(jnp.int32, v.shape, 0)
    k = lax.broadcasted_iota(jnp.int32, v.shape, 1) // 8
    for b in (1, 2, 4):
        low_r, low_k = (r & b) == 0, (k & b) == 0
        from_above = pltpu.roll(pltpu.roll(v, b, 0), lanes - 8 * b, 1)
        from_below = pltpu.roll(pltpu.roll(v, rows - b, 0), 8 * b, 1)
        v = jnp.where(low_r == low_k, v, jnp.where(low_r, from_below, from_above))
    return v


def stream_kernel(got, fx, dx, out):
    a = swap_blocks(got[:, 0, :])
    w = swap_blocks(got[:, 1, :])
    upper = lax.broadcasted_iota(jnp.int32, a.shape, 1) < COLS
    fx2, dx2 = (fx[0], fx[1]), (dx[0], dx[1])
    moved = jnp.where(upper, w, a)
    both = dot3(fx2, parts(moved)) + jnp.where(upper, dot3(dx2, parts(a)), 0.0)
    for i in range(4):
        out[i] = both


def solve_kernel(place, got, forth, back, kx2, ky2, fxt, dxt, out):
    full = None
    for i in range(4):
        term = dot3(parts(got[i]), (forth[0, i], forth[1, i]))
        full = term if full is None else full + term
    mode = (place[:, 0:1] % (NZ // 2)).astype(F32) * (2 * np.pi / NZ)
    k2 = kx2[...] + ky2[...] + mode * mode
    mine = jnp.max(place[:, 1:2])
    q = full / jnp.where(k2 > 0, k2, 1.0)
    lines = parts(dot3(parts(q), (back[0, mine], back[1, mine])))
    first = dot3((fxt[0], fxt[1]), lines)
    second = dot3((dxt[0], dxt[1]), lines)
    out[:, 0, :] = swap_blocks(first)
    out[:, 1, :] = swap_blocks(second)


def finish_kernel(got, mid, fz, dz, out):
    fz2, dz2 = (fz[0], fz[1]), (dz[0], dz[1])
    first = parts(jnp.transpose(got[:, 0, :]))
    second = parts(jnp.transpose(got[:, 1, :]))
    a = dot3(second, fz2)[:COLS]
    b = dot3(first, fz2)[COLS:]
    c = dot3(first, dz2)[:COLS]
    out[0] = mid[0]
    out[1] = mid[1] + a.reshape(CX, CY, NZ)
    out[2] = mid[2] + b.reshape(CX, CY, NZ)
    out[3] = mid[3] - c.reshape(CX, CY, NZ)
    out[4] = mid[4]


def far(v):
    return pltpu.with_memory_space_constraint(jnp.asarray(v), pltpu.HBM)


def call(kernel, out_shapes, in_specs, scratch=(), out_specs=None):
    pairs = [v if isinstance(v[0], tuple) else (v, F32) for v in out_shapes]
    out = [jax.ShapeDtypeStruct(*v) for v in pairs]
    one = len(out) == 1
    return pl.pallas_call(
        kernel,
        out_shape=out[0] if one else out,
        in_specs=[VMEM] * in_specs if isinstance(in_specs, int) else in_specs,
        out_specs=VMEM if one else out_specs or [VMEM] * len(out),
        scratch_shapes=list(scratch),
        compiler_params=pltpu.CompilerParams(vmem_limit_bytes=LIMIT),
    )


def react(fields, halos, classes, diffusivity, left, right, stoich, heat, prefactor, energy, newton, fz, dz):
    row = lambda v: v[None, :]
    bf16 = jnp.bfloat16
    weights = call(
        weights_kernel,
        [
            ((GROUPS * FORM, WIDE), bf16),
            ((2 * (FORM + ROWS), 192), bf16),
            ((MAIN + 8, NZ), F32),
            ((16, NZ), F32),
            ((8, NZ), jnp.int32),
        ],
        9,
    )(classes, left.T, right.T, stoich.T, row(heat), row(prefactor), row(energy), newton, row(diffusivity))
    return call(
        react_kernel,
        [(NSPEC, CX, CY, NZ), (5, CX, CY, NZ), (NZ, 2, 2 * COLS)],
        [VMEM] * 11 + [HBM] * 2,
        [
            pltpu.VMEM((COLS, ROWS, NZ), F32),
            pltpu.VMEM((COLS, NZ), F32),
            pltpu.VMEM((CAP, ROWS, NZ), F32),
            pltpu.VMEM((COLS, FORM, NZ), F32),
            pltpu.VMEM((CAP, FORM, NZ), F32),
            pltpu.SMEM((8, NZ), jnp.int32),
            pltpu.VMEM((NSPEC, CX, CY, NZ), F32),
            pltpu.VMEM((2, NZ, NZ), bf16),
            pltpu.VMEM((2, NZ, NZ), bf16),
            pltpu.SemaphoreType.DMA((4,)),
        ],
        [HBM, VMEM, VMEM],
    )(*fields, *halos, *weights, far(fz), far(dz))


def ring(axes, n, step):
    return functools.partial(
        lax.ppermute, axis_name=axes, perm=[(i, (i + step) % n) for i in range(n)]
    )


def shards(
    species,
    flow,
    classes,
    diffusivity,
    left,
    right,
    stoich,
    heat,
    prefactor,
    energy,
    newton,
):
    n_gx, n_gy = NX // CX, NY // CY
    edges = call(
        halo_kernel,
        [(NF, 8, NZ)] * 4,
        [HBM] * 2,
        [
            pltpu.VMEM((NSPEC, CX, CY, NZ), F32),
            pltpu.VMEM((5, CX, CY, NZ), F32),
            pltpu.SemaphoreType.DMA((2,)),
        ],
    )(far(species), far(flow))
    ylo = ring(GY, n_gy, 1)(edges[2])
    yhi = ring(GY, n_gy, -1)(edges[3])
    xlo = ring(GX, n_gx, 1)(edges[0])
    xhi = ring(GX, n_gx, -1)(edges[1])

    fz, dz, _ = basis(NZ)
    fy, dy, ky = basis(NY)
    fx, dx, kx = basis(NX)
    f32 = lambda v: np.ascontiguousarray(v, np.float32)

    def table(v):
        v = f32(v)
        hi = v.astype(jnp.bfloat16)
        return np.stack([hi, (v - hi.astype(np.float32)).astype(jnp.bfloat16)])

    y_of = ((np.arange(8)[None, :, None] * 4 + np.arange(4)[:, None, None]) * CY + np.arange(CY)).reshape(4, COLS)
    forth = np.stack([np.concatenate([fy[:, y].T, dy[:, y].T], axis=0) for y in y_of])
    back = np.stack([np.concatenate([fy[:, y], -dy[:, y]], axis=1) for y in y_of])

    species_out, mid, spectra = react(
        (species, flow),
        (ylo, yhi, xlo, xhi),
        classes,
        diffusivity,
        left,
        right,
        stoich,
        heat,
        prefactor,
        energy,
        newton,
        table(fz),
        table(dz),
    )
    place = jnp.stack([lax.axis_index(MODES), lax.axis_index("x")]).astype(jnp.int32)[None, :]
    spectra, place = lax.optimization_barrier((spectra, place))
    got = lax.all_to_all(spectra, MODES, 0, 0, tiled=True)
    lines = call(stream_kernel, [(4, NX, 2 * COLS)], 3)(got, table(fx), table(dx))
    lines = lax.all_to_all(lines, "x", 0, 0, tiled=True)
    grads = call(solve_kernel, [(NX, 2, 2 * COLS)], 8)(
        place,
        lines,
        table(forth),
        table(back),
        f32(kx * kx)[:, None],
        f32(ky * ky)[None, :],
        table(fx.T),
        table(-dx.T),
    )
    got = lax.all_to_all(grads, MODES, 0, 0, tiled=True)
    flow_out = call(finish_kernel, [(5, CX, CY, NZ)], 4)(got, mid, table(fz), table(dz))
    return (species_out, flow_out)


def solution(mesh):
    finer = Mesh(mesh.devices.reshape(8, 2, 8, 4), GX + GY)
    return jax.shard_map(
        shards,
        mesh=finer,
        in_specs=(P(None, GX, GY, None), P(None, GX, GY, None), P(GX, GY)) + (P(),) * 8,
        out_specs=(P(None, GX, GY, None), P(None, GX, GY, None)),
        check_vma=False,
    )
```

```python
import functools

import jax
import jax.numpy as jnp
import numpy as np
from jax import lax
from jax.experimental import pallas as pl
from jax.experimental.pallas import tpu as pltpu
from jax.sharding import Mesh
from jax.sharding import PartitionSpec as P

GX = ("y", "c")
GY = ("z", "x")
MODES = ("y", "c", "z")

NSPEC = 9
NREAC = 19
NS = NSPEC + 1
NF = 14
NX = 128
NY = 256
NZ = 128
CX = 8
CY = 8
COLS = CX * CY
CAP = COLS // 2
DT = 0.25
PRECISE = lax.Precision.HIGHEST
F32 = jnp.float32
VMEM = pl.BlockSpec(memory_space=pltpu.VMEM)
HBM = pl.BlockSpec(memory_space=pltpu.HBM)
LIMIT = 32 * 1024 * 1024


def basis(n):
    j = np.arange(n)
    h = n // 2
    f = np.zeros((n, n))
    k = np.zeros(n)
    f[0] = 1.0 / np.sqrt(n)
    f[h] = (-1.0) ** j / np.sqrt(n)
    for m in range(1, h):
        f[m] = np.sqrt(2.0 / n) * np.cos(2 * np.pi * (m * j % n) / n)
        f[h + m] = np.sqrt(2.0 / n) * np.sin(2 * np.pi * (m * j % n) / n)
        k[m] = k[h + m] = 2 * np.pi * m / n
    d = np.zeros((n, n))
    for m in range(1, h):
        d[m] = k[m] * f[h + m]
        d[h + m] = -k[m] * f[m]
    return f, d, k


def dot(a, b, dims=((1,), (0,))):
    return lax.dot_general(a, b, (dims, ((), ())), precision=PRECISE, preferred_element_type=F32)


def parts(v):
    hi = v.astype(jnp.bfloat16)
    return hi, (v - hi.astype(F32)).astype(jnp.bfloat16)


def dot3(a, b, dims=((1,), (0,))):
    one = lambda p, q: lax.dot_general(p, q, (dims, ((), ())), preferred_element_type=F32)
    return one(a[0], b[0]) + (one(a[0], b[1]) + one(a[1], b[0]))


OFF = 3
ROWS = 16
FORM = 40
MAIN = 16
REST = NREAC - MAIN
GROUPS = 4
CHANGE = FORM + ROWS + 8
WIDE = GROUPS * 3 * ROWS


def one_hot(shape, f):
    r = lax.broadcasted_iota(jnp.int32, shape, 0)
    c = lax.broadcasted_iota(jnp.int32, shape, 1)
    return f(r, c).astype(F32)


def spread(block, height, width, copies, low):
    every = jnp.concatenate([block] * copies, axis=0)
    r = lax.broadcasted_iota(jnp.int32, every.shape, 0)
    c = lax.broadcasted_iota(jnp.int32, every.shape, 1)
    hi, lo = parts(jnp.where(r // height == c // width, every, 0.0))
    return jnp.where(c % width < low, hi.astype(F32), lo.astype(F32)).astype(jnp.bfloat16)


def form_weights(left_t, right_t):
    tn = ((1,), (1,))
    pick_l = one_hot((FORM, NREAC), lambda r, c: r == c + jnp.where(c < MAIN, 0, MAIN))
    pick_r = one_hot((FORM, NREAC), lambda r, c: r == c + jnp.where(c < MAIN, MAIN, MAIN + REST))
    w = dot(pick_l, left_t, tn) + dot(pick_r, right_t, tn)
    wide = dot(w, one_hot((NSPEC, WIDE), lambda r, c: c % ROWS == r + OFF))
    return w, spread(wide, FORM, 3 * ROWS, GROUPS, 2 * ROWS)


def update_weights(w, stoich_t, heat, prefactor, newton):
    both = dot(one_hot((NS, NSPEC), lambda r, c: r == c), stoich_t)
    both = both + one_hot((NS, NREAC), lambda r, c: r == NSPEC) * heat
    msa = dot(newton, both) * (0.5 * prefactor)
    v = dot(msa, one_hot((NREAC, 192), lambda r, c: c % 32 == r))
    v = v - dot(newton, one_hot((NS, 192), lambda r, c: c % 32 == r + NREAC))
    by_forms = dot(w, v[:NSPEC])
    by_rows = dot(one_hot((ROWS, NS), lambda r, c: r == c + OFF), v)
    block = jnp.concatenate([by_forms, by_rows, jnp.zeros((8, 192), F32)], axis=0)
    return spread(block[:, :96], CHANGE, 96, 1, 64)


def column_plan(cls):
    pick_x = one_hot((COLS, CX), lambda r, c: r // CY == c)
    pick_y = one_hot((COLS, CY), lambda r, c: r % CY == c)
    class_col = jnp.sum(dot(pick_x, cls) * pick_y, axis=1, keepdims=True)
    rows = dot(cls, pick_y, ((1,), (1,)))
    class_row = jnp.sum(one_hot((CX, COLS), lambda r, c: c // CY == r) * rows, axis=0, keepdims=True)
    ii = lax.broadcasted_iota(jnp.int32, (COLS, COLS), 0).astype(F32)
    jj = lax.broadcasted_iota(jnp.int32, (COLS, COLS), 1).astype(F32)
    rank_col = jnp.sum((class_row * COLS - jj > class_col * COLS - ii).astype(F32), axis=1, keepdims=True)
    at = (rank_col == jj).astype(F32)
    order = jnp.sum(at * ii, axis=0, keepdims=True)
    sorted_class = jnp.sum(at * class_col, axis=0, keepdims=True)
    table = jnp.concatenate([order, class_row, sorted_class, jnp.zeros((5, COLS), F32)], axis=0)
    return jnp.concatenate([table, jnp.zeros_like(table)], axis=1).astype(jnp.int32)


def step_of(c):
    return jnp.where(c == 1, DT, jnp.where(c == 2, DT / 2, jnp.where(c == 3, DT / 3, DT / 4)))


def joined(cols):
    per = len(cols) // GROUPS
    return [jnp.concatenate(cols[g * per : (g + 1) * per], axis=1) for g in range(GROUPS)]


def all_forms(cols, forms):
    stack = []
    for z in joined(cols):
        hi, lo = parts(z)
        stack += [hi, lo, hi]
    t = jnp.dot(forms, jnp.concatenate(stack, axis=0), preferred_element_type=F32)
    return [t[g * FORM : (g + 1) * FORM] for g in range(GROUPS)]


def substep(cols, a, steps, update, energy):
    per = len(cols) // GROUPS
    wide = per * NZ
    z0 = joined(cols)
    h = joined([jnp.full((1, NZ), 1.0, F32) * v for v in steps])
    top = lax.broadcasted_iota(jnp.int32, (8, wide), 0) < REST
    z = z0
    for repeat in range(3):
        pairs = []
        for g in range(GROUPS):
            heat = jnp.tanh(energy * z[g][OFF + NSPEC : OFF + NS])
            p = jnp.tanh(a[g][:MAIN]) * jnp.tanh(a[g][MAIN : 2 * MAIN])
            p = (p + p * heat[:MAIN]) * h[g]
            q = jnp.tanh(a[g][2 * MAIN :])
            q = q * pltpu.roll(q, 8 - REST, 0)
            q = (q + q * heat[MAIN:]) * h[g]
            if repeat:
                d = z[g] - z0[g]
                x = jnp.concatenate([p, jnp.where(top, q, d[:8]), d[8:]], axis=0)
            else:
                zero = jnp.zeros((8, wide), F32)
                x = jnp.concatenate([p, jnp.where(top, q, zero), zero], axis=0)
            hi, lo = parts(x)
            pairs.append(jnp.concatenate([hi, lo, hi], axis=0))
        side = jnp.concatenate(pairs, axis=1)
        change = jnp.dot(update, side, preferred_element_type=F32)
        part = [change[:, g * wide : (g + 1) * wide] for g in range(GROUPS)]
        a = [a[g] + part[g][:FORM] for g in range(GROUPS)]
        z = [z[g] + part[g][FORM : FORM + ROWS] for g in range(GROUPS)]
    cut = lambda v: [v[k // per][:, (k % per) * NZ : (k % per + 1) * NZ] for k in range(len(cols))]
    return cut(z), cut(a)


def halo_kernel(species, flow, last_x, first_x, last_y, first_y, own_s, own_f, sems):
    copies = [
        pltpu.make_async_copy(species, own_s, sems.at[0]),
        pltpu.make_async_copy(flow, own_f, sems.at[1]),
    ]
    for c in copies:
        c.start()
    for c in copies:
        c.wait()
    for f in range(NF):
        src, at = (own_s, f) if f < NSPEC else (own_f, f - NSPEC)
        last_x[f] = src[at, CX - 1]
        first_x[f] = src[at, 0]
        last_y[f] = src[at, :, CY - 1, :]
        first_y[f] = src[at, :, 0, :]


def weights_kernel(classes, left_t, right_t, stoich_t, heat, prefactor, energy, newton, diffusivity, forms, update, energy_col, diff, table):
    table[...] = column_plan(classes[...].astype(F32))
    w, forms[...] = form_weights(left_t[...], right_t[...])
    update[...] = update_weights(w, stoich_t[...], heat[...], prefactor[...], newton[...])
    at_e = one_hot((MAIN + 8, NREAC), lambda r, c: r == c)
    col = jnp.sum(at_e * (0.5 * energy[...]), axis=1, keepdims=True)
    energy_col[...] = jnp.broadcast_to(col, (MAIN + 8, NZ))
    col = jnp.sum(one_hot((16, NF), lambda r, c: r == c) * diffusivity[...], axis=1, keepdims=True)
    diff[...] = jnp.broadcast_to(col, (16, NZ))


def react_kernel(
    species,
    flow,
    ylo,
    yhi,
    xlo,
    xhi,
    forms,
    update,
    energy_col,
    diff,
    table,
    fz_far,
    dz_far,
    species_out,
    flow_mid,
    spectra,
    state,
    temp0,
    buf,
    held,
    buf_forms,
    plan,
    burnt,
    fz,
    dz,
    sems,
):
    to_scalar = pltpu.make_async_copy(table, plan, sems.at[0])
    to_scalar.start()
    near = [pltpu.make_async_copy(fz_far, fz, sems.at[2]), pltpu.make_async_copy(dz_far, dz, sems.at[3])]
    for c in near:
        c.start()

    ysub = lax.broadcasted_iota(jnp.int32, (CY, NZ), 0)
    half = [0.5 * flow[c] for c in (1, 2, 3)]

    def transport(f, field):
        coef = diff[f : f + 1, :]
        ahead_x = jnp.concatenate([field[1:], xhi[f][None]], axis=0)
        behind_x = jnp.concatenate([xlo[f][None], field[:-1]], axis=0)
        up = pltpu.roll(field, CY - 1, 1)
        down = pltpu.roll(field, 1, 1)
        ahead_y = jnp.stack([jnp.where(ysub == CY - 1, yhi[f, x : x + 1, :], up[x]) for x in range(CX)])
        behind_y = jnp.stack([jnp.where(ysub == 0, ylo[f, x : x + 1, :], down[x]) for x in range(CX)])
        ahead_z = pltpu.roll(field, NZ - 1, 2)
        behind_z = pltpu.roll(field, 1, 2)
        lap = (ahead_x + behind_x) + (ahead_y + behind_y) + (ahead_z + behind_z) - 6.0 * field
        adv = (
            half[0] * (ahead_x - behind_x)
            + half[1] * (ahead_y - behind_y)
            + half[2] * (ahead_z - behind_z)
        )
        return field + DT * (coef * lap - adv)

    zero = jnp.zeros((COLS, NZ), F32)
    for row in list(range(OFF)) + list(range(OFF + NS, ROWS)):
        state[:, row, :] = zero
    for f in range(NF):
        field = species[f] if f < NSPEC else flow[f - NSPEC]
        moved = transport(f, field)
        if f < NSPEC:
            state[:, OFF + f, :] = moved.reshape(COLS, NZ)
        elif f == NF - 1:
            state[:, OFF + NSPEC, :] = moved.reshape(COLS, NZ)
            temp0[...] = moved.reshape(COLS, NZ)
        else:
            flow_mid[f - NSPEC] = moved

    to_scalar.wait()
    steps = [step_of(plan[1, k]) for k in range(COLS)]
    cols = [state[k] for k in range(COLS)]
    done, lines = substep(cols, all_forms(cols, forms[...]), steps, update[...], energy_col[:, 0:1])
    for k in range(COLS):
        state[k] = done[k]
        held[k] = lines[k]

    for k in range(CAP):
        buf[k] = state[plan[0, k]]
        buf_forms[k] = held[plan[0, k]]

    def some(count, s):
        kinds = [plan[2, k] for k in range(count)]
        cols = [buf[k] for k in range(count)]
        olds = [buf_forms[k] for k in range(count)]
        done, lines = substep(cols, joined(olds), [step_of(c) for c in kinds], update[...], energy_col[:, 0:1])
        for k in range(count):
            buf[k] = jnp.where(kinds[k] > s, done[k], cols[k])
            buf_forms[k] = jnp.where(kinds[k] > s, lines[k], olds[k])

    def section(s, _):
        many = plan[2, CAP // 2] > s

        @pl.when(many)
        def _():
            some(CAP, s)

        @pl.when(jnp.logical_and(jnp.logical_not(many), plan[2, 0] > s))
        def _():
            some(CAP // 2, s)

        return 0

    lax.fori_loop(1, 4, section, 0)

    for k in range(CAP):
        state[plan[0, k]] = buf[k]
    for i in range(NSPEC):
        burnt[i] = state[:, OFF + i, :].reshape(CX, CY, NZ)
    to_out = pltpu.make_async_copy(burnt, species_out, sems.at[1])
    to_out.start()
    last = state[:, OFF + NSPEC, :]
    flow_mid[4] = last.reshape(CX, CY, NZ)
    source = (last - temp0[...]) * (1.0 / DT)
    for c in near:
        c.wait()
    nt = ((1,), (1,))
    horizontal = flow_mid[1:3].reshape(2 * COLS, NZ)
    fz2, dz2 = (fz[0], fz[1]), (dz[0], dz[1])
    spectra[:, 0, :] = dot3(fz2, parts(horizontal), nt)
    vertical = flow_mid[3].reshape(COLS, NZ)
    third = dot3(dz2, parts(vertical), nt) - dot3(fz2, parts(source), nt)
    spectra[:, 1, :] = jnp.concatenate([third, jnp.zeros_like(third)], axis=1)
    to_out.wait()


def swap_blocks(v):
    rows, lanes = v.shape
    r = lax.broadcasted_iota(jnp.int32, v.shape, 0)
    k = lax.broadcasted_iota(jnp.int32, v.shape, 1) // 8
    for b in (1, 2, 4):
        low_r, low_k = (r & b) == 0, (k & b) == 0
        from_above = pltpu.roll(pltpu.roll(v, b, 0), lanes - 8 * b, 1)
        from_below = pltpu.roll(pltpu.roll(v, rows - b, 0), 8 * b, 1)
        v = jnp.where(low_r == low_k, v, jnp.where(low_r, from_below, from_above))
    return v


def stream_kernel(got, fx, dx, out):
    a = swap_blocks(got[:, 0, :])
    w = swap_blocks(got[:, 1, :])
    upper = lax.broadcasted_iota(jnp.int32, a.shape, 1) < COLS
    fx2, dx2 = (fx[0], fx[1]), (dx[0], dx[1])
    moved = jnp.where(upper, w, a)
    both = dot3(fx2, parts(moved)) + jnp.where(upper, dot3(dx2, parts(a)), 0.0)
    for i in range(4):
        out[i] = both


def once(a, b):
    return jnp.dot(a, b, preferred_element_type=F32)


def solve_kernel(place, got, forth, back, kx2, ky2, left, out):
    hi, lo = parts(jnp.concatenate([got[i] for i in range(4)], axis=1))
    full = once(jnp.concatenate([hi, hi, lo], axis=1), forth[...])
    mode = (place[:, 0:1] % (NZ // 2)).astype(F32) * (2 * np.pi / NZ)
    k2 = kx2[...] + ky2[...] + mode * mode
    mine = jnp.max(place[:, 1:2])
    hi, lo = parts(full / jnp.where(k2 > 0, k2, 1.0))
    hi, lo = parts(once(jnp.concatenate([hi, hi, lo], axis=1), back[mine]))
    lines = once(left[...], jnp.concatenate([hi, lo, hi], axis=0))
    out[:, 0, :] = swap_blocks(lines[:NX])
    out[:, 1, :] = swap_blocks(lines[NX:])


def finish_kernel(got, mid, fz, dz, out):
    fz2, dz2 = (fz[0], fz[1]), (dz[0], dz[1])
    first = parts(jnp.transpose(got[:, 0, :]))
    second = parts(jnp.transpose(got[:, 1, :]))
    a = dot3(second, fz2)[:COLS]
    b = dot3(first, fz2)[COLS:]
    c = dot3(first, dz2)[:COLS]
    out[0] = mid[0]
    out[1] = mid[1] + a.reshape(CX, CY, NZ)
    out[2] = mid[2] + b.reshape(CX, CY, NZ)
    out[3] = mid[3] - c.reshape(CX, CY, NZ)
    out[4] = mid[4]


def far(v):
    return pltpu.with_memory_space_constraint(jnp.asarray(v), pltpu.HBM)


def call(kernel, out_shapes, in_specs, scratch=(), out_specs=None):
    pairs = [v if isinstance(v[0], tuple) else (v, F32) for v in out_shapes]
    out = [jax.ShapeDtypeStruct(*v) for v in pairs]
    one = len(out) == 1
    return pl.pallas_call(
        kernel,
        out_shape=out[0] if one else out,
        in_specs=[VMEM] * in_specs if isinstance(in_specs, int) else in_specs,
        out_specs=VMEM if one else out_specs or [VMEM] * len(out),
        scratch_shapes=list(scratch),
        compiler_params=pltpu.CompilerParams(vmem_limit_bytes=LIMIT),
    )


def react(fields, halos, classes, diffusivity, left, right, stoich, heat, prefactor, energy, newton, fz, dz):
    row = lambda v: v[None, :]
    bf16 = jnp.bfloat16
    weights = call(
        weights_kernel,
        [
            ((GROUPS * FORM, WIDE), bf16),
            ((CHANGE, 96), bf16),
            ((MAIN + 8, NZ), F32),
            ((16, NZ), F32),
            ((8, NZ), jnp.int32),
        ],
        9,
    )(classes, left.T, right.T, stoich.T, row(heat), row(prefactor), row(energy), newton, row(diffusivity))
    return call(
        react_kernel,
        [(NSPEC, CX, CY, NZ), (5, CX, CY, NZ), (NZ, 2, 2 * COLS)],
        [VMEM] * 11 + [HBM] * 2,
        [
            pltpu.VMEM((COLS, ROWS, NZ), F32),
            pltpu.VMEM((COLS, NZ), F32),
            pltpu.VMEM((CAP, ROWS, NZ), F32),
            pltpu.VMEM((COLS, FORM, NZ), F32),
            pltpu.VMEM((CAP, FORM, NZ), F32),
            pltpu.SMEM((8, NZ), jnp.int32),
            pltpu.VMEM((NSPEC, CX, CY, NZ), F32),
            pltpu.VMEM((2, NZ, NZ), bf16),
            pltpu.VMEM((2, NZ, NZ), bf16),
            pltpu.SemaphoreType.DMA((4,)),
        ],
        [HBM, VMEM, VMEM],
    )(*fields, *halos, *weights, far(fz), far(dz))


def ring(axes, n, step):
    return functools.partial(
        lax.ppermute, axis_name=axes, perm=[(i, (i + step) % n) for i in range(n)]
    )


def shards(
    species,
    flow,
    classes,
    diffusivity,
    left,
    right,
    stoich,
    heat,
    prefactor,
    energy,
    newton,
):
    n_gx, n_gy = NX // CX, NY // CY
    edges = call(
        halo_kernel,
        [(NF, 8, NZ)] * 4,
        [HBM] * 2,
        [
            pltpu.VMEM((NSPEC, CX, CY, NZ), F32),
            pltpu.VMEM((5, CX, CY, NZ), F32),
            pltpu.SemaphoreType.DMA((2,)),
        ],
    )(far(species), far(flow))
    ylo = ring(GY, n_gy, 1)(edges[2])
    yhi = ring(GY, n_gy, -1)(edges[3])
    xlo = ring(GX, n_gx, 1)(edges[0])
    xhi = ring(GX, n_gx, -1)(edges[1])

    fz, dz, _ = basis(NZ)
    fy, dy, ky = basis(NY)
    fx, dx, kx = basis(NX)
    f32 = lambda v: np.ascontiguousarray(v, np.float32)

    def table(v):
        v = f32(v)
        hi = v.astype(jnp.bfloat16)
        return np.stack([hi, (v - hi.astype(np.float32)).astype(jnp.bfloat16)])

    def stacked(v, axis, first=False):
        hi, lo = table(v)
        return np.concatenate([hi, hi, lo] if first else [hi, lo, hi], axis=axis)

    y_of = ((np.arange(8)[None, :, None] * 4 + np.arange(4)[:, None, None]) * CY + np.arange(CY)).reshape(4, COLS)
    forth = np.stack([np.concatenate([fy[:, y].T, dy[:, y].T], axis=0) for y in y_of])
    back = np.stack([np.concatenate([fy[:, y], -dy[:, y]], axis=1) for y in y_of])

    species_out, mid, spectra = react(
        (species, flow),
        (ylo, yhi, xlo, xhi),
        classes,
        diffusivity,
        left,
        right,
        stoich,
        heat,
        prefactor,
        energy,
        newton,
        table(fz),
        table(dz),
    )
    place = jnp.stack([lax.axis_index(MODES), lax.axis_index("x")]).astype(jnp.int32)[None, :]
    spectra, place = lax.optimization_barrier((spectra, place))
    got = lax.all_to_all(spectra, MODES, 0, 0, tiled=True)
    lines = call(stream_kernel, [(4, NX, 2 * COLS)], 3)(got, table(fx), table(dx))
    lines = lax.all_to_all(lines, "x", 0, 0, tiled=True)
    grads = call(solve_kernel, [(NX, 2, 2 * COLS)], 7)(
        place,
        lines,
        stacked(forth.reshape(-1, NY), 0),
        stacked(back, 1),
        f32(kx * kx)[:, None],
        f32(ky * ky)[None, :],
        stacked(np.concatenate([fx.T, -dx.T], axis=0), 1, first=True),
    )
    got = lax.all_to_all(grads, MODES, 0, 0, tiled=True)
    flow_out = call(finish_kernel, [(5, CX, CY, NZ)], 4)(got, mid, table(fz), table(dz))
    return (species_out, flow_out)


def solution(mesh):
    finer = Mesh(mesh.devices.reshape(8, 2, 8, 4), GX + GY)
    return jax.shard_map(
        shards,
        mesh=finer,
        in_specs=(P(None, GX, GY, None), P(None, GX, GY, None), P(GX, GY)) + (P(),) * 8,
        out_specs=(P(None, GX, GY, None), P(None, GX, GY, None)),
        check_vma=False,
    )
```

```python
import functools

import jax
import jax.numpy as jnp
import numpy as np
from jax import lax
from jax.experimental import pallas as pl
from jax.experimental.pallas import tpu as pltpu
from jax.sharding import Mesh
from jax.sharding import PartitionSpec as P

GX = ("y", "c")
GY = ("z", "x")
MODES = ("y", "c", "z")

NSPEC = 9
NREAC = 19
NS = NSPEC + 1
NF = 14
NX = 128
NY = 256
NZ = 128
CX = 8
CY = 8
COLS = CX * CY
CAP = COLS // 2
DT = 0.25
PRECISE = lax.Precision.HIGHEST
F32 = jnp.float32
VMEM = pl.BlockSpec(memory_space=pltpu.VMEM)
HBM = pl.BlockSpec(memory_space=pltpu.HBM)
LIMIT = 32 * 1024 * 1024


def basis(n):
    j = np.arange(n)
    h = n // 2
    f = np.zeros((n, n))
    k = np.zeros(n)
    f[0] = 1.0 / np.sqrt(n)
    f[h] = (-1.0) ** j / np.sqrt(n)
    for m in range(1, h):
        f[m] = np.sqrt(2.0 / n) * np.cos(2 * np.pi * (m * j % n) / n)
        f[h + m] = np.sqrt(2.0 / n) * np.sin(2 * np.pi * (m * j % n) / n)
        k[m] = k[h + m] = 2 * np.pi * m / n
    d = np.zeros((n, n))
    for m in range(1, h):
        d[m] = k[m] * f[h + m]
        d[h + m] = -k[m] * f[m]
    return f, d, k


def dot(a, b, dims=((1,), (0,))):
    return lax.dot_general(a, b, (dims, ((), ())), precision=PRECISE, preferred_element_type=F32)


def parts(v):
    hi = v.astype(jnp.bfloat16)
    return hi, (v - hi.astype(F32)).astype(jnp.bfloat16)


def dot3(a, b, dims=((1,), (0,))):
    one = lambda p, q: lax.dot_general(p, q, (dims, ((), ())), preferred_element_type=F32)
    return one(a[0], b[0]) + (one(a[0], b[1]) + one(a[1], b[0]))


SMALL = 9
OFF = 3
ROWS = 16
FORM = 40
MAIN = 16
REST = NREAC - MAIN
GROUPS = 4
CHANGE = FORM + ROWS + 8
WIDE = GROUPS * 3 * ROWS


def one_hot(shape, f):
    r = lax.broadcasted_iota(jnp.int32, shape, 0)
    c = lax.broadcasted_iota(jnp.int32, shape, 1)
    return f(r, c).astype(F32)


def spread(block, height, width, copies, low):
    every = jnp.concatenate([block] * copies, axis=0)
    r = lax.broadcasted_iota(jnp.int32, every.shape, 0)
    c = lax.broadcasted_iota(jnp.int32, every.shape, 1)
    hi, lo = parts(jnp.where(r // height == c // width, every, 0.0))
    return jnp.where(c % width < low, hi.astype(F32), lo.astype(F32)).astype(jnp.bfloat16)


def form_weights(left_t, right_t):
    tn = ((1,), (1,))
    pick_l = one_hot((FORM, NREAC), lambda r, c: r == c + jnp.where(c < MAIN, 0, MAIN))
    pick_r = one_hot((FORM, NREAC), lambda r, c: r == c + jnp.where(c < MAIN, MAIN, MAIN + REST))
    w = dot(pick_l, left_t, tn) + dot(pick_r, right_t, tn)
    wide = dot(w, one_hot((NSPEC, WIDE), lambda r, c: c % ROWS == r + OFF))
    return w, spread(wide, FORM, 3 * ROWS, GROUPS, 2 * ROWS)


def update_weights(w, stoich_t, heat, prefactor, newton):
    both = dot(one_hot((NS, NSPEC), lambda r, c: r == c), stoich_t)
    both = both + one_hot((NS, NREAC), lambda r, c: r == NSPEC) * heat
    msa = dot(newton, both) * (0.5 * prefactor)
    v = dot(msa, one_hot((NREAC, 192), lambda r, c: c % 32 == r))
    v = v - dot(newton, one_hot((NS, 192), lambda r, c: c % 32 == r + NREAC))
    by_forms = dot(w, v[:NSPEC])
    by_rows = dot(one_hot((ROWS, NS), lambda r, c: r == c + OFF), v)
    block = jnp.concatenate([by_forms, by_rows, jnp.zeros((8, 192), F32)], axis=0)
    return spread(block[:, :96], CHANGE, 96, 1, 64)


def column_plan(cls):
    pick_x = one_hot((COLS, CX), lambda r, c: r // CY == c)
    pick_y = one_hot((COLS, CY), lambda r, c: r % CY == c)
    class_col = jnp.sum(dot(pick_x, cls) * pick_y, axis=1, keepdims=True)
    rows = dot(cls, pick_y, ((1,), (1,)))
    class_row = jnp.sum(one_hot((CX, COLS), lambda r, c: c // CY == r) * rows, axis=0, keepdims=True)
    ii = lax.broadcasted_iota(jnp.int32, (COLS, COLS), 0).astype(F32)
    jj = lax.broadcasted_iota(jnp.int32, (COLS, COLS), 1).astype(F32)
    rank_col = jnp.sum((class_row * COLS - jj > class_col * COLS - ii).astype(F32), axis=1, keepdims=True)
    at = (rank_col == jj).astype(F32)
    order = jnp.sum(at * ii, axis=0, keepdims=True)
    sorted_class = jnp.sum(at * class_col, axis=0, keepdims=True)
    table = jnp.concatenate([order, class_row, sorted_class, jnp.zeros((5, COLS), F32)], axis=0)
    return jnp.concatenate([table, jnp.zeros_like(table)], axis=1).astype(jnp.int32)


def step_of(c):
    return jnp.where(c == 1, DT, jnp.where(c == 2, DT / 2, jnp.where(c == 3, DT / 3, DT / 4)))


def joined(cols):
    per = len(cols) // GROUPS
    return [jnp.concatenate(cols[g * per : (g + 1) * per], axis=1) for g in range(GROUPS)]


def all_forms(cols, forms):
    stack = []
    for z in joined(cols):
        hi, lo = parts(z)
        stack += [hi, lo, hi]
    t = jnp.dot(forms, jnp.concatenate(stack, axis=0), preferred_element_type=F32)
    return [t[g * FORM : (g + 1) * FORM] for g in range(GROUPS)]


def substep(cols, a, steps, update, energy):
    per = len(cols) // GROUPS
    wide = per * NZ
    z0 = joined(cols)
    h = joined([jnp.full((1, NZ), 1.0, F32) * v for v in steps])
    top = lax.broadcasted_iota(jnp.int32, (8, wide), 0) < REST
    z = z0
    for repeat in range(3):
        pairs = []
        for g in range(GROUPS):
            heat = jnp.tanh(energy * z[g][OFF + NSPEC : OFF + NS])
            p = jnp.tanh(a[g][:MAIN]) * jnp.tanh(a[g][MAIN : 2 * MAIN])
            p = (p + p * heat[:MAIN]) * h[g]
            q = jnp.tanh(a[g][2 * MAIN :])
            q = q * pltpu.roll(q, 8 - REST, 0)
            q = (q + q * heat[MAIN:]) * h[g]
            if repeat:
                d = z[g] - z0[g]
                x = jnp.concatenate([p, jnp.where(top, q, d[:8]), d[8:]], axis=0)
            else:
                zero = jnp.zeros((8, wide), F32)
                x = jnp.concatenate([p, jnp.where(top, q, zero), zero], axis=0)
            hi, lo = parts(x)
            pairs.append(jnp.concatenate([hi, lo, hi], axis=0))
        side = jnp.concatenate(pairs, axis=1)
        change = jnp.dot(update, side, preferred_element_type=F32)
        part = [change[:, g * wide : (g + 1) * wide] for g in range(GROUPS)]
        a = [a[g] + part[g][:FORM] for g in range(GROUPS)]
        z = [z[g] + part[g][FORM : FORM + ROWS] for g in range(GROUPS)]
    cut = lambda v: [v[k // per][:, (k % per) * NZ : (k % per + 1) * NZ] for k in range(len(cols))]
    return cut(z), cut(a)


def halo_kernel(species, flow, *refs):
    small, (last_x, first_x, last_y, first_y) = refs[:SMALL], refs[SMALL : SMALL + 4]
    small_out, (own_s, own_f, sems) = refs[SMALL + 4 : -3], refs[-3:]
    pairs = [(species, own_s), (flow, own_f)] + list(zip(small, small_out))
    copies = [pltpu.make_async_copy(a, b, sems.at[k]) for k, (a, b) in enumerate(pairs)]
    for c in copies:
        c.start()
    for c in copies:
        c.wait()
    for f in range(NF):
        src, at = (own_s, f) if f < NSPEC else (own_f, f - NSPEC)
        last_x[f] = src[at, CX - 1]
        first_x[f] = src[at, 0]
        last_y[f] = src[at, :, CY - 1, :]
        first_y[f] = src[at, :, 0, :]


def weights_kernel(classes, left_t, right_t, stoich_t, heat, prefactor, energy, newton, diffusivity, forms, update, energy_col, diff, table):
    table[...] = column_plan(classes[...].astype(F32))
    w, forms[...] = form_weights(left_t[...], right_t[...])
    update[...] = update_weights(w, stoich_t[...], heat[...], prefactor[...], newton[...])
    at_e = one_hot((MAIN + 8, NREAC), lambda r, c: r == c)
    col = jnp.sum(at_e * (0.5 * energy[...]), axis=1, keepdims=True)
    energy_col[...] = jnp.broadcast_to(col, (MAIN + 8, NZ))
    col = jnp.sum(one_hot((16, NF), lambda r, c: r == c) * diffusivity[...], axis=1, keepdims=True)
    diff[...] = jnp.broadcast_to(col, (16, NZ))


def react_kernel(
    species,
    flow,
    xhi,
    ylo,
    yhi,
    xlo,
    forms,
    update,
    energy_col,
    diff,
    table,
    fz_far,
    dz_far,
    species_out,
    flow_mid,
    spectra,
    state,
    temp0,
    buf,
    held,
    buf_forms,
    plan,
    burnt,
    fz,
    dz,
    sems,
):
    to_scalar = pltpu.make_async_copy(table, plan, sems.at[0])
    to_scalar.start()
    near = [pltpu.make_async_copy(fz_far, fz, sems.at[2]), pltpu.make_async_copy(dz_far, dz, sems.at[3])]
    for c in near:
        c.start()

    ysub = lax.broadcasted_iota(jnp.int32, (CY, NZ), 0)
    half = [0.5 * flow[c] for c in (1, 2, 3)]

    def transport(f, field):
        coef = diff[f : f + 1, :]
        ahead_x = jnp.concatenate([field[1:], xhi[f][None]], axis=0)
        behind_x = jnp.concatenate([xlo[f][None], field[:-1]], axis=0)
        up = pltpu.roll(field, CY - 1, 1)
        down = pltpu.roll(field, 1, 1)
        ahead_y = jnp.stack([jnp.where(ysub == CY - 1, yhi[f, x : x + 1, :], up[x]) for x in range(CX)])
        behind_y = jnp.stack([jnp.where(ysub == 0, ylo[f, x : x + 1, :], down[x]) for x in range(CX)])
        ahead_z = pltpu.roll(field, NZ - 1, 2)
        behind_z = pltpu.roll(field, 1, 2)
        lap = (ahead_x + behind_x) + (ahead_y + behind_y) + (ahead_z + behind_z) - 6.0 * field
        adv = (
            half[0] * (ahead_x - behind_x)
            + half[1] * (ahead_y - behind_y)
            + half[2] * (ahead_z - behind_z)
        )
        return field + DT * (coef * lap - adv)

    zero = jnp.zeros((COLS, NZ), F32)
    for row in list(range(OFF)) + list(range(OFF + NS, ROWS)):
        state[:, row, :] = zero
    for f in range(NF):
        field = species[f] if f < NSPEC else flow[f - NSPEC]
        moved = transport(f, field)
        if f < NSPEC:
            state[:, OFF + f, :] = moved.reshape(COLS, NZ)
        elif f == NF - 1:
            state[:, OFF + NSPEC, :] = moved.reshape(COLS, NZ)
            temp0[...] = moved.reshape(COLS, NZ)
        else:
            flow_mid[f - NSPEC] = moved

    to_scalar.wait()
    steps = [step_of(plan[1, k]) for k in range(COLS)]
    cols = [state[k] for k in range(COLS)]
    done, lines = substep(cols, all_forms(cols, forms[...]), steps, update[...], energy_col[:, 0:1])
    for k in range(COLS):
        state[k] = done[k]
        held[k] = lines[k]

    for k in range(CAP):
        buf[k] = state[plan[0, k]]
        buf_forms[k] = held[plan[0, k]]

    def some(count, s):
        kinds = [plan[2, k] for k in range(count)]
        cols = [buf[k] for k in range(count)]
        olds = [buf_forms[k] for k in range(count)]
        done, lines = substep(cols, joined(olds), [step_of(c) for c in kinds], update[...], energy_col[:, 0:1])
        for k in range(count):
            buf[k] = jnp.where(kinds[k] > s, done[k], cols[k])
            buf_forms[k] = jnp.where(kinds[k] > s, lines[k], olds[k])

    def section(s, _):
        many = plan[2, CAP // 2] > s

        @pl.when(many)
        def _():
            some(CAP, s)

        @pl.when(jnp.logical_and(jnp.logical_not(many), plan[2, 0] > s))
        def _():
            some(CAP // 2, s)

        return 0

    lax.fori_loop(1, 4, section, 0)

    for k in range(CAP):
        state[plan[0, k]] = buf[k]
    for i in range(NSPEC):
        burnt[i] = state[:, OFF + i, :].reshape(CX, CY, NZ)
    to_out = pltpu.make_async_copy(burnt, species_out, sems.at[1])
    to_out.start()
    last = state[:, OFF + NSPEC, :]
    flow_mid[4] = last.reshape(CX, CY, NZ)
    source = (last - temp0[...]) * (1.0 / DT)
    for c in near:
        c.wait()
    nt = ((1,), (1,))
    horizontal = flow_mid[1:3].reshape(2 * COLS, NZ)
    fz2, dz2 = (fz[0], fz[1]), (dz[0], dz[1])
    spectra[:, 0, :] = dot3(fz2, parts(horizontal), nt)
    vertical = flow_mid[3].reshape(COLS, NZ)
    third = dot3(dz2, parts(vertical), nt) - dot3(fz2, parts(source), nt)
    spectra[:, 1, :] = jnp.concatenate([third, jnp.zeros_like(third)], axis=1)
    to_out.wait()


def swap_blocks(v):
    rows, lanes = v.shape
    r = lax.broadcasted_iota(jnp.int32, v.shape, 0)
    k = lax.broadcasted_iota(jnp.int32, v.shape, 1) // 8
    for b in (1, 2, 4):
        low_r, low_k = (r & b) == 0, (k & b) == 0
        from_above = pltpu.roll(pltpu.roll(v, b, 0), lanes - 8 * b, 1)
        from_below = pltpu.roll(pltpu.roll(v, rows - b, 0), 8 * b, 1)
        v = jnp.where(low_r == low_k, v, jnp.where(low_r, from_below, from_above))
    return v


def stream_kernel(got, fx, dx, out):
    a = swap_blocks(got[:, 0, :])
    w = swap_blocks(got[:, 1, :])
    upper = lax.broadcasted_iota(jnp.int32, a.shape, 1) < COLS
    fx2, dx2 = (fx[0], fx[1]), (dx[0], dx[1])
    moved = jnp.where(upper, w, a)
    both = dot3(fx2, parts(moved)) + jnp.where(upper, dot3(dx2, parts(a)), 0.0)
    for i in range(4):
        out[i] = both


def once(a, b):
    return jnp.dot(a, b, preferred_element_type=F32)


def solve_kernel(place, got, forth, back, kx2, ky2, left, out):
    hi, lo = parts(jnp.concatenate([got[i] for i in range(4)], axis=1))
    full = once(jnp.concatenate([hi, hi, lo], axis=1), forth[...])
    mode = (place[:, 0:1] % (NZ // 2)).astype(F32) * (2 * np.pi / NZ)
    k2 = kx2[...] + ky2[...] + mode * mode
    mine = jnp.max(place[:, 1:2])
    hi, lo = parts(full / jnp.where(k2 > 0, k2, 1.0))
    hi, lo = parts(once(jnp.concatenate([hi, hi, lo], axis=1), back[mine]))
    lines = once(left[...], jnp.concatenate([hi, lo, hi], axis=0))
    out[:, 0, :] = swap_blocks(lines[:NX])
    out[:, 1, :] = swap_blocks(lines[NX:])


def finish_kernel(got, mid, fz, dz, out):
    fz2, dz2 = (fz[0], fz[1]), (dz[0], dz[1])
    first = parts(jnp.transpose(got[:, 0, :]))
    second = parts(jnp.transpose(got[:, 1, :]))
    a = dot3(second, fz2)[:COLS]
    b = dot3(first, fz2)[COLS:]
    c = dot3(first, dz2)[:COLS]
    out[0] = mid[0]
    out[1] = mid[1] + a.reshape(CX, CY, NZ)
    out[2] = mid[2] + b.reshape(CX, CY, NZ)
    out[3] = mid[3] - c.reshape(CX, CY, NZ)
    out[4] = mid[4]


def far(v):
    return pltpu.with_memory_space_constraint(jnp.asarray(v), pltpu.HBM)


def call(kernel, out_shapes, in_specs, scratch=(), out_specs=None):
    pairs = [v if isinstance(v[0], tuple) else (v, F32) for v in out_shapes]
    out = [jax.ShapeDtypeStruct(*v) for v in pairs]
    one = len(out) == 1
    return pl.pallas_call(
        kernel,
        out_shape=out[0] if one else out,
        in_specs=[VMEM] * in_specs if isinstance(in_specs, int) else in_specs,
        out_specs=VMEM if one else out_specs or [VMEM] * len(out),
        scratch_shapes=list(scratch),
        compiler_params=pltpu.CompilerParams(vmem_limit_bytes=LIMIT),
    )


def react(fields, halos, small, fz, dz):
    bf16 = jnp.bfloat16
    weights = call(
        weights_kernel,
        [
            ((GROUPS * FORM, WIDE), bf16),
            ((CHANGE, 96), bf16),
            ((MAIN + 8, NZ), F32),
            ((16, NZ), F32),
            ((8, NZ), jnp.int32),
        ],
        9,
    )(*small)
    return call(
        react_kernel,
        [(NSPEC, CX, CY, NZ), (5, CX, CY, NZ), (NZ, 2, 2 * COLS)],
        [VMEM] * 11 + [HBM] * 2,
        [
            pltpu.VMEM((COLS, ROWS, NZ), F32),
            pltpu.VMEM((COLS, NZ), F32),
            pltpu.VMEM((CAP, ROWS, NZ), F32),
            pltpu.VMEM((COLS, FORM, NZ), F32),
            pltpu.VMEM((CAP, FORM, NZ), F32),
            pltpu.SMEM((8, NZ), jnp.int32),
            pltpu.VMEM((NSPEC, CX, CY, NZ), F32),
            pltpu.VMEM((2, NZ, NZ), bf16),
            pltpu.VMEM((2, NZ, NZ), bf16),
            pltpu.SemaphoreType.DMA((4,)),
        ],
        [HBM, VMEM, VMEM],
    )(*fields, *halos, *weights, far(fz), far(dz))


def ring(axes, n, step):
    return functools.partial(
        lax.ppermute, axis_name=axes, perm=[(i, (i + step) % n) for i in range(n)]
    )


def shards(
    species,
    flow,
    classes,
    diffusivity,
    left,
    right,
    stoich,
    heat,
    prefactor,
    energy,
    newton,
):
    n_gx, n_gy = NX // CX, NY // CY
    row = lambda v: v[None, :]
    small = (
        classes,
        left.T,
        right.T,
        stoich.T,
        row(heat),
        row(prefactor),
        row(energy),
        newton,
        row(diffusivity),
    )
    edges = call(
        halo_kernel,
        [(NF, 8, NZ)] * 4 + [(v.shape, v.dtype) for v in small],
        [HBM] * (2 + SMALL),
        [
            pltpu.VMEM((NSPEC, CX, CY, NZ), F32),
            pltpu.VMEM((5, CX, CY, NZ), F32),
            pltpu.SemaphoreType.DMA((2 + SMALL,)),
        ],
    )(far(species), far(flow), *(far(v) for v in small))
    ylo = ring(GY, n_gy, 1)(edges[2])
    yhi = ring(GY, n_gy, -1)(edges[3])
    xlo = ring(GX, n_gx, 1)(edges[0])
    xhi = ring(GX, n_gx, -1)(edges[1])

    fz, dz, _ = basis(NZ)
    fy, dy, ky = basis(NY)
    fx, dx, kx = basis(NX)
    f32 = lambda v: np.ascontiguousarray(v, np.float32)

    def table(v):
        v = f32(v)
        hi = v.astype(jnp.bfloat16)
        return np.stack([hi, (v - hi.astype(np.float32)).astype(jnp.bfloat16)])

    def stacked(v, axis, first=False):
        hi, lo = table(v)
        return np.concatenate([hi, hi, lo] if first else [hi, lo, hi], axis=axis)

    y_of = ((np.arange(8)[None, :, None] * 4 + np.arange(4)[:, None, None]) * CY + np.arange(CY)).reshape(4, COLS)
    forth = np.stack([np.concatenate([fy[:, y].T, dy[:, y].T], axis=0) for y in y_of])
    back = np.stack([np.concatenate([fy[:, y], -dy[:, y]], axis=1) for y in y_of])

    species_out, mid, spectra = react(
        (species, flow),
        (xhi, ylo, yhi, xlo),
        edges[4:],
        table(fz),
        table(dz),
    )
    place = jnp.stack([lax.axis_index(MODES), lax.axis_index("x")]).astype(jnp.int32)[None, :]
    spectra, place = lax.optimization_barrier((spectra, place))
    got = lax.all_to_all(spectra, MODES, 0, 0, tiled=True)
    lines = call(stream_kernel, [(4, NX, 2 * COLS)], 3)(got, table(fx), table(dx))
    lines = lax.all_to_all(lines, "x", 0, 0, tiled=True)
    grads = call(solve_kernel, [(NX, 2, 2 * COLS)], 7)(
        place,
        lines,
        stacked(forth.reshape(-1, NY), 0),
        stacked(back, 1),
        f32(kx * kx)[:, None],
        f32(ky * ky)[None, :],
        stacked(np.concatenate([fx.T, -dx.T], axis=0), 1, first=True),
    )
    got = lax.all_to_all(grads, MODES, 0, 0, tiled=True)
    flow_out = call(finish_kernel, [(5, CX, CY, NZ)], 4)(got, mid, table(fz), table(dz))
    return (species_out, flow_out)


def solution(mesh):
    finer = Mesh(mesh.devices.reshape(8, 2, 8, 4), GX + GY)
    return jax.shard_map(
        shards,
        mesh=finer,
        in_specs=(P(None, GX, GY, None), P(None, GX, GY, None), P(GX, GY)) + (P(),) * 8,
        out_specs=(P(None, GX, GY, None), P(None, GX, GY, None)),
        check_vma=False,
    )
```

```python
import functools

import jax
import jax.numpy as jnp
import numpy as np
from jax import lax
from jax.experimental import pallas as pl
from jax.experimental.pallas import tpu as pltpu
from jax.sharding import Mesh
from jax.sharding import PartitionSpec as P

GX = ("y", "c")
GY = ("z", "x")
MODES = ("y", "c", "z")

NSPEC = 9
NREAC = 19
NS = NSPEC + 1
NF = 14
NX = 128
NY = 256
NZ = 128
CX = 8
CY = 8
COLS = CX * CY
CAP = COLS // 2
DT = 0.25
PRECISE = lax.Precision.HIGHEST
F32 = jnp.float32
VMEM = pl.BlockSpec(memory_space=pltpu.VMEM)
HBM = pl.BlockSpec(memory_space=pltpu.HBM)
LIMIT = 32 * 1024 * 1024


def basis(n):
    j = np.arange(n)
    h = n // 2
    f = np.zeros((n, n))
    k = np.zeros(n)
    f[0] = 1.0 / np.sqrt(n)
    f[h] = (-1.0) ** j / np.sqrt(n)
    for m in range(1, h):
        f[m] = np.sqrt(2.0 / n) * np.cos(2 * np.pi * (m * j % n) / n)
        f[h + m] = np.sqrt(2.0 / n) * np.sin(2 * np.pi * (m * j % n) / n)
        k[m] = k[h + m] = 2 * np.pi * m / n
    d = np.zeros((n, n))
    for m in range(1, h):
        d[m] = k[m] * f[h + m]
        d[h + m] = -k[m] * f[m]
    return f, d, k


def dot(a, b, dims=((1,), (0,))):
    return lax.dot_general(a, b, (dims, ((), ())), precision=PRECISE, preferred_element_type=F32)


def parts(v):
    hi = v.astype(jnp.bfloat16)
    return hi, (v - hi.astype(F32)).astype(jnp.bfloat16)


def dot3(a, b, dims=((1,), (0,))):
    one = lambda p, q: lax.dot_general(p, q, (dims, ((), ())), preferred_element_type=F32)
    return one(a[0], b[0]) + (one(a[0], b[1]) + one(a[1], b[0]))


SMALL = 9
OFF = 3
ROWS = 16
FORM = 40
MAIN = 16
REST = NREAC - MAIN
GROUPS = 4
CHANGE = FORM + ROWS + 8
WIDE = GROUPS * 3 * ROWS


def one_hot(shape, f):
    r = lax.broadcasted_iota(jnp.int32, shape, 0)
    c = lax.broadcasted_iota(jnp.int32, shape, 1)
    return f(r, c).astype(F32)


def spread(block, height, width, copies, low):
    every = jnp.concatenate([block] * copies, axis=0)
    r = lax.broadcasted_iota(jnp.int32, every.shape, 0)
    c = lax.broadcasted_iota(jnp.int32, every.shape, 1)
    hi, lo = parts(jnp.where(r // height == c // width, every, 0.0))
    return jnp.where(c % width < low, hi.astype(F32), lo.astype(F32)).astype(jnp.bfloat16)


def form_weights(left_t, right_t):
    tn = ((1,), (1,))
    pick_l = one_hot((FORM, NREAC), lambda r, c: r == c + jnp.where(c < MAIN, 0, MAIN))
    pick_r = one_hot((FORM, NREAC), lambda r, c: r == c + jnp.where(c < MAIN, MAIN, MAIN + REST))
    w = dot(pick_l, left_t, tn) + dot(pick_r, right_t, tn)
    wide = dot(w, one_hot((NSPEC, WIDE), lambda r, c: c % ROWS == r + OFF))
    return w, spread(wide, FORM, 3 * ROWS, GROUPS, 2 * ROWS)


def update_weights(w, stoich_t, heat, prefactor, newton):
    both = dot(one_hot((NS, NSPEC), lambda r, c: r == c), stoich_t)
    both = both + one_hot((NS, NREAC), lambda r, c: r == NSPEC) * heat
    msa = dot(newton, both) * (0.5 * prefactor)
    v = dot(msa, one_hot((NREAC, 192), lambda r, c: c % 32 == r))
    v = v - dot(newton, one_hot((NS, 192), lambda r, c: c % 32 == r + NREAC))
    by_forms = dot(w, v[:NSPEC])
    by_rows = dot(one_hot((ROWS, NS), lambda r, c: r == c + OFF), v)
    block = jnp.concatenate([by_forms, by_rows, jnp.zeros((8, 192), F32)], axis=0)
    return spread(block[:, :96], CHANGE, 96, 1, 64)


def column_plan(cls):
    pick_x = one_hot((COLS, CX), lambda r, c: r // CY == c)
    pick_y = one_hot((COLS, CY), lambda r, c: r % CY == c)
    class_col = jnp.sum(dot(pick_x, cls) * pick_y, axis=1, keepdims=True)
    rows = dot(cls, pick_y, ((1,), (1,)))
    class_row = jnp.sum(one_hot((CX, COLS), lambda r, c: c // CY == r) * rows, axis=0, keepdims=True)
    ii = lax.broadcasted_iota(jnp.int32, (COLS, COLS), 0).astype(F32)
    jj = lax.broadcasted_iota(jnp.int32, (COLS, COLS), 1).astype(F32)
    rank_col = jnp.sum((class_row * COLS - jj > class_col * COLS - ii).astype(F32), axis=1, keepdims=True)
    at = (rank_col == jj).astype(F32)
    order = jnp.sum(at * ii, axis=0, keepdims=True)
    sorted_class = jnp.sum(at * class_col, axis=0, keepdims=True)
    table = jnp.concatenate([order, class_row, sorted_class, jnp.zeros((5, COLS), F32)], axis=0)
    return jnp.concatenate([table, jnp.zeros_like(table)], axis=1).astype(jnp.int32)


def step_of(c):
    return jnp.where(c == 1, DT, jnp.where(c == 2, DT / 2, jnp.where(c == 3, DT / 3, DT / 4)))


def joined(cols):
    per = len(cols) // GROUPS
    return [jnp.concatenate(cols[g * per : (g + 1) * per], axis=1) for g in range(GROUPS)]


def all_forms(cols, forms):
    stack = []
    for z in joined(cols):
        hi, lo = parts(z)
        stack += [hi, lo, hi]
    t = jnp.dot(forms, jnp.concatenate(stack, axis=0), preferred_element_type=F32)
    return [t[g * FORM : (g + 1) * FORM] for g in range(GROUPS)]


def substep(cols, a, steps, update, energy):
    per = len(cols) // GROUPS
    wide = per * NZ
    z0 = joined(cols)
    h = joined([jnp.full((1, NZ), 1.0, F32) * v for v in steps])
    top = lax.broadcasted_iota(jnp.int32, (8, wide), 0) < REST
    z = z0
    for repeat in range(3):
        pairs = []
        for g in range(GROUPS):
            heat = jnp.tanh(energy * z[g][OFF + NSPEC : OFF + NS])
            p = jnp.tanh(a[g][:MAIN]) * jnp.tanh(a[g][MAIN : 2 * MAIN])
            p = (p + p * heat[:MAIN]) * h[g]
            q = jnp.tanh(a[g][2 * MAIN :])
            q = q * pltpu.roll(q, 8 - REST, 0)
            q = (q + q * heat[MAIN:]) * h[g]
            if repeat:
                d = z[g] - z0[g]
                x = jnp.concatenate([p, jnp.where(top, q, d[:8]), d[8:]], axis=0)
            else:
                zero = jnp.zeros((8, wide), F32)
                x = jnp.concatenate([p, jnp.where(top, q, zero), zero], axis=0)
            hi, lo = parts(x)
            pairs.append(jnp.concatenate([hi, lo, hi], axis=0))
        side = jnp.concatenate(pairs, axis=1)
        change = jnp.dot(update, side, preferred_element_type=F32)
        part = [change[:, g * wide : (g + 1) * wide] for g in range(GROUPS)]
        a = [a[g] + part[g][:FORM] for g in range(GROUPS)]
        z = [z[g] + part[g][FORM : FORM + ROWS] for g in range(GROUPS)]
    cut = lambda v: [v[k // per][:, (k % per) * NZ : (k % per + 1) * NZ] for k in range(len(cols))]
    return cut(z), cut(a)


def halo_kernel(species, flow, *refs):
    small, (last_x, first_x, last_y, first_y) = refs[:SMALL], refs[SMALL : SMALL + 4]
    small_out, (own_s, own_f, sems) = refs[SMALL + 4 : -3], refs[-3:]
    pairs = [(species, own_s), (flow, own_f)] + list(zip(small, small_out))
    copies = [pltpu.make_async_copy(a, b, sems.at[k]) for k, (a, b) in enumerate(pairs)]
    for c in copies:
        c.start()
    for c in copies:
        c.wait()
    for f in range(NF):
        src, at = (own_s, f) if f < NSPEC else (own_f, f - NSPEC)
        last_x[f] = src[at, CX - 1]
        first_x[f] = src[at, 0]
        last_y[f] = src[at, :, CY - 1, :]
        first_y[f] = src[at, :, 0, :]


def weights_kernel(classes, left_t, right_t, stoich_t, heat, prefactor, energy, newton, diffusivity, forms, update, energy_col, diff, table):
    table[...] = column_plan(classes[...].astype(F32))
    w, forms[...] = form_weights(left_t[...], right_t[...])
    update[...] = update_weights(w, stoich_t[...], heat[...], prefactor[...], newton[...])
    at_e = one_hot((MAIN + 8, NREAC), lambda r, c: r == c)
    col = jnp.sum(at_e * (0.5 * energy[...]), axis=1, keepdims=True)
    energy_col[...] = jnp.broadcast_to(col, (MAIN + 8, NZ))
    col = jnp.sum(one_hot((16, NF), lambda r, c: r == c) * diffusivity[...], axis=1, keepdims=True)
    diff[...] = jnp.broadcast_to(col, (16, NZ))


def react_kernel(
    species,
    flow,
    ylo,
    yhi,
    xhi,
    xlo,
    forms,
    update,
    energy_col,
    diff,
    table,
    fz_far,
    dz_far,
    species_out,
    flow_mid,
    spectra,
    state,
    temp0,
    buf,
    held,
    buf_forms,
    plan,
    burnt,
    fz,
    dz,
    sems,
):
    to_scalar = pltpu.make_async_copy(table, plan, sems.at[0])
    to_scalar.start()
    near = [pltpu.make_async_copy(fz_far, fz, sems.at[2]), pltpu.make_async_copy(dz_far, dz, sems.at[3])]
    for c in near:
        c.start()

    ysub = lax.broadcasted_iota(jnp.int32, (CY, NZ), 0)
    half = [0.5 * flow[c] for c in (1, 2, 3)]

    def transport(f, field):
        coef = diff[f : f + 1, :]
        ahead_x = jnp.concatenate([field[1:], xhi[f][None]], axis=0)
        behind_x = jnp.concatenate([xlo[f][None], field[:-1]], axis=0)
        up = pltpu.roll(field, CY - 1, 1)
        down = pltpu.roll(field, 1, 1)
        ahead_y = jnp.stack([jnp.where(ysub == CY - 1, yhi[f, x : x + 1, :], up[x]) for x in range(CX)])
        behind_y = jnp.stack([jnp.where(ysub == 0, ylo[f, x : x + 1, :], down[x]) for x in range(CX)])
        ahead_z = pltpu.roll(field, NZ - 1, 2)
        behind_z = pltpu.roll(field, 1, 2)
        lap = (ahead_x + behind_x) + (ahead_y + behind_y) + (ahead_z + behind_z) - 6.0 * field
        adv = (
            half[0] * (ahead_x - behind_x)
            + half[1] * (ahead_y - behind_y)
            + half[2] * (ahead_z - behind_z)
        )
        return field + DT * (coef * lap - adv)

    zero = jnp.zeros((COLS, NZ), F32)
    for row in list(range(OFF)) + list(range(OFF + NS, ROWS)):
        state[:, row, :] = zero
    for f in range(NF):
        field = species[f] if f < NSPEC else flow[f - NSPEC]
        moved = transport(f, field)
        if f < NSPEC:
            state[:, OFF + f, :] = moved.reshape(COLS, NZ)
        elif f == NF - 1:
            state[:, OFF + NSPEC, :] = moved.reshape(COLS, NZ)
            temp0[...] = moved.reshape(COLS, NZ)
        else:
            flow_mid[f - NSPEC] = moved

    to_scalar.wait()
    steps = [step_of(plan[1, k]) for k in range(COLS)]
    cols = [state[k] for k in range(COLS)]
    done, lines = substep(cols, all_forms(cols, forms[...]), steps, update[...], energy_col[:, 0:1])
    for k in range(COLS):
        state[k] = done[k]
        held[k] = lines[k]

    for k in range(CAP):
        buf[k] = state[plan[0, k]]
        buf_forms[k] = held[plan[0, k]]

    def some(count, s):
        kinds = [plan[2, k] for k in range(count)]
        cols = [buf[k] for k in range(count)]
        olds = [buf_forms[k] for k in range(count)]
        done, lines = substep(cols, joined(olds), [step_of(c) for c in kinds], update[...], energy_col[:, 0:1])
        for k in range(count):
            buf[k] = jnp.where(kinds[k] > s, done[k], cols[k])
            buf_forms[k] = jnp.where(kinds[k] > s, lines[k], olds[k])

    def section(s, _):
        many = plan[2, CAP // 2] > s

        @pl.when(many)
        def _():
            some(CAP, s)

        @pl.when(jnp.logical_and(jnp.logical_not(many), plan[2, 0] > s))
        def _():
            some(CAP // 2, s)

        return 0

    lax.fori_loop(1, 4, section, 0)

    for k in range(CAP):
        state[plan[0, k]] = buf[k]
    for i in range(NSPEC):
        burnt[i] = state[:, OFF + i, :].reshape(CX, CY, NZ)
    to_out = pltpu.make_async_copy(burnt, species_out, sems.at[1])
    to_out.start()
    last = state[:, OFF + NSPEC, :]
    flow_mid[4] = last.reshape(CX, CY, NZ)
    source = (last - temp0[...]) * (1.0 / DT)
    for c in near:
        c.wait()
    nt = ((1,), (1,))
    horizontal = flow_mid[1:3].reshape(2 * COLS, NZ)
    fz2, dz2 = (fz[0], fz[1]), (dz[0], dz[1])
    spectra[:, 0, :] = dot3(fz2, parts(horizontal), nt)
    vertical = flow_mid[3].reshape(COLS, NZ)
    third = dot3(dz2, parts(vertical), nt) - dot3(fz2, parts(source), nt)
    spectra[:, 1, :] = jnp.concatenate([third, jnp.zeros_like(third)], axis=1)
    to_out.wait()


def swap_blocks(v):
    rows, lanes = v.shape
    r = lax.broadcasted_iota(jnp.int32, v.shape, 0)
    k = lax.broadcasted_iota(jnp.int32, v.shape, 1) // 8
    for b in (1, 2, 4):
        low_r, low_k = (r & b) == 0, (k & b) == 0
        from_above = pltpu.roll(pltpu.roll(v, b, 0), lanes - 8 * b, 1)
        from_below = pltpu.roll(pltpu.roll(v, rows - b, 0), 8 * b, 1)
        v = jnp.where(low_r == low_k, v, jnp.where(low_r, from_below, from_above))
    return v


def stream_kernel(got, fx, dx, out):
    a = swap_blocks(got[:, 0, :])
    w = swap_blocks(got[:, 1, :])
    upper = lax.broadcasted_iota(jnp.int32, a.shape, 1) < COLS
    fx2, dx2 = (fx[0], fx[1]), (dx[0], dx[1])
    moved = jnp.where(upper, w, a)
    both = dot3(fx2, parts(moved)) + jnp.where(upper, dot3(dx2, parts(a)), 0.0)
    for i in range(4):
        out[i] = both


def once(a, b):
    return jnp.dot(a, b, preferred_element_type=F32)


def solve_kernel(place, got, forth, back, kx2, ky2, left, out):
    hi, lo = parts(jnp.concatenate([got[i] for i in range(4)], axis=1))
    full = once(jnp.concatenate([hi, hi, lo], axis=1), forth[...])
    mode = (place[:, 0:1] % (NZ // 2)).astype(F32) * (2 * np.pi / NZ)
    k2 = kx2[...] + ky2[...] + mode * mode
    mine = jnp.max(place[:, 1:2])
    hi, lo = parts(full / jnp.where(k2 > 0, k2, 1.0))
    hi, lo = parts(once(jnp.concatenate([hi, hi, lo], axis=1), back[mine]))
    lines = once(left[...], jnp.concatenate([hi, lo, hi], axis=0))
    out[:, 0, :] = swap_blocks(lines[:NX])
    out[:, 1, :] = swap_blocks(lines[NX:])


def finish_kernel(got, mid, fz, dz, out):
    fz2, dz2 = (fz[0], fz[1]), (dz[0], dz[1])
    first = parts(jnp.transpose(got[:, 0, :]))
    second = parts(jnp.transpose(got[:, 1, :]))
    a = dot3(second, fz2)[:COLS]
    b = dot3(first, fz2)[COLS:]
    c = dot3(first, dz2)[:COLS]
    out[0] = mid[0]
    out[1] = mid[1] + a.reshape(CX, CY, NZ)
    out[2] = mid[2] + b.reshape(CX, CY, NZ)
    out[3] = mid[3] - c.reshape(CX, CY, NZ)
    out[4] = mid[4]


def far(v):
    return pltpu.with_memory_space_constraint(jnp.asarray(v), pltpu.HBM)


def call(kernel, out_shapes, in_specs, scratch=(), out_specs=None):
    pairs = [v if isinstance(v[0], tuple) else (v, F32) for v in out_shapes]
    out = [jax.ShapeDtypeStruct(*v) for v in pairs]
    one = len(out) == 1
    return pl.pallas_call(
        kernel,
        out_shape=out[0] if one else out,
        in_specs=[VMEM] * in_specs if isinstance(in_specs, int) else in_specs,
        out_specs=VMEM if one else out_specs or [VMEM] * len(out),
        scratch_shapes=list(scratch),
        compiler_params=pltpu.CompilerParams(vmem_limit_bytes=LIMIT),
    )


def react(fields, halos, small, fz, dz):
    bf16 = jnp.bfloat16
    weights = call(
        weights_kernel,
        [
            ((GROUPS * FORM, WIDE), bf16),
            ((CHANGE, 96), bf16),
            ((MAIN + 8, NZ), F32),
            ((16, NZ), F32),
            ((8, NZ), jnp.int32),
        ],
        9,
    )(*small)
    return call(
        react_kernel,
        [(NSPEC, CX, CY, NZ), (5, CX, CY, NZ), (NZ, 2, 2 * COLS)],
        [VMEM] * 11 + [HBM] * 2,
        [
            pltpu.VMEM((COLS, ROWS, NZ), F32),
            pltpu.VMEM((COLS, NZ), F32),
            pltpu.VMEM((CAP, ROWS, NZ), F32),
            pltpu.VMEM((COLS, FORM, NZ), F32),
            pltpu.VMEM((CAP, FORM, NZ), F32),
            pltpu.SMEM((8, NZ), jnp.int32),
            pltpu.VMEM((NSPEC, CX, CY, NZ), F32),
            pltpu.VMEM((2, NZ, NZ), bf16),
            pltpu.VMEM((2, NZ, NZ), bf16),
            pltpu.SemaphoreType.DMA((4,)),
        ],
        [HBM, VMEM, VMEM],
    )(*fields, *halos, *weights, far(fz), far(dz))


def ring(axes, n, step):
    return functools.partial(
        lax.ppermute, axis_name=axes, perm=[(i, (i + step) % n) for i in range(n)]
    )


def shards(
    species,
    flow,
    classes,
    diffusivity,
    left,
    right,
    stoich,
    heat,
    prefactor,
    energy,
    newton,
):
    n_gx, n_gy = NX // CX, NY // CY
    row = lambda v: v[None, :]
    small = (
        classes,
        left.T,
        right.T,
        stoich.T,
        row(heat),
        row(prefactor),
        row(energy),
        newton,
        row(diffusivity),
    )
    edges = call(
        halo_kernel,
        [(NF, 8, NZ)] * 4 + [(v.shape, v.dtype) for v in small] + [species.shape, flow.shape],
        [HBM] * (2 + SMALL),
        [pltpu.SemaphoreType.DMA((2 + SMALL,))],
    )(far(species), far(flow), *(far(v) for v in small))
    ylo = ring(GY, n_gy, 1)(edges[2])
    yhi = ring(GY, n_gy, -1)(edges[3])
    xlo = ring(GX, n_gx, 1)(edges[0])
    xhi = ring(GX, n_gx, -1)(edges[1])

    fz, dz, _ = basis(NZ)
    fy, dy, ky = basis(NY)
    fx, dx, kx = basis(NX)
    f32 = lambda v: np.ascontiguousarray(v, np.float32)

    def table(v):
        v = f32(v)
        hi = v.astype(jnp.bfloat16)
        return np.stack([hi, (v - hi.astype(np.float32)).astype(jnp.bfloat16)])

    def stacked(v, axis, first=False):
        hi, lo = table(v)
        return np.concatenate([hi, hi, lo] if first else [hi, lo, hi], axis=axis)

    y_of = ((np.arange(8)[None, :, None] * 4 + np.arange(4)[:, None, None]) * CY + np.arange(CY)).reshape(4, COLS)
    forth = np.stack([np.concatenate([fy[:, y].T, dy[:, y].T], axis=0) for y in y_of])
    back = np.stack([np.concatenate([fy[:, y], -dy[:, y]], axis=1) for y in y_of])

    species_out, mid, spectra = react(
        edges[-2:],
        (ylo, yhi, xhi, xlo),
        edges[4:-2],
        table(fz),
        table(dz),
    )
    place = jnp.stack([lax.axis_index(MODES), lax.axis_index("x")]).astype(jnp.int32)[None, :]
    spectra, place = lax.optimization_barrier((spectra, place))
    got = lax.all_to_all(spectra, MODES, 0, 0, tiled=True)
    lines = call(stream_kernel, [(4, NX, 2 * COLS)], 3)(got, table(fx), table(dx))
    lines = lax.all_to_all(lines, "x", 0, 0, tiled=True)
    grads = call(solve_kernel, [(NX, 2, 2 * COLS)], 7)(
        place,
        lines,
        stacked(forth.reshape(-1, NY), 0),
        stacked(back, 1),
        f32(kx * kx)[:, None],
        f32(ky * ky)[None, :],
        stacked(np.concatenate([fx.T, -dx.T], axis=0), 1, first=True),
    )
    got = lax.all_to_all(grads, MODES, 0, 0, tiled=True)
    flow_out = call(finish_kernel, [(5, CX, CY, NZ)], 4)(got, mid, table(fz), table(dz))
    return (species_out, flow_out)


def solution(mesh):
    finer = Mesh(mesh.devices.reshape(8, 2, 8, 4), GX + GY)
    return jax.shard_map(
        shards,
        mesh=finer,
        in_specs=(P(None, GX, GY, None), P(None, GX, GY, None), P(GX, GY)) + (P(),) * 8,
        out_specs=(P(None, GX, GY, None), P(None, GX, GY, None)),
        check_vma=False,
    )
```

```python
import functools

import jax
import jax.numpy as jnp
import numpy as np
from jax import lax
from jax.experimental import pallas as pl
from jax.experimental.pallas import tpu as pltpu
from jax.sharding import Mesh
from jax.sharding import PartitionSpec as P

GX = ("y", "c")
GY = ("z", "x")
MODES = ("y", "c", "z")

NSPEC = 9
NREAC = 19
NS = NSPEC + 1
NF = 14
NX = 128
NY = 256
NZ = 128
CX = 8
CY = 8
COLS = CX * CY
CAP = COLS // 2
DT = 0.25
PRECISE = lax.Precision.HIGHEST
F32 = jnp.float32
VMEM = pl.BlockSpec(memory_space=pltpu.VMEM)
HBM = pl.BlockSpec(memory_space=pltpu.HBM)
LIMIT = 32 * 1024 * 1024


def basis(n):
    j = np.arange(n)
    h = n // 2
    f = np.zeros((n, n))
    k = np.zeros(n)
    f[0] = 1.0 / np.sqrt(n)
    f[h] = (-1.0) ** j / np.sqrt(n)
    for m in range(1, h):
        f[m] = np.sqrt(2.0 / n) * np.cos(2 * np.pi * (m * j % n) / n)
        f[h + m] = np.sqrt(2.0 / n) * np.sin(2 * np.pi * (m * j % n) / n)
        k[m] = k[h + m] = 2 * np.pi * m / n
    d = np.zeros((n, n))
    for m in range(1, h):
        d[m] = k[m] * f[h + m]
        d[h + m] = -k[m] * f[m]
    return f, d, k


def dot(a, b, dims=((1,), (0,))):
    return lax.dot_general(a, b, (dims, ((), ())), precision=PRECISE, preferred_element_type=F32)


def parts(v):
    hi = v.astype(jnp.bfloat16)
    return hi, (v - hi.astype(F32)).astype(jnp.bfloat16)


def dot3(a, b, dims=((1,), (0,))):
    one = lambda p, q: lax.dot_general(p, q, (dims, ((), ())), preferred_element_type=F32)
    return one(a[0], b[0]) + (one(a[0], b[1]) + one(a[1], b[0]))


SMALL = 9
OFF = 3
ROWS = 16
FORM = 40
MAIN = 16
REST = NREAC - MAIN
GROUPS = 4
CHANGE = FORM + ROWS + 8
WIDE = GROUPS * 3 * ROWS


def one_hot(shape, f):
    r = lax.broadcasted_iota(jnp.int32, shape, 0)
    c = lax.broadcasted_iota(jnp.int32, shape, 1)
    return f(r, c).astype(F32)


def spread(block, height, width, copies, low):
    every = jnp.concatenate([block] * copies, axis=0)
    r = lax.broadcasted_iota(jnp.int32, every.shape, 0)
    c = lax.broadcasted_iota(jnp.int32, every.shape, 1)
    hi, lo = parts(jnp.where(r // height == c // width, every, 0.0))
    return jnp.where(c % width < low, hi.astype(F32), lo.astype(F32)).astype(jnp.bfloat16)


def form_weights(left_t, right_t):
    tn = ((1,), (1,))
    pick_l = one_hot((FORM, NREAC), lambda r, c: r == c + jnp.where(c < MAIN, 0, MAIN))
    pick_r = one_hot((FORM, NREAC), lambda r, c: r == c + jnp.where(c < MAIN, MAIN, MAIN + REST))
    w = dot(pick_l, left_t, tn) + dot(pick_r, right_t, tn)
    wide = dot(w, one_hot((NSPEC, WIDE), lambda r, c: c % ROWS == r + OFF))
    return w, spread(wide, FORM, 3 * ROWS, GROUPS, 2 * ROWS)


def update_weights(w, stoich_t, heat, prefactor, newton):
    both = dot(one_hot((NS, NSPEC), lambda r, c: r == c), stoich_t)
    both = both + one_hot((NS, NREAC), lambda r, c: r == NSPEC) * heat
    msa = dot(newton, both) * (0.5 * prefactor)
    v = dot(msa, one_hot((NREAC, 192), lambda r, c: c % 32 == r))
    v = v - dot(newton, one_hot((NS, 192), lambda r, c: c % 32 == r + NREAC))
    by_forms = dot(w, v[:NSPEC])
    by_rows = dot(one_hot((ROWS, NS), lambda r, c: r == c + OFF), v)
    block = jnp.concatenate([by_forms, by_rows, jnp.zeros((8, 192), F32)], axis=0)
    return spread(block[:, :96], CHANGE, 96, 1, 64)


def column_plan(cls):
    pick_x = one_hot((COLS, CX), lambda r, c: r // CY == c)
    pick_y = one_hot((COLS, CY), lambda r, c: r % CY == c)
    class_col = jnp.sum(dot(pick_x, cls) * pick_y, axis=1, keepdims=True)
    rows = dot(cls, pick_y, ((1,), (1,)))
    class_row = jnp.sum(one_hot((CX, COLS), lambda r, c: c // CY == r) * rows, axis=0, keepdims=True)
    ii = lax.broadcasted_iota(jnp.int32, (COLS, COLS), 0).astype(F32)
    jj = lax.broadcasted_iota(jnp.int32, (COLS, COLS), 1).astype(F32)
    rank_col = jnp.sum((class_row * COLS - jj > class_col * COLS - ii).astype(F32), axis=1, keepdims=True)
    at = (rank_col == jj).astype(F32)
    order = jnp.sum(at * ii, axis=0, keepdims=True)
    sorted_class = jnp.sum(at * class_col, axis=0, keepdims=True)
    table = jnp.concatenate([order, class_row, sorted_class, jnp.zeros((5, COLS), F32)], axis=0)
    return jnp.concatenate([table, jnp.zeros_like(table)], axis=1).astype(jnp.int32)


def step_of(c):
    return jnp.where(c == 1, DT, jnp.where(c == 2, DT / 2, jnp.where(c == 3, DT / 3, DT / 4)))


def joined(cols):
    per = len(cols) // GROUPS
    return [jnp.concatenate(cols[g * per : (g + 1) * per], axis=1) for g in range(GROUPS)]


def all_forms(cols, forms):
    stack = []
    for z in joined(cols):
        hi, lo = parts(z)
        stack += [hi, lo, hi]
    t = jnp.dot(forms, jnp.concatenate(stack, axis=0), preferred_element_type=F32)
    return [t[g * FORM : (g + 1) * FORM] for g in range(GROUPS)]


def substep(cols, a, steps, update, energy):
    per = len(cols) // GROUPS
    wide = per * NZ
    z0 = joined(cols)
    h = joined([jnp.full((1, NZ), 1.0, F32) * v for v in steps])
    top = lax.broadcasted_iota(jnp.int32, (8, wide), 0) < REST
    z = z0
    for repeat in range(3):
        pairs = []
        for g in range(GROUPS):
            heat = jnp.tanh(energy * z[g][OFF + NSPEC : OFF + NS])
            p = jnp.tanh(a[g][:MAIN]) * jnp.tanh(a[g][MAIN : 2 * MAIN])
            p = (p + p * heat[:MAIN]) * h[g]
            q = jnp.tanh(a[g][2 * MAIN :])
            q = q * pltpu.roll(q, 8 - REST, 0)
            q = (q + q * heat[MAIN:]) * h[g]
            if repeat:
                d = z[g] - z0[g]
                x = jnp.concatenate([p, jnp.where(top, q, d[:8]), d[8:]], axis=0)
            else:
                zero = jnp.zeros((8, wide), F32)
                x = jnp.concatenate([p, jnp.where(top, q, zero), zero], axis=0)
            hi, lo = parts(x)
            pairs.append(jnp.concatenate([hi, lo, hi], axis=0))
        side = jnp.concatenate(pairs, axis=1)
        change = jnp.dot(update, side, preferred_element_type=F32)
        part = [change[:, g * wide : (g + 1) * wide] for g in range(GROUPS)]
        a = [a[g] + part[g][:FORM] for g in range(GROUPS)]
        z = [z[g] + part[g][FORM : FORM + ROWS] for g in range(GROUPS)]
    cut = lambda v: [v[k // per][:, (k % per) * NZ : (k % per + 1) * NZ] for k in range(len(cols))]
    return cut(z), cut(a)


def is_even(place, k):
    return jnp.broadcast_to(place[:, k : k + 1], (8, NZ)) == 0


def halo_kernel(species, flow, odd, *refs):
    small, (outer_x, inner_x, outer_y, inner_y) = refs[:SMALL], refs[SMALL : SMALL + 4]
    small_out, (own_s, own_f, sems) = refs[SMALL + 4 : -3], refs[-3:]
    pairs = [(species, own_s), (flow, own_f)] + list(zip(small, small_out))
    copies = [pltpu.make_async_copy(a, b, sems.at[k]) for k, (a, b) in enumerate(pairs)]
    for c in copies:
        c.start()
    for c in copies:
        c.wait()
    for f in range(NF):
        src, at = (own_s, f) if f < NSPEC else (own_f, f - NSPEC)
        last_x, first_x = src[at, CX - 1], src[at, 0]
        last_y, first_y = src[at, :, CY - 1, :], src[at, :, 0, :]
        outer_x[f] = jnp.where(is_even(odd, 0), first_x, last_x)
        inner_x[f] = jnp.where(is_even(odd, 0), last_x, first_x)
        outer_y[f] = jnp.where(is_even(odd, 1), first_y, last_y)
        inner_y[f] = jnp.where(is_even(odd, 1), last_y, first_y)


def weights_kernel(classes, left_t, right_t, stoich_t, heat, prefactor, energy, newton, diffusivity, forms, update, energy_col, diff, table):
    table[...] = column_plan(classes[...].astype(F32))
    w, forms[...] = form_weights(left_t[...], right_t[...])
    update[...] = update_weights(w, stoich_t[...], heat[...], prefactor[...], newton[...])
    at_e = one_hot((MAIN + 8, NREAC), lambda r, c: r == c)
    col = jnp.sum(at_e * (0.5 * energy[...]), axis=1, keepdims=True)
    energy_col[...] = jnp.broadcast_to(col, (MAIN + 8, NZ))
    col = jnp.sum(one_hot((16, NF), lambda r, c: r == c) * diffusivity[...], axis=1, keepdims=True)
    diff[...] = jnp.broadcast_to(col, (16, NZ))


def react_kernel(
    species,
    flow,
    outer_y,
    outer_x,
    inner_y,
    inner_x,
    odd,
    forms,
    update,
    energy_col,
    diff,
    table,
    fz_far,
    dz_far,
    species_out,
    flow_mid,
    spectra,
    state,
    temp0,
    buf,
    held,
    buf_forms,
    plan,
    burnt,
    fz,
    dz,
    sems,
):
    to_scalar = pltpu.make_async_copy(table, plan, sems.at[0])
    to_scalar.start()
    near = [pltpu.make_async_copy(fz_far, fz, sems.at[2]), pltpu.make_async_copy(dz_far, dz, sems.at[3])]
    for c in near:
        c.start()

    ysub = lax.broadcasted_iota(jnp.int32, (CY, NZ), 0)
    half = [0.5 * flow[c] for c in (1, 2, 3)]

    def transport(f, field):
        coef = diff[f : f + 1, :]
        xlo = jnp.where(is_even(odd, 0), outer_x[f], inner_x[f])
        xhi = jnp.where(is_even(odd, 0), inner_x[f], outer_x[f])
        ylo = jnp.where(is_even(odd, 1), outer_y[f], inner_y[f])
        yhi = jnp.where(is_even(odd, 1), inner_y[f], outer_y[f])
        ahead_x = jnp.concatenate([field[1:], xhi[None]], axis=0)
        behind_x = jnp.concatenate([xlo[None], field[:-1]], axis=0)
        up = pltpu.roll(field, CY - 1, 1)
        down = pltpu.roll(field, 1, 1)
        ahead_y = jnp.stack([jnp.where(ysub == CY - 1, yhi[x : x + 1, :], up[x]) for x in range(CX)])
        behind_y = jnp.stack([jnp.where(ysub == 0, ylo[x : x + 1, :], down[x]) for x in range(CX)])
        ahead_z = pltpu.roll(field, NZ - 1, 2)
        behind_z = pltpu.roll(field, 1, 2)
        lap = (ahead_x + behind_x) + (ahead_y + behind_y) + (ahead_z + behind_z) - 6.0 * field
        adv = (
            half[0] * (ahead_x - behind_x)
            + half[1] * (ahead_y - behind_y)
            + half[2] * (ahead_z - behind_z)
        )
        return field + DT * (coef * lap - adv)

    zero = jnp.zeros((COLS, NZ), F32)
    for row in list(range(OFF)) + list(range(OFF + NS, ROWS)):
        state[:, row, :] = zero
    for f in range(NF):
        field = species[f] if f < NSPEC else flow[f - NSPEC]
        moved = transport(f, field)
        if f < NSPEC:
            state[:, OFF + f, :] = moved.reshape(COLS, NZ)
        elif f == NF - 1:
            state[:, OFF + NSPEC, :] = moved.reshape(COLS, NZ)
            temp0[...] = moved.reshape(COLS, NZ)
        else:
            flow_mid[f - NSPEC] = moved

    to_scalar.wait()
    steps = [step_of(plan[1, k]) for k in range(COLS)]
    cols = [state[k] for k in range(COLS)]
    done, lines = substep(cols, all_forms(cols, forms[...]), steps, update[...], energy_col[:, 0:1])
    for k in range(COLS):
        state[k] = done[k]
        held[k] = lines[k]

    for k in range(CAP):
        buf[k] = state[plan[0, k]]
        buf_forms[k] = held[plan[0, k]]

    def some(count, s):
        kinds = [plan[2, k] for k in range(count)]
        cols = [buf[k] for k in range(count)]
        olds = [buf_forms[k] for k in range(count)]
        done, lines = substep(cols, joined(olds), [step_of(c) for c in kinds], update[...], energy_col[:, 0:1])
        for k in range(count):
            buf[k] = jnp.where(kinds[k] > s, done[k], cols[k])
            buf_forms[k] = jnp.where(kinds[k] > s, lines[k], olds[k])

    def section(s, _):
        many = plan[2, CAP // 2] > s

        @pl.when(many)
        def _():
            some(CAP, s)

        @pl.when(jnp.logical_and(jnp.logical_not(many), plan[2, 0] > s))
        def _():
            some(CAP // 2, s)

        return 0

    lax.fori_loop(1, 4, section, 0)

    for k in range(CAP):
        state[plan[0, k]] = buf[k]
    for i in range(NSPEC):
        burnt[i] = state[:, OFF + i, :].reshape(CX, CY, NZ)
    to_out = pltpu.make_async_copy(burnt, species_out, sems.at[1])
    to_out.start()
    last = state[:, OFF + NSPEC, :]
    flow_mid[4] = last.reshape(CX, CY, NZ)
    source = (last - temp0[...]) * (1.0 / DT)
    for c in near:
        c.wait()
    nt = ((1,), (1,))
    horizontal = flow_mid[1:3].reshape(2 * COLS, NZ)
    fz2, dz2 = (fz[0], fz[1]), (dz[0], dz[1])
    spectra[:, 0, :] = dot3(fz2, parts(horizontal), nt)
    vertical = flow_mid[3].reshape(COLS, NZ)
    third = dot3(dz2, parts(vertical), nt) - dot3(fz2, parts(source), nt)
    spectra[:, 1, :] = jnp.concatenate([third, jnp.zeros_like(third)], axis=1)
    to_out.wait()


def swap_blocks(v):
    rows, lanes = v.shape
    r = lax.broadcasted_iota(jnp.int32, v.shape, 0)
    k = lax.broadcasted_iota(jnp.int32, v.shape, 1) // 8
    for b in (1, 2, 4):
        low_r, low_k = (r & b) == 0, (k & b) == 0
        from_above = pltpu.roll(pltpu.roll(v, b, 0), lanes - 8 * b, 1)
        from_below = pltpu.roll(pltpu.roll(v, rows - b, 0), 8 * b, 1)
        v = jnp.where(low_r == low_k, v, jnp.where(low_r, from_below, from_above))
    return v


def stream_kernel(got, fx, dx, out):
    a = swap_blocks(got[:, 0, :])
    w = swap_blocks(got[:, 1, :])
    upper = lax.broadcasted_iota(jnp.int32, a.shape, 1) < COLS
    fx2, dx2 = (fx[0], fx[1]), (dx[0], dx[1])
    moved = jnp.where(upper, w, a)
    both = dot3(fx2, parts(moved)) + jnp.where(upper, dot3(dx2, parts(a)), 0.0)
    for i in range(4):
        out[i] = both


def once(a, b):
    return jnp.dot(a, b, preferred_element_type=F32)


def solve_kernel(place, got, forth, back, kx2, ky2, left, out):
    hi, lo = parts(jnp.concatenate([got[i] for i in range(4)], axis=1))
    full = once(jnp.concatenate([hi, hi, lo], axis=1), forth[...])
    mode = (place[:, 0:1] % (NZ // 2)).astype(F32) * (2 * np.pi / NZ)
    k2 = kx2[...] + ky2[...] + mode * mode
    mine = jnp.max(place[:, 1:2])
    hi, lo = parts(full / jnp.where(k2 > 0, k2, 1.0))
    hi, lo = parts(once(jnp.concatenate([hi, hi, lo], axis=1), back[mine]))
    lines = once(left[...], jnp.concatenate([hi, lo, hi], axis=0))
    out[:, 0, :] = swap_blocks(lines[:NX])
    out[:, 1, :] = swap_blocks(lines[NX:])


def finish_kernel(got, mid, fz, dz, out):
    fz2, dz2 = (fz[0], fz[1]), (dz[0], dz[1])
    first = parts(jnp.transpose(got[:, 0, :]))
    second = parts(jnp.transpose(got[:, 1, :]))
    a = dot3(second, fz2)[:COLS]
    b = dot3(first, fz2)[COLS:]
    c = dot3(first, dz2)[:COLS]
    out[0] = mid[0]
    out[1] = mid[1] + a.reshape(CX, CY, NZ)
    out[2] = mid[2] + b.reshape(CX, CY, NZ)
    out[3] = mid[3] - c.reshape(CX, CY, NZ)
    out[4] = mid[4]


def far(v):
    return pltpu.with_memory_space_constraint(jnp.asarray(v), pltpu.HBM)


def call(kernel, out_shapes, in_specs, scratch=(), out_specs=None):
    pairs = [v if isinstance(v[0], tuple) else (v, F32) for v in out_shapes]
    out = [jax.ShapeDtypeStruct(*v) for v in pairs]
    one = len(out) == 1
    return pl.pallas_call(
        kernel,
        out_shape=out[0] if one else out,
        in_specs=[VMEM] * in_specs if isinstance(in_specs, int) else in_specs,
        out_specs=VMEM if one else out_specs or [VMEM] * len(out),
        scratch_shapes=list(scratch),
        compiler_params=pltpu.CompilerParams(vmem_limit_bytes=LIMIT),
    )


def react(fields, halos, small, fz, dz):
    bf16 = jnp.bfloat16
    weights = call(
        weights_kernel,
        [
            ((GROUPS * FORM, WIDE), bf16),
            ((CHANGE, 96), bf16),
            ((MAIN + 8, NZ), F32),
            ((16, NZ), F32),
            ((8, NZ), jnp.int32),
        ],
        9,
    )(*small)
    return call(
        react_kernel,
        [(NSPEC, CX, CY, NZ), (5, CX, CY, NZ), (NZ, 2, 2 * COLS)],
        [VMEM] * 12 + [HBM] * 2,
        [
            pltpu.VMEM((COLS, ROWS, NZ), F32),
            pltpu.VMEM((COLS, NZ), F32),
            pltpu.VMEM((CAP, ROWS, NZ), F32),
            pltpu.VMEM((COLS, FORM, NZ), F32),
            pltpu.VMEM((CAP, FORM, NZ), F32),
            pltpu.SMEM((8, NZ), jnp.int32),
            pltpu.VMEM((NSPEC, CX, CY, NZ), F32),
            pltpu.VMEM((2, NZ, NZ), bf16),
            pltpu.VMEM((2, NZ, NZ), bf16),
            pltpu.SemaphoreType.DMA((4,)),
        ],
        [HBM, VMEM, VMEM],
    )(*fields, *halos, *weights, far(fz), far(dz))


def swap(axes, n, first):
    pairs = [(k % n, (k + 1) % n) for k in range(first, n + first, 2)]
    return functools.partial(lax.ppermute, axis_name=axes, perm=pairs + [(b, a) for a, b in pairs])


def shards(
    species,
    flow,
    classes,
    diffusivity,
    left,
    right,
    stoich,
    heat,
    prefactor,
    energy,
    newton,
):
    n_gx, n_gy = NX // CX, NY // CY
    odd = (jnp.stack([lax.axis_index(GX), lax.axis_index(GY)]) % 2).astype(jnp.int32)[None, :]
    row = lambda v: v[None, :]
    small = (
        classes,
        left.T,
        right.T,
        stoich.T,
        row(heat),
        row(prefactor),
        row(energy),
        newton,
        row(diffusivity),
    )
    edges = call(
        halo_kernel,
        [(NF, 8, NZ)] * 4 + [(v.shape, v.dtype) for v in small] + [species.shape, flow.shape],
        [HBM] * 2 + [VMEM] + [HBM] * SMALL,
        [pltpu.SemaphoreType.DMA((2 + SMALL,))],
    )(far(species), far(flow), odd, *(far(v) for v in small))
    halos = (
        swap(GY, n_gy, 1)(edges[2]),
        swap(GX, n_gx, 1)(edges[0]),
        swap(GY, n_gy, 0)(edges[3]),
        swap(GX, n_gx, 0)(edges[1]),
        odd,
    )

    fz, dz, _ = basis(NZ)
    fy, dy, ky = basis(NY)
    fx, dx, kx = basis(NX)
    f32 = lambda v: np.ascontiguousarray(v, np.float32)

    def table(v):
        v = f32(v)
        hi = v.astype(jnp.bfloat16)
        return np.stack([hi, (v - hi.astype(np.float32)).astype(jnp.bfloat16)])

    def stacked(v, axis, first=False):
        hi, lo = table(v)
        return np.concatenate([hi, hi, lo] if first else [hi, lo, hi], axis=axis)

    y_of = ((np.arange(8)[None, :, None] * 4 + np.arange(4)[:, None, None]) * CY + np.arange(CY)).reshape(4, COLS)
    forth = np.stack([np.concatenate([fy[:, y].T, dy[:, y].T], axis=0) for y in y_of])
    back = np.stack([np.concatenate([fy[:, y], -dy[:, y]], axis=1) for y in y_of])

    species_out, mid, spectra = react(
        edges[-2:],
        halos,
        edges[4:-2],
        table(fz),
        table(dz),
    )
    place = jnp.stack([lax.axis_index(MODES), lax.axis_index("x")]).astype(jnp.int32)[None, :]
    spectra, place = lax.optimization_barrier((spectra, place))
    got = lax.all_to_all(spectra, MODES, 0, 0, tiled=True)
    lines = call(stream_kernel, [(4, NX, 2 * COLS)], 3)(got, table(fx), table(dx))
    lines = lax.all_to_all(lines, "x", 0, 0, tiled=True)
    grads = call(solve_kernel, [(NX, 2, 2 * COLS)], 7)(
        place,
        lines,
        stacked(forth.reshape(-1, NY), 0),
        stacked(back, 1),
        f32(kx * kx)[:, None],
        f32(ky * ky)[None, :],
        stacked(np.concatenate([fx.T, -dx.T], axis=0), 1, first=True),
    )
    got = lax.all_to_all(grads, MODES, 0, 0, tiled=True)
    flow_out = call(finish_kernel, [(5, CX, CY, NZ)], 4)(got, mid, table(fz), table(dz))
    return (species_out, flow_out)


def solution(mesh):
    finer = Mesh(mesh.devices.reshape(8, 2, 8, 4), GX + GY)
    return jax.shard_map(
        shards,
        mesh=finer,
        in_specs=(P(None, GX, GY, None), P(None, GX, GY, None), P(GX, GY)) + (P(),) * 8,
        out_specs=(P(None, GX, GY, None), P(None, GX, GY, None)),
        check_vma=False,
    )
```

```python
import functools

import jax
import jax.numpy as jnp
import numpy as np
from jax import lax
from jax.experimental import pallas as pl
from jax.experimental.pallas import tpu as pltpu
from jax.sharding import Mesh
from jax.sharding import PartitionSpec as P

GX = ("y", "c")
GY = ("z", "x")
MODES = ("y", "c", "z")

NSPEC = 9
NREAC = 19
NS = NSPEC + 1
NF = 14
NX = 128
NY = 256
NZ = 128
CX = 8
CY = 8
COLS = CX * CY
CAP = COLS // 2
DT = 0.25
PRECISE = lax.Precision.HIGHEST
F32 = jnp.float32
VMEM = pl.BlockSpec(memory_space=pltpu.VMEM)
HBM = pl.BlockSpec(memory_space=pltpu.HBM)
LIMIT = 32 * 1024 * 1024


def basis(n):
    j = np.arange(n)
    h = n // 2
    f = np.zeros((n, n))
    k = np.zeros(n)
    f[0] = 1.0 / np.sqrt(n)
    f[h] = (-1.0) ** j / np.sqrt(n)
    for m in range(1, h):
        f[m] = np.sqrt(2.0 / n) * np.cos(2 * np.pi * (m * j % n) / n)
        f[h + m] = np.sqrt(2.0 / n) * np.sin(2 * np.pi * (m * j % n) / n)
        k[m] = k[h + m] = 2 * np.pi * m / n
    d = np.zeros((n, n))
    for m in range(1, h):
        d[m] = k[m] * f[h + m]
        d[h + m] = -k[m] * f[m]
    return f, d, k


def dot(a, b, dims=((1,), (0,))):
    return lax.dot_general(a, b, (dims, ((), ())), precision=PRECISE, preferred_element_type=F32)


def parts(v):
    hi = v.astype(jnp.bfloat16)
    return hi, (v - hi.astype(F32)).astype(jnp.bfloat16)


def dot3(a, b, dims=((1,), (0,))):
    one = lambda p, q: lax.dot_general(p, q, (dims, ((), ())), preferred_element_type=F32)
    return one(a[0], b[0]) + (one(a[0], b[1]) + one(a[1], b[0]))


SMALL = 9
OFF = 3
ROWS = 16
FORM = 40
MAIN = 16
REST = NREAC - MAIN
GROUPS = 4
CHANGE = FORM + ROWS + 8
WIDE = GROUPS * 3 * ROWS


def one_hot(shape, f):
    r = lax.broadcasted_iota(jnp.int32, shape, 0)
    c = lax.broadcasted_iota(jnp.int32, shape, 1)
    return f(r, c).astype(F32)


def spread(block, height, width, copies, low):
    every = jnp.concatenate([block] * copies, axis=0)
    r = lax.broadcasted_iota(jnp.int32, every.shape, 0)
    c = lax.broadcasted_iota(jnp.int32, every.shape, 1)
    hi, lo = parts(jnp.where(r // height == c // width, every, 0.0))
    return jnp.where(c % width < low, hi.astype(F32), lo.astype(F32)).astype(jnp.bfloat16)


def form_weights(left_t, right_t):
    tn = ((1,), (1,))
    pick_l = one_hot((FORM, NREAC), lambda r, c: r == c + jnp.where(c < MAIN, 0, MAIN))
    pick_r = one_hot((FORM, NREAC), lambda r, c: r == c + jnp.where(c < MAIN, MAIN, MAIN + REST))
    w = dot(pick_l, left_t, tn) + dot(pick_r, right_t, tn)
    wide = dot(w, one_hot((NSPEC, WIDE), lambda r, c: c % ROWS == r + OFF))
    return w, spread(wide, FORM, 3 * ROWS, GROUPS, 2 * ROWS)


def update_weights(w, stoich_t, heat, prefactor, newton):
    both = dot(one_hot((NS, NSPEC), lambda r, c: r == c), stoich_t)
    both = both + one_hot((NS, NREAC), lambda r, c: r == NSPEC) * heat
    msa = dot(newton, both) * (0.5 * prefactor)
    v = dot(msa, one_hot((NREAC, 192), lambda r, c: c % 32 == r))
    v = v - dot(newton, one_hot((NS, 192), lambda r, c: c % 32 == r + NREAC))
    by_forms = dot(w, v[:NSPEC])
    by_rows = dot(one_hot((ROWS, NS), lambda r, c: r == c + OFF), v)
    block = jnp.concatenate([by_forms, by_rows, jnp.zeros((8, 192), F32)], axis=0)
    return spread(block[:, :96], CHANGE, 96, 1, 64)


def column_plan(cls):
    pick_x = one_hot((COLS, CX), lambda r, c: r // CY == c)
    pick_y = one_hot((COLS, CY), lambda r, c: r % CY == c)
    class_col = jnp.sum(dot(pick_x, cls) * pick_y, axis=1, keepdims=True)
    rows = dot(cls, pick_y, ((1,), (1,)))
    class_row = jnp.sum(one_hot((CX, COLS), lambda r, c: c // CY == r) * rows, axis=0, keepdims=True)
    ii = lax.broadcasted_iota(jnp.int32, (COLS, COLS), 0).astype(F32)
    jj = lax.broadcasted_iota(jnp.int32, (COLS, COLS), 1).astype(F32)
    rank_col = jnp.sum((class_row * COLS - jj > class_col * COLS - ii).astype(F32), axis=1, keepdims=True)
    at = (rank_col == jj).astype(F32)
    order = jnp.sum(at * ii, axis=0, keepdims=True)
    sorted_class = jnp.sum(at * class_col, axis=0, keepdims=True)
    table = jnp.concatenate([order, class_row, sorted_class, jnp.zeros((5, COLS), F32)], axis=0)
    return jnp.concatenate([table, jnp.zeros_like(table)], axis=1).astype(jnp.int32)


def step_of(c):
    return jnp.where(c == 1, DT, jnp.where(c == 2, DT / 2, jnp.where(c == 3, DT / 3, DT / 4)))


def joined(cols):
    per = len(cols) // GROUPS
    return [jnp.concatenate(cols[g * per : (g + 1) * per], axis=1) for g in range(GROUPS)]


def all_forms(cols, forms):
    stack = []
    for z in joined(cols):
        hi, lo = parts(z)
        stack += [hi, lo, hi]
    t = jnp.dot(forms, jnp.concatenate(stack, axis=0), preferred_element_type=F32)
    return [t[g * FORM : (g + 1) * FORM] for g in range(GROUPS)]


def substep(cols, a, steps, update, energy):
    per = len(cols) // GROUPS
    wide = per * NZ
    z0 = joined(cols)
    h = joined([jnp.full((1, NZ), 1.0, F32) * v for v in steps])
    top = lax.broadcasted_iota(jnp.int32, (8, wide), 0) < REST
    z = z0
    for repeat in range(3):
        pairs = []
        for g in range(GROUPS):
            heat = jnp.tanh(energy * z[g][OFF + NSPEC : OFF + NS])
            p = jnp.tanh(a[g][:MAIN]) * jnp.tanh(a[g][MAIN : 2 * MAIN])
            p = (p + p * heat[:MAIN]) * h[g]
            q = jnp.tanh(a[g][2 * MAIN :])
            q = q * pltpu.roll(q, 8 - REST, 0)
            q = (q + q * heat[MAIN:]) * h[g]
            if repeat:
                d = z[g] - z0[g]
                x = jnp.concatenate([p, jnp.where(top, q, d[:8]), d[8:]], axis=0)
            else:
                zero = jnp.zeros((8, wide), F32)
                x = jnp.concatenate([p, jnp.where(top, q, zero), zero], axis=0)
            hi, lo = parts(x)
            pairs.append(jnp.concatenate([hi, lo, hi], axis=0))
        side = jnp.concatenate(pairs, axis=1)
        change = jnp.dot(update, side, preferred_element_type=F32)
        part = [change[:, g * wide : (g + 1) * wide] for g in range(GROUPS)]
        a = [a[g] + part[g][:FORM] for g in range(GROUPS)]
        z = [z[g] + part[g][FORM : FORM + ROWS] for g in range(GROUPS)]
    cut = lambda v: [v[k // per][:, (k % per) * NZ : (k % per + 1) * NZ] for k in range(len(cols))]
    return cut(z), cut(a)


def is_even(odd):
    return jnp.broadcast_to(odd[...], (8, NZ)) == 0


def halo_kernel(species, flow, odd, *refs):
    small, (end_x, start_x, outer_y, inner_y) = refs[:SMALL], refs[SMALL : SMALL + 4]
    small_out, (own_s, own_f, sems) = refs[SMALL + 4 : -3], refs[-3:]
    pairs = [(species, own_s), (flow, own_f)] + list(zip(small, small_out))
    copies = [pltpu.make_async_copy(a, b, sems.at[k]) for k, (a, b) in enumerate(pairs)]
    for c in copies:
        c.start()
    for c in copies:
        c.wait()
    for f in range(NF):
        src, at = (own_s, f) if f < NSPEC else (own_f, f - NSPEC)
        last_y, first_y = src[at, :, CY - 1, :], src[at, :, 0, :]
        end_x[f] = src[at, CX - 1]
        start_x[f] = src[at, 0]
        outer_y[f] = jnp.where(is_even(odd), first_y, last_y)
        inner_y[f] = jnp.where(is_even(odd), last_y, first_y)


def weights_kernel(classes, left_t, right_t, stoich_t, heat, prefactor, energy, newton, diffusivity, forms, update, energy_col, diff, table):
    table[...] = column_plan(classes[...].astype(F32))
    w, forms[...] = form_weights(left_t[...], right_t[...])
    update[...] = update_weights(w, stoich_t[...], heat[...], prefactor[...], newton[...])
    at_e = one_hot((MAIN + 8, NREAC), lambda r, c: r == c)
    col = jnp.sum(at_e * (0.5 * energy[...]), axis=1, keepdims=True)
    energy_col[...] = jnp.broadcast_to(col, (MAIN + 8, NZ))
    col = jnp.sum(one_hot((16, NF), lambda r, c: r == c) * diffusivity[...], axis=1, keepdims=True)
    diff[...] = jnp.broadcast_to(col, (16, NZ))


def react_kernel(
    species,
    flow,
    outer_y,
    inner_y,
    xhi,
    xlo,
    odd,
    forms,
    update,
    energy_col,
    diff,
    table,
    fz_far,
    dz_far,
    species_out,
    flow_mid,
    spectra,
    state,
    temp0,
    buf,
    held,
    buf_forms,
    plan,
    burnt,
    fz,
    dz,
    sems,
):
    to_scalar = pltpu.make_async_copy(table, plan, sems.at[0])
    to_scalar.start()
    near = [pltpu.make_async_copy(fz_far, fz, sems.at[2]), pltpu.make_async_copy(dz_far, dz, sems.at[3])]
    for c in near:
        c.start()

    ysub = lax.broadcasted_iota(jnp.int32, (CY, NZ), 0)
    half = [0.5 * flow[c] for c in (1, 2, 3)]

    def transport(f, field):
        coef = diff[f : f + 1, :]
        ylo = jnp.where(is_even(odd), outer_y[f], inner_y[f])
        yhi = jnp.where(is_even(odd), inner_y[f], outer_y[f])
        ahead_x = jnp.concatenate([field[1:], xhi[f][None]], axis=0)
        behind_x = jnp.concatenate([xlo[f][None], field[:-1]], axis=0)
        up = pltpu.roll(field, CY - 1, 1)
        down = pltpu.roll(field, 1, 1)
        ahead_y = jnp.stack([jnp.where(ysub == CY - 1, yhi[x : x + 1, :], up[x]) for x in range(CX)])
        behind_y = jnp.stack([jnp.where(ysub == 0, ylo[x : x + 1, :], down[x]) for x in range(CX)])
        ahead_z = pltpu.roll(field, NZ - 1, 2)
        behind_z = pltpu.roll(field, 1, 2)
        lap = (ahead_x + behind_x) + (ahead_y + behind_y) + (ahead_z + behind_z) - 6.0 * field
        adv = (
            half[0] * (ahead_x - behind_x)
            + half[1] * (ahead_y - behind_y)
            + half[2] * (ahead_z - behind_z)
        )
        return field + DT * (coef * lap - adv)

    zero = jnp.zeros((COLS, NZ), F32)
    for row in list(range(OFF)) + list(range(OFF + NS, ROWS)):
        state[:, row, :] = zero
    for f in range(NF):
        field = species[f] if f < NSPEC else flow[f - NSPEC]
        moved = transport(f, field)
        if f < NSPEC:
            state[:, OFF + f, :] = moved.reshape(COLS, NZ)
        elif f == NF - 1:
            state[:, OFF + NSPEC, :] = moved.reshape(COLS, NZ)
            temp0[...] = moved.reshape(COLS, NZ)
        else:
            flow_mid[f - NSPEC] = moved

    to_scalar.wait()
    steps = [step_of(plan[1, k]) for k in range(COLS)]
    cols = [state[k] for k in range(COLS)]
    done, lines = substep(cols, all_forms(cols, forms[...]), steps, update[...], energy_col[:, 0:1])
    for k in range(COLS):
        state[k] = done[k]
        held[k] = lines[k]

    for k in range(CAP):
        buf[k] = state[plan[0, k]]
        buf_forms[k] = held[plan[0, k]]

    def some(count, s):
        kinds = [plan[2, k] for k in range(count)]
        cols = [buf[k] for k in range(count)]
        olds = [buf_forms[k] for k in range(count)]
        done, lines = substep(cols, joined(olds), [step_of(c) for c in kinds], update[...], energy_col[:, 0:1])
        for k in range(count):
            buf[k] = jnp.where(kinds[k] > s, done[k], cols[k])
            buf_forms[k] = jnp.where(kinds[k] > s, lines[k], olds[k])

    def section(s, _):
        many = plan[2, CAP // 2] > s

        @pl.when(many)
        def _():
            some(CAP, s)

        @pl.when(jnp.logical_and(jnp.logical_not(many), plan[2, 0] > s))
        def _():
            some(CAP // 2, s)

        return 0

    lax.fori_loop(1, 4, section, 0)

    for k in range(CAP):
        state[plan[0, k]] = buf[k]
    for i in range(NSPEC):
        burnt[i] = state[:, OFF + i, :].reshape(CX, CY, NZ)
    to_out = pltpu.make_async_copy(burnt, species_out, sems.at[1])
    to_out.start()
    last = state[:, OFF + NSPEC, :]
    flow_mid[4] = last.reshape(CX, CY, NZ)
    source = (last - temp0[...]) * (1.0 / DT)
    for c in near:
        c.wait()
    nt = ((1,), (1,))
    horizontal = flow_mid[1:3].reshape(2 * COLS, NZ)
    fz2, dz2 = (fz[0], fz[1]), (dz[0], dz[1])
    spectra[:, 0, :] = dot3(fz2, parts(horizontal), nt)
    vertical = flow_mid[3].reshape(COLS, NZ)
    third = dot3(dz2, parts(vertical), nt) - dot3(fz2, parts(source), nt)
    spectra[:, 1, :] = jnp.concatenate([third, jnp.zeros_like(third)], axis=1)
    to_out.wait()


def swap_blocks(v):
    rows, lanes = v.shape
    r = lax.broadcasted_iota(jnp.int32, v.shape, 0)
    k = lax.broadcasted_iota(jnp.int32, v.shape, 1) // 8
    for b in (1, 2, 4):
        low_r, low_k = (r & b) == 0, (k & b) == 0
        from_above = pltpu.roll(pltpu.roll(v, b, 0), lanes - 8 * b, 1)
        from_below = pltpu.roll(pltpu.roll(v, rows - b, 0), 8 * b, 1)
        v = jnp.where(low_r == low_k, v, jnp.where(low_r, from_below, from_above))
    return v


def stream_kernel(got, fx, dx, out):
    a = swap_blocks(got[:, 0, :])
    w = swap_blocks(got[:, 1, :])
    upper = lax.broadcasted_iota(jnp.int32, a.shape, 1) < COLS
    fx2, dx2 = (fx[0], fx[1]), (dx[0], dx[1])
    moved = jnp.where(upper, w, a)
    both = dot3(fx2, parts(moved)) + jnp.where(upper, dot3(dx2, parts(a)), 0.0)
    for i in range(4):
        out[i] = both


def once(a, b):
    return jnp.dot(a, b, preferred_element_type=F32)


def solve_kernel(place, got, forth, back, kx2, ky2, left, out):
    hi, lo = parts(jnp.concatenate([got[i] for i in range(4)], axis=1))
    full = once(jnp.concatenate([hi, hi, lo], axis=1), forth[...])
    mode = (place[:, 0:1] % (NZ // 2)).astype(F32) * (2 * np.pi / NZ)
    k2 = kx2[...] + ky2[...] + mode * mode
    mine = jnp.max(place[:, 1:2])
    hi, lo = parts(full / jnp.where(k2 > 0, k2, 1.0))
    hi, lo = parts(once(jnp.concatenate([hi, hi, lo], axis=1), back[mine]))
    lines = once(left[...], jnp.concatenate([hi, lo, hi], axis=0))
    out[:, 0, :] = swap_blocks(lines[:NX])
    out[:, 1, :] = swap_blocks(lines[NX:])


def finish_kernel(got, mid, fz, dz, out):
    fz2, dz2 = (fz[0], fz[1]), (dz[0], dz[1])
    first = parts(jnp.transpose(got[:, 0, :]))
    second = parts(jnp.transpose(got[:, 1, :]))
    a = dot3(second, fz2)[:COLS]
    b = dot3(first, fz2)[COLS:]
    c = dot3(first, dz2)[:COLS]
    out[0] = mid[0]
    out[1] = mid[1] + a.reshape(CX, CY, NZ)
    out[2] = mid[2] + b.reshape(CX, CY, NZ)
    out[3] = mid[3] - c.reshape(CX, CY, NZ)
    out[4] = mid[4]


def far(v):
    return pltpu.with_memory_space_constraint(jnp.asarray(v), pltpu.HBM)


def call(kernel, out_shapes, in_specs, scratch=(), out_specs=None):
    pairs = [v if isinstance(v[0], tuple) else (v, F32) for v in out_shapes]
    out = [jax.ShapeDtypeStruct(*v) for v in pairs]
    one = len(out) == 1
    return pl.pallas_call(
        kernel,
        out_shape=out[0] if one else out,
        in_specs=[VMEM] * in_specs if isinstance(in_specs, int) else in_specs,
        out_specs=VMEM if one else out_specs or [VMEM] * len(out),
        scratch_shapes=list(scratch),
        compiler_params=pltpu.CompilerParams(vmem_limit_bytes=LIMIT),
    )


def react(fields, halos, small, fz, dz):
    bf16 = jnp.bfloat16
    weights = call(
        weights_kernel,
        [
            ((GROUPS * FORM, WIDE), bf16),
            ((CHANGE, 96), bf16),
            ((MAIN + 8, NZ), F32),
            ((16, NZ), F32),
            ((8, NZ), jnp.int32),
        ],
        9,
    )(*small)
    return call(
        react_kernel,
        [(NSPEC, CX, CY, NZ), (5, CX, CY, NZ), (NZ, 2, 2 * COLS)],
        [VMEM] * 12 + [HBM] * 2,
        [
            pltpu.VMEM((COLS, ROWS, NZ), F32),
            pltpu.VMEM((COLS, NZ), F32),
            pltpu.VMEM((CAP, ROWS, NZ), F32),
            pltpu.VMEM((COLS, FORM, NZ), F32),
            pltpu.VMEM((CAP, FORM, NZ), F32),
            pltpu.SMEM((8, NZ), jnp.int32),
            pltpu.VMEM((NSPEC, CX, CY, NZ), F32),
            pltpu.VMEM((2, NZ, NZ), bf16),
            pltpu.VMEM((2, NZ, NZ), bf16),
            pltpu.SemaphoreType.DMA((4,)),
        ],
        [HBM, VMEM, VMEM],
    )(*fields, *halos, *weights, far(fz), far(dz))


def swap(axes, n, first):
    pairs = [(k % n, (k + 1) % n) for k in range(first, n + first, 2)]
    return functools.partial(lax.ppermute, axis_name=axes, perm=pairs + [(b, a) for a, b in pairs])


def shift(axes, n, step):
    return functools.partial(
        lax.ppermute, axis_name=axes, perm=[(i, (i + step) % n) for i in range(n)]
    )


def shards(
    species,
    flow,
    classes,
    diffusivity,
    left,
    right,
    stoich,
    heat,
    prefactor,
    energy,
    newton,
):
    n_gx, n_gy = NX // CX, NY // CY
    odd = (lax.axis_index(GY) % 2).astype(jnp.int32).reshape(1, 1)
    row = lambda v: v[None, :]
    small = (
        classes,
        left.T,
        right.T,
        stoich.T,
        row(heat),
        row(prefactor),
        row(energy),
        newton,
        row(diffusivity),
    )
    edges = call(
        halo_kernel,
        [(NF, 8, NZ)] * 4 + [(v.shape, v.dtype) for v in small] + [species.shape, flow.shape],
        [HBM] * 2 + [VMEM] + [HBM] * SMALL,
        [pltpu.SemaphoreType.DMA((2 + SMALL,))],
    )(far(species), far(flow), odd, *(far(v) for v in small))
    halos = (
        swap(GY, n_gy, 1)(edges[2]),
        swap(GY, n_gy, 0)(edges[3]),
        shift(GX, n_gx, -1)(edges[1]),
        shift(GX, n_gx, 1)(edges[0]),
        odd,
    )

    fz, dz, _ = basis(NZ)
    fy, dy, ky = basis(NY)
    fx, dx, kx = basis(NX)
    f32 = lambda v: np.ascontiguousarray(v, np.float32)

    def table(v):
        v = f32(v)
        hi = v.astype(jnp.bfloat16)
        return np.stack([hi, (v - hi.astype(np.float32)).astype(jnp.bfloat16)])

    def stacked(v, axis, first=False):
        hi, lo = table(v)
        return np.concatenate([hi, hi, lo] if first else [hi, lo, hi], axis=axis)

    y_of = ((np.arange(8)[None, :, None] * 4 + np.arange(4)[:, None, None]) * CY + np.arange(CY)).reshape(4, COLS)
    forth = np.stack([np.concatenate([fy[:, y].T, dy[:, y].T], axis=0) for y in y_of])
    back = np.stack([np.concatenate([fy[:, y], -dy[:, y]], axis=1) for y in y_of])

    species_out, mid, spectra = react(
        edges[-2:],
        halos,
        edges[4:-2],
        table(fz),
        table(dz),
    )
    place = jnp.stack([lax.axis_index(MODES), lax.axis_index("x")]).astype(jnp.int32)[None, :]
    spectra, place = lax.optimization_barrier((spectra, place))
    got = lax.all_to_all(spectra, MODES, 0, 0, tiled=True)
    lines = call(stream_kernel, [(4, NX, 2 * COLS)], 3)(got, table(fx), table(dx))
    lines = lax.all_to_all(lines, "x", 0, 0, tiled=True)
    grads = call(solve_kernel, [(NX, 2, 2 * COLS)], 7)(
        place,
        lines,
        stacked(forth.reshape(-1, NY), 0),
        stacked(back, 1),
        f32(kx * kx)[:, None],
        f32(ky * ky)[None, :],
        stacked(np.concatenate([fx.T, -dx.T], axis=0), 1, first=True),
    )
    got = lax.all_to_all(grads, MODES, 0, 0, tiled=True)
    flow_out = call(finish_kernel, [(5, CX, CY, NZ)], 4)(got, mid, table(fz), table(dz))
    return (species_out, flow_out)


def solution(mesh):
    finer = Mesh(mesh.devices.reshape(8, 2, 8, 4), GX + GY)
    return jax.shard_map(
        shards,
        mesh=finer,
        in_specs=(P(None, GX, GY, None), P(None, GX, GY, None), P(GX, GY)) + (P(),) * 8,
        out_specs=(P(None, GX, GY, None), P(None, GX, GY, None)),
        check_vma=False,
    )
```

```python
import functools

import jax
import jax.numpy as jnp
import numpy as np
from jax import lax
from jax.experimental import pallas as pl
from jax.experimental.pallas import tpu as pltpu
from jax.sharding import Mesh
from jax.sharding import PartitionSpec as P

GX = ("y", "c")
GY = ("z", "x")
MODES = ("y", "c", "z")

NSPEC = 9
NREAC = 19
NS = NSPEC + 1
NF = 14
NX = 128
NY = 256
NZ = 128
CX = 8
CY = 8
COLS = CX * CY
CAP = COLS // 2
DT = 0.25
PRECISE = lax.Precision.HIGHEST
F32 = jnp.float32
VMEM = pl.BlockSpec(memory_space=pltpu.VMEM)
HBM = pl.BlockSpec(memory_space=pltpu.HBM)
LIMIT = 32 * 1024 * 1024


def basis(n):
    j = np.arange(n)
    h = n // 2
    f = np.zeros((n, n))
    k = np.zeros(n)
    f[0] = 1.0 / np.sqrt(n)
    f[h] = (-1.0) ** j / np.sqrt(n)
    for m in range(1, h):
        f[m] = np.sqrt(2.0 / n) * np.cos(2 * np.pi * (m * j % n) / n)
        f[h + m] = np.sqrt(2.0 / n) * np.sin(2 * np.pi * (m * j % n) / n)
        k[m] = k[h + m] = 2 * np.pi * m / n
    d = np.zeros((n, n))
    for m in range(1, h):
        d[m] = k[m] * f[h + m]
        d[h + m] = -k[m] * f[m]
    return f, d, k


def dot(a, b, dims=((1,), (0,))):
    return lax.dot_general(a, b, (dims, ((), ())), precision=PRECISE, preferred_element_type=F32)


def parts(v):
    hi = v.astype(jnp.bfloat16)
    return hi, (v - hi.astype(F32)).astype(jnp.bfloat16)


def dot3(a, b, dims=((1,), (0,))):
    one = lambda p, q: lax.dot_general(p, q, (dims, ((), ())), preferred_element_type=F32)
    return one(a[0], b[0]) + (one(a[0], b[1]) + one(a[1], b[0]))


SMALL = 9
OFF = 3
ROWS = 16
FORM = 40
MAIN = 16
REST = NREAC - MAIN
GROUPS = 4
CHANGE = FORM + ROWS + 8
WIDE = GROUPS * 3 * ROWS


def one_hot(shape, f):
    r = lax.broadcasted_iota(jnp.int32, shape, 0)
    c = lax.broadcasted_iota(jnp.int32, shape, 1)
    return f(r, c).astype(F32)


def spread(block, height, width, copies, low):
    every = jnp.concatenate([block] * copies, axis=0)
    r = lax.broadcasted_iota(jnp.int32, every.shape, 0)
    c = lax.broadcasted_iota(jnp.int32, every.shape, 1)
    hi, lo = parts(jnp.where(r // height == c // width, every, 0.0))
    return jnp.where(c % width < low, hi.astype(F32), lo.astype(F32)).astype(jnp.bfloat16)


def form_weights(left_t, right_t):
    tn = ((1,), (1,))
    pick_l = one_hot((FORM, NREAC), lambda r, c: r == c + jnp.where(c < MAIN, 0, MAIN))
    pick_r = one_hot((FORM, NREAC), lambda r, c: r == c + jnp.where(c < MAIN, MAIN, MAIN + REST))
    w = dot(pick_l, left_t, tn) + dot(pick_r, right_t, tn)
    wide = dot(w, one_hot((NSPEC, WIDE), lambda r, c: c % ROWS == r + OFF))
    return w, spread(wide, FORM, 3 * ROWS, GROUPS, 2 * ROWS)


def update_weights(w, stoich_t, heat, prefactor, newton):
    both = dot(one_hot((NS, NSPEC), lambda r, c: r == c), stoich_t)
    both = both + one_hot((NS, NREAC), lambda r, c: r == NSPEC) * heat
    msa = dot(newton, both) * (0.5 * prefactor)
    v = dot(msa, one_hot((NREAC, 192), lambda r, c: c % 32 == r))
    v = v - dot(newton, one_hot((NS, 192), lambda r, c: c % 32 == r + NREAC))
    by_forms = dot(w, v[:NSPEC])
    by_rows = dot(one_hot((ROWS, NS), lambda r, c: r == c + OFF), v)
    block = jnp.concatenate([by_forms, by_rows, jnp.zeros((8, 192), F32)], axis=0)
    return spread(block[:, :96], CHANGE, 96, 1, 64)


def column_plan(cls):
    pick_x = one_hot((COLS, CX), lambda r, c: r // CY == c)
    pick_y = one_hot((COLS, CY), lambda r, c: r % CY == c)
    class_col = jnp.sum(dot(pick_x, cls) * pick_y, axis=1, keepdims=True)
    rows = dot(cls, pick_y, ((1,), (1,)))
    class_row = jnp.sum(one_hot((CX, COLS), lambda r, c: c // CY == r) * rows, axis=0, keepdims=True)
    ii = lax.broadcasted_iota(jnp.int32, (COLS, COLS), 0).astype(F32)
    jj = lax.broadcasted_iota(jnp.int32, (COLS, COLS), 1).astype(F32)
    rank_col = jnp.sum((class_row * COLS - jj > class_col * COLS - ii).astype(F32), axis=1, keepdims=True)
    at = (rank_col == jj).astype(F32)
    order = jnp.sum(at * ii, axis=0, keepdims=True)
    sorted_class = jnp.sum(at * class_col, axis=0, keepdims=True)
    table = jnp.concatenate([order, class_row, sorted_class, jnp.zeros((5, COLS), F32)], axis=0)
    return jnp.concatenate([table, jnp.zeros_like(table)], axis=1).astype(jnp.int32)


def step_of(c):
    return jnp.where(c == 1, DT, jnp.where(c == 2, DT / 2, jnp.where(c == 3, DT / 3, DT / 4)))


def joined(cols):
    per = len(cols) // GROUPS
    return [jnp.concatenate(cols[g * per : (g + 1) * per], axis=1) for g in range(GROUPS)]


def all_forms(cols, forms):
    stack = []
    for z in joined(cols):
        hi, lo = parts(z)
        stack += [hi, lo, hi]
    t = jnp.dot(forms, jnp.concatenate(stack, axis=0), preferred_element_type=F32)
    return [t[g * FORM : (g + 1) * FORM] for g in range(GROUPS)]


def substep(cols, a, steps, update, energy):
    per = len(cols) // GROUPS
    wide = per * NZ
    z0 = joined(cols)
    h = joined([jnp.full((1, NZ), 1.0, F32) * v for v in steps])
    top = lax.broadcasted_iota(jnp.int32, (8, wide), 0) < REST
    z = z0
    for repeat in range(3):
        pairs = []
        for g in range(GROUPS):
            heat = jnp.tanh(energy * z[g][OFF + NSPEC : OFF + NS])
            p = jnp.tanh(a[g][:MAIN]) * jnp.tanh(a[g][MAIN : 2 * MAIN])
            p = (p + p * heat[:MAIN]) * h[g]
            q = jnp.tanh(a[g][2 * MAIN :])
            q = q * pltpu.roll(q, 8 - REST, 0)
            q = (q + q * heat[MAIN:]) * h[g]
            if repeat:
                d = z[g] - z0[g]
                x = jnp.concatenate([p, jnp.where(top, q, d[:8]), d[8:]], axis=0)
            else:
                zero = jnp.zeros((8, wide), F32)
                x = jnp.concatenate([p, jnp.where(top, q, zero), zero], axis=0)
            hi, lo = parts(x)
            pairs.append(jnp.concatenate([hi, lo, hi], axis=0))
        side = jnp.concatenate(pairs, axis=1)
        change = jnp.dot(update, side, preferred_element_type=F32)
        part = [change[:, g * wide : (g + 1) * wide] for g in range(GROUPS)]
        a = [a[g] + part[g][:FORM] for g in range(GROUPS)]
        z = [z[g] + part[g][FORM : FORM + ROWS] for g in range(GROUPS)]
    cut = lambda v: [v[k // per][:, (k % per) * NZ : (k % per + 1) * NZ] for k in range(len(cols))]
    return cut(z), cut(a)


def is_even(odd):
    return jnp.broadcast_to(odd[...], (8, NZ)) == 0


def halo_kernel(species, flow, odd, *refs):
    small, (end_x, start_x, outer_y, inner_y) = refs[:SMALL], refs[SMALL : SMALL + 4]
    small_out, (own_s, own_f, sems) = refs[SMALL + 4 : -3], refs[-3:]
    pairs = [(species, own_s), (flow, own_f)] + list(zip(small, small_out))
    copies = [pltpu.make_async_copy(a, b, sems.at[k]) for k, (a, b) in enumerate(pairs)]
    for c in copies:
        c.start()
    for c in copies:
        c.wait()
    for f in range(NF):
        src, at = (own_s, f) if f < NSPEC else (own_f, f - NSPEC)
        last_y, first_y = src[at, :, CY - 1, :], src[at, :, 0, :]
        end_x[f] = src[at, CX - 1]
        start_x[f] = src[at, 0]
        outer_y[f] = jnp.where(is_even(odd), first_y, last_y)
        inner_y[f] = jnp.where(is_even(odd), last_y, first_y)


def weights_kernel(classes, left_t, right_t, stoich_t, heat, prefactor, energy, newton, diffusivity, forms, update, energy_col, diff, table):
    table[...] = column_plan(classes[...].astype(F32))
    w, forms[...] = form_weights(left_t[...], right_t[...])
    update[...] = update_weights(w, stoich_t[...], heat[...], prefactor[...], newton[...])
    at_e = one_hot((MAIN + 8, NREAC), lambda r, c: r == c)
    col = jnp.sum(at_e * (0.5 * energy[...]), axis=1, keepdims=True)
    energy_col[...] = jnp.broadcast_to(col, (MAIN + 8, NZ))
    col = jnp.sum(one_hot((16, NF), lambda r, c: r == c) * diffusivity[...], axis=1, keepdims=True)
    diff[...] = jnp.broadcast_to(col, (16, NZ))


def react_kernel(
    species,
    flow,
    outer_y,
    inner_y,
    xlo,
    xhi,
    odd,
    forms,
    update,
    energy_col,
    diff,
    table,
    fz_far,
    dz_far,
    species_out,
    flow_mid,
    spectra,
    state,
    temp0,
    buf,
    held,
    buf_forms,
    plan,
    burnt,
    fz,
    dz,
    sems,
):
    to_scalar = pltpu.make_async_copy(table, plan, sems.at[0])
    to_scalar.start()
    near = [pltpu.make_async_copy(fz_far, fz, sems.at[2]), pltpu.make_async_copy(dz_far, dz, sems.at[3])]
    for c in near:
        c.start()

    ysub = lax.broadcasted_iota(jnp.int32, (CY, NZ), 0)
    half = [0.5 * flow[c] for c in (1, 2, 3)]

    def transport(f, field):
        coef = diff[f : f + 1, :]
        ylo = jnp.where(is_even(odd), outer_y[f], inner_y[f])
        yhi = jnp.where(is_even(odd), inner_y[f], outer_y[f])
        ahead_x = jnp.concatenate([field[1:], xhi[f][None]], axis=0)
        behind_x = jnp.concatenate([xlo[f][None], field[:-1]], axis=0)
        up = pltpu.roll(field, CY - 1, 1)
        down = pltpu.roll(field, 1, 1)
        ahead_y = jnp.stack([jnp.where(ysub == CY - 1, yhi[x : x + 1, :], up[x]) for x in range(CX)])
        behind_y = jnp.stack([jnp.where(ysub == 0, ylo[x : x + 1, :], down[x]) for x in range(CX)])
        ahead_z = pltpu.roll(field, NZ - 1, 2)
        behind_z = pltpu.roll(field, 1, 2)
        lap = (ahead_x + behind_x) + (ahead_y + behind_y) + (ahead_z + behind_z) - 6.0 * field
        adv = (
            half[0] * (ahead_x - behind_x)
            + half[1] * (ahead_y - behind_y)
            + half[2] * (ahead_z - behind_z)
        )
        return field + DT * (coef * lap - adv)

    zero = jnp.zeros((COLS, NZ), F32)
    for row in list(range(OFF)) + list(range(OFF + NS, ROWS)):
        state[:, row, :] = zero
    for f in range(NF):
        field = species[f] if f < NSPEC else flow[f - NSPEC]
        moved = transport(f, field)
        if f < NSPEC:
            state[:, OFF + f, :] = moved.reshape(COLS, NZ)
        elif f == NF - 1:
            state[:, OFF + NSPEC, :] = moved.reshape(COLS, NZ)
            temp0[...] = moved.reshape(COLS, NZ)
        else:
            flow_mid[f - NSPEC] = moved

    to_scalar.wait()
    steps = [step_of(plan[1, k]) for k in range(COLS)]
    cols = [state[k] for k in range(COLS)]
    done, lines = substep(cols, all_forms(cols, forms[...]), steps, update[...], energy_col[:, 0:1])
    for k in range(COLS):
        state[k] = done[k]
        held[k] = lines[k]

    for k in range(CAP):
        buf[k] = state[plan[0, k]]
        buf_forms[k] = held[plan[0, k]]

    def some(count, s):
        kinds = [plan[2, k] for k in range(count)]
        cols = [buf[k] for k in range(count)]
        olds = [buf_forms[k] for k in range(count)]
        done, lines = substep(cols, joined(olds), [step_of(c) for c in kinds], update[...], energy_col[:, 0:1])
        for k in range(count):
            buf[k] = jnp.where(kinds[k] > s, done[k], cols[k])
            buf_forms[k] = jnp.where(kinds[k] > s, lines[k], olds[k])

    def section(s, _):
        many = plan[2, CAP // 2] > s

        @pl.when(many)
        def _():
            some(CAP, s)

        @pl.when(jnp.logical_and(jnp.logical_not(many), plan[2, 0] > s))
        def _():
            some(CAP // 2, s)

        return 0

    lax.fori_loop(1, 4, section, 0)

    for k in range(CAP):
        state[plan[0, k]] = buf[k]
    for i in range(NSPEC):
        burnt[i] = state[:, OFF + i, :].reshape(CX, CY, NZ)
    to_out = pltpu.make_async_copy(burnt, species_out, sems.at[1])
    to_out.start()
    last = state[:, OFF + NSPEC, :]
    flow_mid[4] = last.reshape(CX, CY, NZ)
    source = (last - temp0[...]) * (1.0 / DT)
    for c in near:
        c.wait()
    nt = ((1,), (1,))
    horizontal = flow_mid[1:3].reshape(2 * COLS, NZ)
    fz2, dz2 = (fz[0], fz[1]), (dz[0], dz[1])
    spectra[:, 0, :] = dot3(fz2, parts(horizontal), nt)
    vertical = flow_mid[3].reshape(COLS, NZ)
    third = dot3(dz2, parts(vertical), nt) - dot3(fz2, parts(source), nt)
    spectra[:, 1, :] = jnp.concatenate([third, jnp.zeros_like(third)], axis=1)
    to_out.wait()


def swap_blocks(v):
    rows, lanes = v.shape
    r = lax.broadcasted_iota(jnp.int32, v.shape, 0)
    k = lax.broadcasted_iota(jnp.int32, v.shape, 1) // 8
    for b in (1, 2, 4):
        low_r, low_k = (r & b) == 0, (k & b) == 0
        from_above = pltpu.roll(pltpu.roll(v, b, 0), lanes - 8 * b, 1)
        from_below = pltpu.roll(pltpu.roll(v, rows - b, 0), 8 * b, 1)
        v = jnp.where(low_r == low_k, v, jnp.where(low_r, from_below, from_above))
    return v


def stream_kernel(got, fx, dx, out):
    a = swap_blocks(got[:, 0, :])
    w = swap_blocks(got[:, 1, :])
    upper = lax.broadcasted_iota(jnp.int32, a.shape, 1) < COLS
    fx2, dx2 = (fx[0], fx[1]), (dx[0], dx[1])
    moved = jnp.where(upper, w, a)
    both = dot3(fx2, parts(moved)) + jnp.where(upper, dot3(dx2, parts(a)), 0.0)
    for i in range(4):
        out[i] = both


def once(a, b):
    return jnp.dot(a, b, preferred_element_type=F32)


def solve_kernel(place, got, forth, back, kx2, ky2, left, out):
    hi, lo = parts(jnp.concatenate([got[i] for i in range(4)], axis=1))
    full = once(jnp.concatenate([hi, hi, lo], axis=1), forth[...])
    mode = (place[:, 0:1] % (NZ // 2)).astype(F32) * (2 * np.pi / NZ)
    k2 = kx2[...] + ky2[...] + mode * mode
    mine = jnp.max(place[:, 1:2])
    hi, lo = parts(full / jnp.where(k2 > 0, k2, 1.0))
    hi, lo = parts(once(jnp.concatenate([hi, hi, lo], axis=1), back[mine]))
    lines = once(left[...], jnp.concatenate([hi, lo, hi], axis=0))
    out[:, 0, :] = swap_blocks(lines[:NX])
    out[:, 1, :] = swap_blocks(lines[NX:])


def finish_kernel(got, mid, fz, dz, out):
    fz2, dz2 = (fz[0], fz[1]), (dz[0], dz[1])
    first = parts(jnp.transpose(got[:, 0, :]))
    second = parts(jnp.transpose(got[:, 1, :]))
    a = dot3(second, fz2)[:COLS]
    b = dot3(first, fz2)[COLS:]
    c = dot3(first, dz2)[:COLS]
    out[0] = mid[0]
    out[1] = mid[1] + a.reshape(CX, CY, NZ)
    out[2] = mid[2] + b.reshape(CX, CY, NZ)
    out[3] = mid[3] - c.reshape(CX, CY, NZ)
    out[4] = mid[4]


def far(v):
    return pltpu.with_memory_space_constraint(jnp.asarray(v), pltpu.HBM)


def call(kernel, out_shapes, in_specs, scratch=(), out_specs=None):
    pairs = [v if isinstance(v[0], tuple) else (v, F32) for v in out_shapes]
    out = [jax.ShapeDtypeStruct(*v) for v in pairs]
    one = len(out) == 1
    return pl.pallas_call(
        kernel,
        out_shape=out[0] if one else out,
        in_specs=[VMEM] * in_specs if isinstance(in_specs, int) else in_specs,
        out_specs=VMEM if one else out_specs or [VMEM] * len(out),
        scratch_shapes=list(scratch),
        compiler_params=pltpu.CompilerParams(vmem_limit_bytes=LIMIT),
    )


def react(fields, halos, small, fz, dz):
    bf16 = jnp.bfloat16
    weights = call(
        weights_kernel,
        [
            ((GROUPS * FORM, WIDE), bf16),
            ((CHANGE, 96), bf16),
            ((MAIN + 8, NZ), F32),
            ((16, NZ), F32),
            ((8, NZ), jnp.int32),
        ],
        9,
    )(*small)
    return call(
        react_kernel,
        [(NSPEC, CX, CY, NZ), (5, CX, CY, NZ), (NZ, 2, 2 * COLS)],
        [VMEM] * 12 + [HBM] * 2,
        [
            pltpu.VMEM((COLS, ROWS, NZ), F32),
            pltpu.VMEM((COLS, NZ), F32),
            pltpu.VMEM((CAP, ROWS, NZ), F32),
            pltpu.VMEM((COLS, FORM, NZ), F32),
            pltpu.VMEM((CAP, FORM, NZ), F32),
            pltpu.SMEM((8, NZ), jnp.int32),
            pltpu.VMEM((NSPEC, CX, CY, NZ), F32),
            pltpu.VMEM((2, NZ, NZ), bf16),
            pltpu.VMEM((2, NZ, NZ), bf16),
            pltpu.SemaphoreType.DMA((4,)),
        ],
        [HBM, VMEM, VMEM],
    )(*fields, *halos, *weights, far(fz), far(dz))


def swap(axes, n, first):
    pairs = [(k % n, (k + 1) % n) for k in range(first, n + first, 2)]
    return functools.partial(lax.ppermute, axis_name=axes, perm=pairs + [(b, a) for a, b in pairs])


def shift(axes, n, step):
    return functools.partial(
        lax.ppermute, axis_name=axes, perm=[(i, (i + step) % n) for i in range(n)]
    )


def shards(
    species,
    flow,
    classes,
    diffusivity,
    left,
    right,
    stoich,
    heat,
    prefactor,
    energy,
    newton,
):
    n_gx, n_gy = NX // CX, NY // CY
    odd = (lax.axis_index(GY) % 2).astype(jnp.int32).reshape(1, 1)
    row = lambda v: v[None, :]
    small = (
        classes,
        left.T,
        right.T,
        stoich.T,
        row(heat),
        row(prefactor),
        row(energy),
        newton,
        row(diffusivity),
    )
    edges = call(
        halo_kernel,
        [(NF, 8, NZ)] * 4 + [(v.shape, v.dtype) for v in small] + [species.shape, flow.shape],
        [HBM] * 2 + [VMEM] + [HBM] * SMALL,
        [pltpu.SemaphoreType.DMA((2 + SMALL,))],
    )(far(species), far(flow), odd, *(far(v) for v in small))
    halos = (
        swap(GY, n_gy, 1)(edges[2]),
        swap(GY, n_gy, 0)(edges[3]),
        shift(GX, n_gx, 1)(edges[0]),
        shift(GX, n_gx, -1)(edges[1]),
        odd,
    )

    fz, dz, _ = basis(NZ)
    fy, dy, ky = basis(NY)
    fx, dx, kx = basis(NX)
    f32 = lambda v: np.ascontiguousarray(v, np.float32)

    def table(v):
        v = f32(v)
        hi = v.astype(jnp.bfloat16)
        return np.stack([hi, (v - hi.astype(np.float32)).astype(jnp.bfloat16)])

    def stacked(v, axis, first=False):
        hi, lo = table(v)
        return np.concatenate([hi, hi, lo] if first else [hi, lo, hi], axis=axis)

    y_of = ((np.arange(8)[None, :, None] * 4 + np.arange(4)[:, None, None]) * CY + np.arange(CY)).reshape(4, COLS)
    forth = np.stack([np.concatenate([fy[:, y].T, dy[:, y].T], axis=0) for y in y_of])
    back = np.stack([np.concatenate([fy[:, y], -dy[:, y]], axis=1) for y in y_of])

    species_out, mid, spectra = react(
        edges[-2:],
        halos,
        edges[4:-2],
        table(fz),
        table(dz),
    )
    place = jnp.stack([lax.axis_index(MODES), lax.axis_index("x")]).astype(jnp.int32)[None, :]
    spectra, place = lax.optimization_barrier((spectra, place))
    got = lax.all_to_all(spectra, MODES, 0, 0, tiled=True)
    lines = call(stream_kernel, [(4, NX, 2 * COLS)], 3)(got, table(fx), table(dx))
    lines = lax.all_to_all(lines, "x", 0, 0, tiled=True)
    grads = call(solve_kernel, [(NX, 2, 2 * COLS)], 7)(
        place,
        lines,
        stacked(forth.reshape(-1, NY), 0),
        stacked(back, 1),
        f32(kx * kx)[:, None],
        f32(ky * ky)[None, :],
        stacked(np.concatenate([fx.T, -dx.T], axis=0), 1, first=True),
    )
    got = lax.all_to_all(grads, MODES, 0, 0, tiled=True)
    flow_out = call(finish_kernel, [(5, CX, CY, NZ)], 4)(got, mid, table(fz), table(dz))
    return (species_out, flow_out)


def solution(mesh):
    finer = Mesh(mesh.devices.reshape(8, 2, 8, 4), GX + GY)
    return jax.shard_map(
        shards,
        mesh=finer,
        in_specs=(P(None, GX, GY, None), P(None, GX, GY, None), P(GX, GY)) + (P(),) * 8,
        out_specs=(P(None, GX, GY, None), P(None, GX, GY, None)),
        check_vma=False,
    )
```
